32 devices in a mesh: dp: 8 (over z, x), tensor: 4 (over y, core).
Axes of the slice: x: 2, y: 2, z: 4, core: 2. Of those that a mesh axis runs over, the one named last changes fastest.
Arguments:
- hidden_in: bfloat16 [32, 1024, 768], P('dp', 'tensor'), may hold values from -6 to 6
- codon_ids: int32 [32, 1024], P('dp', 'tensor'), may hold values from 0 to 63
- start_flags: int32 [32, 1024], P('dp', 'tensor'), may hold values 0 or 1
- cotangent: bfloat16 [32, 1024, 768], P('dp', 'tensor'), may hold values from -6 to 6
- codon_table: float32 [128, 768], replicated, may hold values from -3 to 3
- norm1_gain: float32 [768], replicated, may hold values from 0.1 to 1.9
- norm1_bias: float32 [768], replicated, may hold values from -1.5 to 1.5
- qkv_weight: bfloat16 [768, 3, 768], P(None, None, 'tensor'), may hold values from -0.21875 to 0.21875
- qkv_bias: float32 [3, 768], P(None, 'tensor'), may hold values from -1.5 to 1.5
- out_weight: bfloat16 [768, 768], P('tensor'), may hold values from -4 to 4
- out_bias: float32 [768], replicated, may hold values from -1.5 to 1.5
- norm2_gain: float32 [768], replicated, may hold values from 0.1 to 1.9
- norm2_bias: float32 [768], replicated, may hold values from -1.5 to 1.5
- up_weight: bfloat16 [768, 3072], P(None, 'tensor'), may hold values from -0.21875 to 0.21875
- up_bias: bfloat16 [3072], P('tensor'), may hold values from -1.5 to 1.5
- down_weight: bfloat16 [3072, 768], P('tensor'), may hold values from -0.109375 to 0.109375
- down_bias: float32 [768], replicated, may hold values from -1.5 to 1.5
Outputs:
- hidden_out: bfloat16 [32, 1024, 768], P('dp', 'tensor')
- hidden_grad: float32 [32, 1024, 768], P('dp', 'tensor')
- table_grad: float32 [128, 768], replicated
- norm1_gain_grad: float32 [768], replicated
- norm1_bias_grad: float32 [768], replicated
- qkv_weight_grad: float32 [768, 3, 768], P(None, None, 'tensor')
- qkv_bias_grad: float32 [3, 768], P(None, 'tensor')
- out_weight_grad: float32 [768, 768], P('tensor')
- out_bias_grad: float32 [768], replicated
- norm2_gain_grad: float32 [768], replicated
- norm2_bias_grad: float32 [768], replicated
- up_weight_grad: float32 [768, 3072], P(None, 'tensor')
- up_bias_grad: float32 [3072], P('tensor')
- down_weight_grad: float32 [3072, 768], P('tensor')
- down_bias_grad: float32 [768], replicated
The draws below stay inside these ranges and needn't reach their ends.
All inputs are finite; a program needn't handle non-finite values. No bound on the sum of `start_flags` on one device may be relied on, other than what follows from the above.
Results may differ from the reference program's by a relative error of at most 0.015.
Values may be sent and summed in bfloat16 or wider, within the bound.
No kernel may reach another device: no remote copies, remote signals or barrier semaphores. Data moves between devices by JAX's collectives and lax.ppermute only.
A program may use at most 192 MiB of HBM per device.

```python
import jax
import jax.numpy as jnp
from jax import lax

D = 768
FF = 3072
HEADS = 12
HEAD_DIM = 64
VOCAB = 64
LEN = 1024
GENES = 32


def place_ends(result, key, smallest, largest):
    shape = result.shape
    place = [jax.random.randint(jax.random.fold_in(key, axis), (), 0, shape[axis]) for axis in range(len(shape))]
    result = result.at[tuple(place)].set(smallest)
    longest = shape.index(max(shape))
    place[longest] = (place[longest] + 1) % shape[longest]
    return result.at[tuple(place)].set(largest)


def levels(key, extent, shards, least, largest):
    level = 1.0
    for axis_at, shards_of in shards:
        draws = jax.random.uniform(jax.random.fold_in(jax.random.fold_in(key, 6), axis_at), (shards_of,), jnp.float32, least / len(shards), largest / len(shards))
        level = level * jnp.repeat(jnp.exp(draws), extent[axis_at] // shards_of).reshape((-1,) + (1,) * (len(extent) - 1 - axis_at))
    return level


def gaussian(own_key, extent, width, limit, pieces=(), held_as=jnp.bfloat16):
    drawn = width * jax.random.normal(own_key, extent, jnp.float32)
    if pieces:
        drawn = drawn * levels(own_key, extent, pieces, -0.22, 0.18)
    return jnp.clip(drawn, -limit, limit).astype(held_as)


def setup_inputs(seed: int = 0) -> dict:
    splits = jax.random.split(jax.random.key(seed), 18)
    hidden_in = gaussian(splits[0], (GENES, LEN, D), 1.0, 6.0, ((0, 8), (1, 4)))
    codon_ids = place_ends(jax.random.randint(splits[1], (GENES, LEN), 0, VOCAB), jax.random.fold_in(splits[1], 1), 0, VOCAB - 1).astype(jnp.int32)
    start_flags = place_ends((jax.random.randint(splits[2], (GENES, LEN), 0, 16) < 1).astype(jnp.int32), jax.random.fold_in(splits[2], 1), 0, 1)
    cotangent = gaussian(splits[3], (GENES, LEN, D), 1.0, 6.0, ((0, 8), (1, 4)))
    codon_table = gaussian(splits[4], (2 * VOCAB, D), 0.5, 3.0, (), jnp.float32)
    norm1_gain = jnp.clip(1.0 + 0.18 * jax.random.normal(splits[5], (D,), jnp.float32), 0.1, 1.9)
    norm1_bias = gaussian(splits[6], (D,), 0.3, 1.5, (), jnp.float32)
    qkv_weight = gaussian(splits[7], (D, 3, D), D ** -0.5, 0.21875, ((2, 4),))
    qkv_bias = gaussian(splits[8], (3, D), 0.3, 1.5, ((1, 4),), jnp.float32)
    out_weight = gaussian(splits[9], (D, D), (2 * D // LEN + 1) ** -0.5, 4.0, ((0, 4),))
    out_bias = gaussian(splits[10], (D,), 0.3, 1.5, (), jnp.float32)
    norm2_gain = jnp.clip(1.0 + 0.18 * jax.random.normal(splits[11], (D,), jnp.float32), 0.1, 1.9)
    norm2_bias = gaussian(splits[12], (D,), 0.3, 1.5, (), jnp.float32)
    up_weight = gaussian(splits[13], (D, FF), D ** -0.5, 0.21875, ((1, 4),))
    up_bias = gaussian(splits[14], (FF,), 0.3, 1.5, ((0, 4),))
    down_weight = gaussian(splits[15], (FF, D), FF ** -0.5, 0.109375, ((0, 4),))
    down_bias = gaussian(splits[16], (D,), 0.3, 1.5, (), jnp.float32)
    return {"hidden_in": hidden_in, "codon_ids": codon_ids, "start_flags": start_flags, "cotangent": cotangent, "codon_table": codon_table, "norm1_gain": norm1_gain, "norm1_bias": norm1_bias, "qkv_weight": qkv_weight, "qkv_bias": qkv_bias, "out_weight": out_weight, "out_bias": out_bias, "norm2_gain": norm2_gain, "norm2_bias": norm2_bias, "up_weight": up_weight, "up_bias": up_bias, "down_weight": down_weight, "down_bias": down_bias}


@jax.custom_vjp
def low(v):
    return lax.optimization_barrier(v.astype(jnp.bfloat16)).astype(jnp.float32)

@jax.custom_vjp
def low_back(v):
    return v

def low_keep(v):
    return (low(v), None)

def low_pass(kept, grad):
    return (grad,)

def back_keep(v):
    return (v, None)

def back_low(kept, grad):
    return (low(grad),)
low.defvjp(low_keep, low_pass)
low_back.defvjp(back_keep, back_low)
EPSILON = 1e-05
HIGHEST = lax.Precision.HIGHEST

def matmul_high(left, right):
    return jnp.dot(left, right, precision=HIGHEST, preferred_element_type=jnp.float32)

def layer_norm(row_data, gain_vec, shift_vec):
    row_mean = lax.optimization_barrier(jnp.mean(row_data, axis=-1, keepdims=True))
    centred = row_data - row_mean
    row_var = lax.optimization_barrier(jnp.mean(centred * centred, axis=-1, keepdims=True))
    return centred * lax.rsqrt(row_var + EPSILON) * gain_vec + shift_vec

def gelu_exact(values_in):
    return jax.nn.gelu(values_in, approximate=False)

def rotate(values_in, cosines, sines):
    half_dim = values_in.shape[-1] // 2
    lower_half = values_in[..., :half_dim]
    upper_half = values_in[..., half_dim:]
    return jnp.concatenate([lower_half * cosines - upper_half * sines, upper_half * cosines + lower_half * sines], -1)

def head_attention(block_item):
    query_block, key_block, value_block = block_item
    scores = low_back(matmul_high(query_block, key_block.T) * HEAD_DIM ** (-0.5))
    row_max = lax.optimization_barrier(jnp.max(scores, -1, keepdims=True))
    exp_scores = jnp.exp(scores - row_max)
    soft_probs = low(exp_scores / lax.optimization_barrier(jnp.sum(exp_scores, -1, keepdims=True)))
    return low(low_back(matmul_high(soft_probs, value_block)))

def gene_layer(param_set, input_rows, table_index):
    table, gain_one, bias_one, wqkv, bqkv, wout, bout, gain_two, bias_two, wup, bup, wdown, bdown = param_set
    embedded = input_rows + table[table_index]
    normed_first = low(layer_norm(embedded, gain_one, bias_one))
    qkv_rows = low_back(matmul_high(normed_first, wqkv.reshape(D, 3 * D)) + bqkv.reshape(3 * D))
    qkv_rows = qkv_rows.reshape(LEN, 3, HEADS, HEAD_DIM)
    frequencies = 10000.0 ** (-jnp.arange(HEAD_DIM // 2, dtype=jnp.float32) * 2.0 / HEAD_DIM)
    positions = jnp.arange(LEN, dtype=jnp.float32)
    angles = (positions[:, None] * frequencies[None, :])[:, None, :]
    cosines = jnp.cos(angles)
    sines = jnp.sin(angles)
    query_rows = low(rotate(qkv_rows[:, 0], cosines, sines))
    key_rows = low(rotate(qkv_rows[:, 1], cosines, sines))
    value_rows = low(qkv_rows[:, 2])
    context = lax.map(jax.checkpoint(head_attention), (query_rows.transpose(1, 0, 2), key_rows.transpose(1, 0, 2), value_rows.transpose(1, 0, 2)))
    context = context.transpose(1, 0, 2).reshape(LEN, D)
    mid_rows = embedded + low_back(matmul_high(context, wout) + bout)
    normed_second = low(layer_norm(mid_rows, gain_two, bias_two))
    gate_in = low_back(matmul_high(normed_second, wup) + bup)
    activation = low(gelu_exact(gate_in))
    return mid_rows + low_back(matmul_high(activation, wdown) + bdown)

def reference(hidden_in, codon_ids, start_flags, cotangent, codon_table, norm1_gain, norm1_bias, qkv_weight, qkv_bias, out_weight, out_bias, norm2_gain, norm2_bias, up_weight, up_bias, down_weight, down_bias):
    params = tuple((item.astype(jnp.float32) for item in (codon_table, norm1_gain, norm1_bias, qkv_weight, qkv_bias, out_weight, out_bias, norm2_gain, norm2_bias, up_weight, up_bias, down_weight, down_bias)))
    table_index = (codon_ids + VOCAB * start_flags).astype(jnp.int32)
    zero_sums = tuple((jnp.zeros(item.shape, jnp.float32) for item in params))

    def gene_step(totals, gene_item):
        input_rows, index_rows, cot_rows = gene_item
        layer_out, pullback = jax.vjp(lambda param_set, rows_in: gene_layer(param_set, rows_in, index_rows), params, input_rows.astype(jnp.float32))
        gradients, grad_rows = pullback(cot_rows.astype(jnp.float32))
        return (tuple((first_sum + more for first_sum, more in zip(totals, gradients))), (layer_out.astype(jnp.bfloat16), grad_rows))
    totals, (outputs, grad_input) = lax.scan(gene_step, zero_sums, (hidden_in, table_index, cotangent))
    return (outputs, grad_input, totals[0], totals[1], totals[2], totals[3], totals[4], totals[5], totals[6], totals[7], totals[8], totals[9], totals[10], totals[11], totals[12])
```

```python
import functools

import jax
import jax.numpy as jnp
from jax import lax
from jax.experimental import pallas as pl
from jax.experimental.pallas import tpu as pltpu
from jax.sharding import PartitionSpec as P

HEAD_DIM = 64
PAIR = 2 * HEAD_DIM
EPSILON = 1e-05
HIGHEST = lax.Precision.HIGHEST
NT = (((1,), (1,)), ((), ()))
TN = (((0,), (0,)), ((), ()))
LOG2E = 1.4426950408889634
TILE = 16
UP_ROW = 10
TABLE_HALF = 64
BIAS_HEADS = 3
SOFT_ROWS = 128
FEED_STEP = 256
bf16 = jnp.bfloat16
f32 = jnp.float32


def params(mebibytes):
    return pltpu.CompilerParams(vmem_limit_bytes=mebibytes * 1024 * 1024)


def cost(microseconds):
    return pl.CostEstimate(
        flops=microseconds * 10**9, bytes_accessed=microseconds * 10**6, transcendentals=0
    )


def dot(left, right):
    return jnp.dot(left, right, preferred_element_type=f32)


def dot_nt(left, right):
    return lax.dot_general(left, right, NT, preferred_element_type=f32)


def dot_tn(left, right):
    return lax.dot_general(left, right, TN, preferred_element_type=f32)


def whole(shape):
    return pl.BlockSpec(shape, lambda i: (0,) * len(shape))


def by_rows(rows, cols):
    return pl.BlockSpec((rows, cols), lambda i: (i, 0))


def by_cols(rows, cols):
    return pl.BlockSpec((rows, cols), lambda i: (0, i))


def swap(array_in, axis, distance):
    size = lax.axis_size(axis)
    return lax.ppermute(array_in, axis, [(i, i ^ distance) for i in range(size)])


def together(items):
    return lax.optimization_barrier(items)


def stage(sends, work, *inputs):
    arrays, inputs = together(([item[0] for item in sends], inputs))
    got = [swap(array, axis, distance) for array, (_, axis, distance) in zip(arrays, sends)]
    return together((got, work(*inputs)))


def add_low(*terms):
    return sum(term.astype(f32) for term in terms).astype(bf16)


def core_sum(mine, other):
    return add_low(mine, swap(other, "tensor", 1))


def halve(rows):
    size = lax.axis_size("dp")
    segment = rows.shape[0] // size
    halves = rows.reshape(size // 2, 2, segment, rows.shape[1])
    mine = lax.axis_index("dp") & 1
    keep = lax.dynamic_index_in_dim(halves, mine, 1, keepdims=False)
    send = lax.dynamic_index_in_dim(halves, 1 - mine, 1, keepdims=False)
    return keep, send


def halve_two(one, two):
    (keep_one, send_one), (keep_two, send_two) = halve(one), halve(two)
    return jnp.stack([keep_one, keep_two]), jnp.stack([send_one, send_two])


def pick(array_in, index):
    return lax.dynamic_index_in_dim(array_in, index, 0, keepdims=False)


class Scatter:
    def __init__(self, current, axis=0):
        self.row = lax.axis_index("dp") >> 1
        self.own, *self.sends = (
            lax.dynamic_index_in_dim(current, self.row ^ j, axis, keepdims=False)
            for j in range(current.shape[axis])
        )

    def transfers(self):
        return [(item, "dp", 2 * j + 2) for j, item in enumerate(self.sends)]

    def finish(self, got):
        return add_low(self.own, *got)


def upper_transfers(segment):
    return [(segment, "dp", 2 * j) for j in range(1, lax.axis_size("dp") // 2)]


def mate_transfer(pieces, crossed):
    return (jnp.stack([pieces[1], crossed[1]]), "tensor", 1)


def four(pieces, crossed, got):
    return [pieces[0], got[0], crossed[0], got[1]]


def normalise(row_data):
    row_mean = jnp.mean(row_data, axis=-1, keepdims=True)
    centred = row_data - row_mean
    row_var = jnp.mean(centred * centred, axis=-1, keepdims=True)
    inverse = lax.rsqrt(row_var + EPSILON)
    return centred * inverse, inverse


def norm_back(scaled, unit, inverse):
    return inverse * (
        scaled
        - jnp.mean(scaled, -1, keepdims=True)
        - unit * jnp.mean(scaled * unit, -1, keepdims=True)
    )


def column_sum(array_in):
    return jnp.sum(array_in, 0, keepdims=True)


def rows_of(*vectors):
    width = vectors[0].shape[1]
    at = lax.broadcasted_iota(jnp.int32, (8, width), 0)
    tile = jnp.zeros((8, width), f32)
    for k, vector in enumerate(vectors):
        tile = jnp.where(at == k, vector, tile)
    return tile


def first_head(rows):
    return lax.broadcasted_iota(jnp.int32, (rows, PAIR), 1) < HEAD_DIM


def turn(values_in, cosines, sines):
    lanes = lax.broadcasted_iota(jnp.int32, values_in.shape, 1)
    lower = (lanes & (HEAD_DIM - 1)) < HEAD_DIM // 2
    other = jnp.where(
        lower,
        pltpu.roll(values_in, PAIR - HEAD_DIM // 2, 1),
        pltpu.roll(values_in, HEAD_DIM // 2, 1),
    )
    return values_in * cosines + other * sines


def unturn(values_in, cosines, sines):
    quarter = HEAD_DIM // 2
    parts = [values_in[k * quarter : (k + 1) * quarter] for k in range(4)]
    out = []
    for low, high in (parts[:2], parts[2:]):
        out += [low * cosines + high * sines, high * cosines - low * sines]
    return jnp.concatenate(out, 0)


def split_three(values_in):
    high = values_in.astype(bf16)
    rest = values_in - high.astype(f32)
    middle = rest.astype(bf16)
    return high, middle, (rest - middle.astype(f32)).astype(bf16)


def parcel_kernel(hidden_ref, ids_ref, flags_ref, bias_ref, up_ref, *outs):
    rank = lax.axis_index("tensor")
    piece, width = hidden_ref.shape[1:]
    at = lax.broadcasted_iota(jnp.int32, (TILE, width), 0)
    tile = jnp.where(at == UP_ROW, up_ref[...].astype(f32), 0.0)
    rest = bias_ref[...]
    for part in range(3):
        high = rest.astype(bf16).astype(f32)
        rest = rest - high
        for k in range(3):
            tile = jnp.where(at == 1 + 3 * part + k, high[k : k + 1], tile)
    for distance, out_ref in enumerate(outs):
        gene = rank ^ distance
        out_ref[:piece] = hidden_ref[gene]
        index = (ids_ref[pl.ds(gene, 1)] + TABLE_HALF * flags_ref[pl.ds(gene, 1)]).astype(f32)
        index = jnp.concatenate([index, jnp.zeros((1, width - piece), f32)], 1)
        out_ref[piece:] = jnp.where(at == 0, index, tile).astype(bf16)


def make_parcels(hidden_in, codon_ids, start_flags, bias, up_bias):
    genes, piece, width = hidden_in.shape
    shape = jax.ShapeDtypeStruct((piece + TILE, width), bf16)
    return pl.pallas_call(
        parcel_kernel,
        out_shape=[shape] * genes,
        name="parcels",
        compiler_params=params(8),
        cost_estimate=cost(2),
    )(hidden_in, codon_ids, start_flags, bias, up_bias)


def onehot_of(tile, table_rows, piece):
    index = tile[0:1, :piece].astype(f32)
    at = lax.broadcasted_iota(jnp.int32, (table_rows, piece), 0).astype(f32)
    return (at == index).astype(bf16)


def embed_kernel(p0, p1, p2, p3, table_ref, gain_ref, shift_ref, base_ref, norm_ref, held):
    step = pl.program_id(0)
    piece = base_ref.shape[0]
    for k, parcel in enumerate((p0, p1, p2, p3)):

        @pl.when(step == k)
        def _():
            held[...] = parcel[...]

    onehot = onehot_of(held[piece:], table_ref.shape[0], piece)
    base = held[:piece].astype(f32)
    for part in split_three(table_ref[...]):
        base = base + dot_tn(onehot, part)
    unit, _ = normalise(base)
    base_ref[...] = base
    norm_ref[...] = (unit * gain_ref[...] + shift_ref[...]).astype(bf16)


def embed(parcels, table, gain, shift):
    rows, width = parcels[0].shape
    piece = rows - TILE
    return pl.pallas_call(
        embed_kernel,
        grid=(len(parcels),),
        in_specs=[whole(parcels[0].shape)] * 4
        + [whole(table.shape), whole(gain.shape), whole(shift.shape)],
        out_specs=[by_rows(piece, width)] * 2,
        out_shape=[
            jax.ShapeDtypeStruct((4 * piece, width), f32),
            jax.ShapeDtypeStruct((4 * piece, width), bf16),
        ],
        scratch_shapes=[pltpu.VMEM((rows, width), bf16)],
        name="embed",
        compiler_params=params(16),
        cost_estimate=cost(4),
    )(*parcels, table, gain, shift)


def pair_rows(a_ref, b_ref, parts):
    return jnp.concatenate([ref[0, part] for part in parts for ref in (a_ref, b_ref)], 0)


def attend_kernel(
    base, norm_ref, a_ref, b_ref, ta_ref, tb_ref, cos_ref, sin_ref,
    q_ref, k_ref, v_ref, context_ref, inverse_ref, exps_ref, attn_ref, biases, scores_ref,
):
    step = pl.program_id(0)
    for head in range(BIAS_HEADS):

        @pl.when(step + base == head)
        def _():
            vectors = []
            lanes = slice(head * PAIR, (head + 1) * PAIR)
            for k in range(3):
                two = []
                for tile in (ta_ref, tb_ref):
                    high = tile[...].astype(f32)[:, lanes]
                    two.append(high[1 + k : 2 + k] + high[4 + k : 5 + k] + high[7 + k : 8 + k])
                vectors.append(jnp.where(first_head(1), two[0], two[1]))
            biases[...] = rows_of(*vectors)

    rows = norm_ref.shape[0]
    product = dot_nt(norm_ref[...], pair_rows(a_ref, b_ref, (0, 1, 2)))
    bias = biases[...]
    cosines, sines = cos_ref[...], sin_ref[...]
    query = turn(product[:, :PAIR] + bias[0:1], cosines, sines).astype(bf16)
    query = query * jnp.asarray(HEAD_DIM**-0.5, bf16)
    keys = turn(product[:, PAIR : 2 * PAIR] + bias[1:2], cosines, sines).astype(bf16)
    values = (product[:, 2 * PAIR :] + bias[2:3]).astype(bf16)
    q_ref[...] = query
    k_ref[...] = keys
    v_ref[...] = values
    values = jnp.concatenate([values, jnp.ones((rows, PAIR), bf16)], 1)
    first = first_head(rows)
    for head in range(2):
        only = jnp.where(first == (head == 0), query, jnp.zeros_like(query))
        scores_ref[head] = dot_nt(only, keys)
    outs = []
    for head in range(2):
        for start in range(0, rows, SOFT_ROWS):
            span = slice(start, start + SOFT_ROWS)
            scores = scores_ref[head, span]
            top = jnp.max(scores, 1, keepdims=True) * LOG2E
            exps_ref[head, span] = jnp.exp2(scores * LOG2E - top).astype(bf16)
        outs.append(dot(exps_ref[head], values))
    inverse = 1.0 / jnp.where(first, outs[0][:, PAIR:], outs[1][:, PAIR:])
    context = (jnp.where(first, outs[0][:, :PAIR], outs[1][:, :PAIR]) * inverse).astype(bf16)
    inverse_ref[...] = inverse
    context_ref[...] = context
    more = dot(context, pair_rows(a_ref, b_ref, (3,)))

    @pl.when(step == 0)
    def _():
        attn_ref[...] = more

    @pl.when(step != 0)
    def _():
        attn_ref[...] += more


def attend(norm, a, b, tile_a, tile_b, tables, heads):
    rows, width = norm.shape
    base, pairs = heads
    low = jax.ShapeDtypeStruct((rows, pairs * PAIR), bf16)
    return pl.pallas_call(
        functools.partial(attend_kernel, base),
        grid=(pairs,),
        in_specs=[whole(norm.shape)]
        + [pl.BlockSpec((1,) + a.shape[1:], lambda i: (i + base, 0, 0, 0))] * 2
        + [tile_spec_of(tile_a)] * 2
        + [whole((rows, PAIR))] * 2,
        out_specs=[by_cols(rows, PAIR)] * 5
        + [pl.BlockSpec((2, rows, rows), lambda i: (i, 0, 0)), whole((rows, width))],
        out_shape=[low] * 4
        + [
            jax.ShapeDtypeStruct((rows, pairs * PAIR), f32),
            jax.ShapeDtypeStruct((2 * pairs, rows, rows), bf16),
            jax.ShapeDtypeStruct((rows, width), f32),
        ],
        scratch_shapes=[pltpu.VMEM((8, PAIR), f32), pltpu.VMEM((2, rows, rows), f32)],
        name="attend",
        compiler_params=params(44),
        cost_estimate=cost(8 * pairs),
    )(norm, a, b, tile_a, tile_b, *tables)


def attend_back_kernel(
    q_ref, k_ref, v_ref, context_ref, inverse_ref, exps_ref, grad_ref, norm_ref,
    a_ref, b_ref, cos_ref, sin_ref, out_a, out_b, back_ref, bias_ref, probs_ref, scores_ref,
):
    step = pl.program_id(0)
    rows = q_ref.shape[0]
    values = v_ref[...]
    first = first_head(rows)
    grad = dot_nt(grad_ref[...], pair_rows(a_ref, b_ref, (3,))) * inverse_ref[...]
    terms = grad * context_ref[...].astype(f32)
    inners = [
        jnp.sum(jnp.where(first == (head == 0), terms, 0.0), 1, keepdims=True) for head in range(2)
    ]
    grad = grad.astype(bf16)
    for head in range(2):
        only = jnp.where(first == (head == 0), grad, jnp.zeros_like(grad))
        probs_ref[head] = dot_nt(only, values)
    grad_turned, query_turned, keys_turned = grad.T, q_ref[...].T, k_ref[...].T
    turned = [[], [], []]
    for head in range(2):
        part = slice(head * HEAD_DIM, (head + 1) * HEAD_DIM)
        turned[2].append(dot(grad_turned[part], exps_ref[head]))
        for start in range(0, rows, SOFT_ROWS):
            span = slice(start, start + SOFT_ROWS)
            low = exps_ref[head, span].astype(f32) * (probs_ref[head, span] - inners[head][span])
            scores_ref[head, span] = low.astype(bf16)
        turned[0].append(dot_nt(keys_turned[part], scores_ref[head]))
        turned[1].append(dot(query_turned[part], scores_ref[head]))
    dq, dk, dv = (jnp.concatenate(item, 0) for item in turned)
    dq = unturn(dq * HEAD_DIM**-0.5, cos_ref[...], sin_ref[...])
    dk = unturn(dk, cos_ref[...], sin_ref[...])
    left = jnp.concatenate([dq, dk, dv], 0).astype(bf16)
    more = dot_tn(left, pair_rows(a_ref, b_ref, (0, 1, 2)))

    @pl.when(step == 0)
    def _():
        back_ref[...] = more

    @pl.when(step != 0)
    def _():
        back_ref[...] += more

    bias_ref[0] = dot_nt(jnp.ones((8, rows), bf16), left)
    inputs = dot(left, norm_ref[...]).astype(bf16)
    outputs = dot_tn(context_ref[...], grad_ref[...]).astype(bf16)
    for k in range(4):
        result = outputs if k == 3 else inputs[k * PAIR : (k + 1) * PAIR]
        out_a[0, k] = result[:HEAD_DIM]
        out_b[0, k] = result[HEAD_DIM:]


def attend_back(kept, grad, norm, a, b, tables, heads):
    query, keys, values, context, inverse, exps = kept
    rows, width = norm.shape
    base, count = heads
    shape = (count,) + a.shape[1:]
    columns = by_cols(rows, PAIR)
    weights = pl.BlockSpec((1,) + a.shape[1:], lambda i: (i + base, 0, 0, 0))
    return pl.pallas_call(
        attend_back_kernel,
        grid=(count,),
        in_specs=[columns] * 5
        + [pl.BlockSpec((2, rows, rows), lambda i: (i, 0, 0))]
        + [whole(norm.shape)] * 2
        + [weights] * 2
        + [whole(tables[0].shape)] * 2,
        out_specs=[pl.BlockSpec((1,) + a.shape[1:], lambda i: (i, 0, 0, 0))] * 2
        + [whole((rows, width)), pl.BlockSpec((1, 8, 3 * PAIR), lambda i: (i, 0, 0))],
        out_shape=[jax.ShapeDtypeStruct(shape, bf16)] * 2
        + [
            jax.ShapeDtypeStruct((rows, width), f32),
            jax.ShapeDtypeStruct((count, 8, 3 * PAIR), f32),
        ],
        scratch_shapes=[pltpu.VMEM((2, rows, rows), f32), pltpu.VMEM((2, rows, rows), bf16)],
        name="attend_back",
        compiler_params=params(50),
        cost_estimate=cost(9 * count),
    )(query, keys, values, context, inverse, exps, grad, norm, a, b, *tables)


def gelu_parts(gate):
    bell = jnp.exp2(gate * gate * (-0.5 * LOG2E))
    span = 1.0 + jnp.abs(gate) * (0.3275911 * 0.5**0.5)
    guess = pl.reciprocal(span, approx=True)
    near = guess * (2.0 - span * guess)
    tail = 1.061405429 * 0.5
    for factor in (-1.453152027, 1.421413741, -0.284496736, 0.254829592):
        tail = tail * near + factor * 0.5
    tail = tail * near * bell
    return jnp.where(gate >= 0, 1.0 - tail, tail), bell * 0.3989422804014327


def feed_block(norm, cot, up_ref, down_ref, tile, act_ref, gate_ref):
    chunk = 256
    units = up_ref.shape[1]
    spans = [slice(start, start + chunk) for start in range(0, units, chunk)]

    def first_products(span):
        bias = tile[UP_ROW : UP_ROW + 1, span].astype(f32)
        return dot(norm, up_ref[:, span]) + bias, dot_nt(cot, down_ref[span])

    sums = []
    ahead = first_products(spans[0])
    for at, span in enumerate(spans):
        gate, grad = ahead
        if at + 1 < len(spans):
            ahead = first_products(spans[at + 1])
        share, density = gelu_parts(gate)
        low = (grad * (share + gate * density)).astype(bf16)
        act_ref[:, span] = (gate * share).astype(bf16)
        gate_ref[:, span] = low
        sums.append(column_sum(low.astype(f32)))
    ffn = dot(act_ref[...], down_ref[...])
    back = dot_nt(gate_ref[...], up_ref[...])
    return ffn, back, jnp.concatenate(sums, 1)


def add_sums(ref, tile):
    @pl.when(pl.program_id(0) == 0)
    def _():
        ref[...] = tile

    @pl.when(pl.program_id(0) != 0)
    def _():
        ref[...] += tile


def feed_first_kernel(
    attn_a, attn_b, attn_c, base_ref, cot_ref, vec_ref, ua, ub, da, db, ta, tb,
    mid_ref, norm_ref, act_a, act_b, gate_a, gate_b, ffn_ref, back_ref, sums_ref,
):
    out_bias, gain, shift = (vec_ref[k : k + 1] for k in range(3))
    attn = attn_a[...] + attn_b[...] + attn_c[...]
    mid = base_ref[...] + (attn + out_bias)
    unit, _ = normalise(mid)
    norm = (unit * gain + shift).astype(bf16)
    mid_ref[...] = mid
    norm_ref[...] = norm
    cot = cot_ref[...]
    ffn, back, sum_a = feed_block(norm, cot, ua, da, ta[...], act_a, gate_a)
    more, back_more, sum_b = feed_block(norm, cot, ub, db, tb[...], act_b, gate_b)
    ffn_ref[...] = ffn + more
    back_ref[...] = back + back_more
    add_sums(sums_ref, rows_of(sum_a, sum_b))


def feed_second_kernel(
    norm_ref, mid_ref, cot_ref, vec_ref, ffn_ref, back_ref, one, two, ta, tb,
    act_a, act_b, gate_a, gate_b, mid_grad_ref, low_ref, sums_ref, *pieces,
):
    down_bias, gain = vec_ref[3:4], vec_ref[1:2]
    norm, cot = norm_ref[...], cot_ref[...]
    ffn, back, sum_a = feed_block(norm, cot, one.at[0], one.at[1], ta[...], act_a, gate_a)
    more, back_more, sum_b = feed_block(norm, cot, two.at[0], two.at[1], tb[...], act_b, gate_b)
    mid = mid_ref[...]
    out = (mid + (ffn_ref[...] + (ffn + more) + down_bias)).astype(bf16)
    rows = pieces[0].shape[0]
    back = back_ref[...] + (back + back_more)
    unit, inverse = normalise(mid)
    high = cot.astype(f32)
    grad = high + norm_back(back * gain, unit, inverse)
    low = grad.astype(bf16)
    mid_grad_ref[...] = grad
    low_ref[...] = low
    per_step = mid.shape[0] // rows
    for k, piece in enumerate(pieces):

        @pl.when(pl.program_id(0) == k // per_step)
        def _():
            piece[...] = out[k % per_step * rows : (k % per_step + 1) * rows]

    add_sums(
        sums_ref,
        rows_of(
            sum_a,
            sum_b,
            column_sum(back * unit),
            column_sum(back),
            column_sum(low.astype(f32)),
            column_sum(high),
        ),
    )


def tile_spec_of(parcel):
    at = parcel.shape[0] // TILE - 1
    return pl.BlockSpec((TILE, parcel.shape[1]), lambda i: (at, 0))


def feed_first(attns, base, cot, vectors, ups, downs, parcels):
    rows, width = base.shape
    units = ups[0].shape[1]
    piece = parcels[0].shape[0] - TILE
    step = FEED_STEP
    low = jax.ShapeDtypeStruct((rows, units), bf16)
    high = jax.ShapeDtypeStruct((rows, width), f32)
    return pl.pallas_call(
        feed_first_kernel,
        grid=(rows // step,),
        in_specs=[by_rows(step, width)] * 5
        + [whole(vectors.shape)]
        + [whole(ups[0].shape)] * 2
        + [whole(downs[0].shape)] * 2
        + [tile_spec_of(parcels[0])] * 2,
        out_specs=[by_rows(step, width)] * 2
        + [by_rows(step, units)] * 4
        + [by_rows(step, width)] * 2
        + [whole((8, width))],
        out_shape=[high, jax.ShapeDtypeStruct((rows, width), bf16)]
        + [low] * 4
        + [high, high, jax.ShapeDtypeStruct((8, width), f32)],
        name="feed_first",
        compiler_params=params(30),
        cost_estimate=cost(18),
    )(*attns, base, cot, vectors, *ups, *downs, *parcels)


def feed_second(norm, mid, cot, vectors, ffn, back, one, two, parcels):
    rows, width = mid.shape
    units = one.shape[2]
    piece = parcels[0].shape[0] - TILE
    step = FEED_STEP
    low = jax.ShapeDtypeStruct((rows, units), bf16)
    return pl.pallas_call(
        feed_second_kernel,
        grid=(rows // step,),
        in_specs=[by_rows(step, width)] * 3
        + [whole(vectors.shape)]
        + [by_rows(step, width)] * 2
        + [whole(one.shape)] * 2
        + [tile_spec_of(parcels[0])] * 2,
        out_specs=[by_rows(step, units)] * 4
        + [by_rows(step, width)] * 2
        + [whole((8, width))]
        + [whole((piece, width))] * (rows // piece),
        out_shape=[low] * 4
        + [
            jax.ShapeDtypeStruct((rows, width), f32),
            jax.ShapeDtypeStruct((rows, width), bf16),
            jax.ShapeDtypeStruct((8, width), f32),
        ]
        + [jax.ShapeDtypeStruct((piece, width), bf16)] * (rows // piece),
        name="feed_second",
        compiler_params=params(30),
        cost_estimate=cost(20),
    )(norm, mid, cot, vectors, ffn, back, one, two, *parcels)


def feed_grad_kernel(act_ref, norm_ref, cot_ref, gate_ref, *refs):
    down_ref, up_ref = refs[-2:]
    down = dot_tn(act_ref[...], cot_ref[...])
    if len(refs) > 2:
        down = down + refs[0][...].astype(f32)
    down_ref[...] = down.astype(bf16)
    up = dot_tn(norm_ref[...], gate_ref[...])
    if len(refs) > 2:
        up = up + refs[1][...].astype(f32)
    up_ref[...] = up.astype(bf16)


def feed_grads(act, norm, cot, gate, *shares):
    units, width = act.shape[1], norm.shape[1]
    return pl.pallas_call(
        feed_grad_kernel,
        out_shape=[
            jax.ShapeDtypeStruct((units, width), bf16),
            jax.ShapeDtypeStruct((width, units), bf16),
        ],
        name="feed_grads",
        compiler_params=params(16),
        cost_estimate=cost(5),
    )(act, norm, cot, gate, *shares)


def finish_kernel(count, *refs):
    backs, refs = refs[:count], refs[count:]
    base_ref, mid_grad_ref, gain_ref, t0, t1, t2, t3, table_ref, sums_ref, *pieces = refs
    step = pl.program_id(0)
    piece = base_ref.shape[0]
    back = sum(ref[...] for ref in backs)
    unit, inverse = normalise(base_ref[...])
    grad = mid_grad_ref[...] + norm_back(back * gain_ref[...], unit, inverse)
    low = grad.astype(bf16)
    tile = t0[...]
    for k, other in enumerate((t1, t2, t3)):
        tile = jnp.where(step == k + 1, other[...], tile)
    onehot = onehot_of(tile, table_ref.shape[0], piece)
    total = 0.0
    for part in split_three(grad):
        total = total + dot(onehot, part)
    add_sums(table_ref, total)
    add_sums(sums_ref, rows_of(column_sum(back * unit), column_sum(back)))
    for k, out_ref in enumerate(pieces):

        @pl.when(step == k)
        def _():
            out_ref[...] = low


def finish(backs, base, mid_grad, gain, parcels, table_rows):
    rows, width = base.shape
    step = parcels[0].shape[0] - TILE
    return pl.pallas_call(
        functools.partial(finish_kernel, len(backs)),
        grid=(rows // step,),
        in_specs=[by_rows(step, width)] * (len(backs) + 2)
        + [whole(gain.shape)]
        + [tile_spec_of(parcels[0])] * 4,
        out_specs=[whole((table_rows, width)), whole((8, width))]
        + [whole((step, width))] * (rows // step),
        out_shape=[
            jax.ShapeDtypeStruct((table_rows, width), f32),
            jax.ShapeDtypeStruct((8, width), f32),
        ]
        + [jax.ShapeDtypeStruct((step, width), bf16)] * (rows // step),
        name="finish",
        compiler_params=params(16),
        cost_estimate=cost(5),
    )(*backs, base, mid_grad, gain, *parcels)


def place_kernel(axis, shift, count, *refs):
    pieces, outs = refs[:count], refs[count:]
    rank = lax.axis_index(axis) >> shift
    for distance, piece in enumerate(pieces):
        for which, out_ref in enumerate(outs):
            part = piece[which] if len(outs) > 1 else piece[...]
            out_ref[rank ^ distance] = part.astype(out_ref.dtype)


def place(pieces, dtype, axis, shift, arrays=1):
    count = len(pieces)
    shape = pieces[0].shape[1:] if arrays > 1 else pieces[0].shape
    outs = pl.pallas_call(
        functools.partial(place_kernel, axis, shift, count),
        out_shape=[jax.ShapeDtypeStruct((count,) + shape, dtype)] * arrays,
        name="place",
        compiler_params=params(12),
        cost_estimate=cost(2),
    )(*pieces)
    return outs if arrays > 1 else outs[0]


def interleave_kernel(mine_ref, other_ref, out_ref):
    bit = lax.axis_index("dp") & 1
    for k in range(mine_ref.shape[0]):
        out_ref[2 * k + bit] = mine_ref[k].astype(out_ref.dtype)
        out_ref[2 * k + 1 - bit] = other_ref[k].astype(out_ref.dtype)


def interleave(mine, other):
    count, segment, width = mine.shape
    out = pl.pallas_call(
        interleave_kernel,
        out_shape=jax.ShapeDtypeStruct((2 * count, segment, width), f32),
        name="interleave",
        compiler_params=params(12),
        cost_estimate=cost(2),
    )(mine, other[: count * segment].reshape(mine.shape))
    return out.reshape(2 * count * segment, width)


def on_device(
    hidden_in,
    codon_ids,
    start_flags,
    cotangent,
    codon_table,
    norm1_gain,
    norm1_bias,
    qkv_weight,
    qkv_bias,
    out_weight,
    out_bias,
    norm2_gain,
    norm2_bias,
    up_weight,
    up_bias,
    down_weight,
    down_bias,
):
    gene_count, piece, width = hidden_in.shape
    group = lax.axis_size("tensor")
    rank = lax.axis_index("tensor")
    local = qkv_weight.shape[2]
    heads = local // HEAD_DIM
    table_rows = codon_table.shape[0]

    spread_bias = jnp.broadcast_to(
        qkv_bias.reshape(3, heads, 1, HEAD_DIM), (3, heads, 2, HEAD_DIM)
    ).reshape(3, 2 * local)
    spread_bias = jnp.pad(spread_bias, ((0, 5), (0, width - 2 * local)))
    own = make_parcels(hidden_in, codon_ids, start_flags, spread_bias, up_bias[None])
    turned = qkv_weight.transpose(1, 2, 0).reshape(3, heads, HEAD_DIM, width)
    mixed = jnp.concatenate(
        [turned.transpose(1, 0, 2, 3), out_weight.reshape(heads, 1, HEAD_DIM, width)], 1
    )
    blocks = (mixed.reshape(4 * local, width), up_weight, down_weight)
    bit = lax.axis_index("dp") & 1
    half = width // 2

    def half_of(block):
        return lax.dynamic_slice_in_dim(block, bit * half, half, 0)

    def join(one, two):
        return jnp.where(
            bit == 0, jnp.concatenate([one, two], -2), jnp.concatenate([two, one], -2)
        )

    def as_mix(block):
        return block.reshape(heads, 4, HEAD_DIM, width)

    def flat(item):
        return item.reshape(-1, width)

    own_cot = [pick(cotangent, rank ^ r) for r in range(group)]
    cot_stack = jnp.stack(own_cot[2:])
    feed_half = jnp.stack([half_of(blocks[1]), half_of(blocks[2])])

    frequencies = 10000.0 ** (-jnp.arange(HEAD_DIM // 2, dtype=f32) * 2.0 / HEAD_DIM)
    positions = jnp.concatenate(
        [((rank ^ r) * piece + jnp.arange(piece)).astype(f32) for r in range(group)]
    )
    angles = positions[:, None] * frequencies[None, :]
    cosines, sines = jnp.cos(angles), jnp.sin(angles)
    tables = (jnp.concatenate([cosines] * 4, 1), jnp.concatenate([-sines, sines] * 2, 1))
    tables_back = (cosines.T, sines.T)

    def local_work():
        return tables, tables_back, half_of(blocks[0]), feed_half, own_cot, cot_stack

    got, (tables, tables_back, mix_half, feed_half, own_cot, cot_stack) = stage(
        [(own[r], "tensor", r) for r in (2, 3, 1)] + [(blocks[0], "tensor", 1)], local_work
    )
    parcels = [own[0], got[2], got[0], got[1]]
    mixes = [as_mix(blocks[0]), as_mix(got[3])]
    early, late, every = (0, 1), (1, heads - 1), (0, heads)

    def first_heads(parcels):
        base, norm1 = embed(parcels, codon_table, norm1_gain[None], norm1_bias[None])
        return base, norm1, attend(norm1, *mixes[:2], *parcels[:2], tables, early)

    got, (base, norm1, (*kept0, attn0)) = stage(
        [(mix_half, "tensor", 2), (blocks[1], "tensor", 1), (blocks[2], "tensor", 1)],
        first_heads,
        parcels,
    )
    mix_half, *mates = got
    (mix_other, cot_across), (*kept1, attn1) = stage(
        [(mix_half, "dp", 1), (cot_stack, "tensor", 2)],
        lambda norm: attend(norm, *mixes[:2], *parcels[:2], tables, late),
        norm1,
    )
    across_mix = join(mix_half, mix_other)
    (across_mate, got), _ = stage(
        [(across_mix, "tensor", 1), mate_transfer(own_cot, cot_across)], lambda: ()
    )
    mixes += [as_mix(across_mix), as_mix(across_mate)]
    cot = jnp.concatenate(four(own_cot, cot_across, got), 0)
    (feed_half,), (*kept2, attn2) = stage(
        [(feed_half, "tensor", 2)],
        lambda norm: attend(norm, *mixes[2:], *parcels[2:], tables, every),
        norm1,
    )
    vectors = jnp.stack([out_bias, norm2_gain, norm2_bias, down_bias])

    def feed_near(base, cot):
        results = feed_first(
            (attn0, attn1, attn2), base, cot, vectors,
            (up_weight, mates[0]), (down_weight, mates[1]), parcels[:2],
        )
        return results, feed_grads(results[3], results[1], cot, results[5])

    (feed_other,), (results, sent) = stage([(feed_half, "dp", 1)], feed_near, base, cot)
    mid, norm2, act0, act1, gate0, gate1, ffn, back, sums_first = results
    sent, feed_across = stage(
        [(item, "tensor", 1) for item in sent], lambda one, two: join(one, two), feed_half, feed_other
    )
    (feed_mate,), near = stage(
        [(feed_across, "tensor", 1)], lambda: feed_grads(act0, norm2, cot, gate0, *sent)
    )
    keep_near, send_near = halve_two(*near)

    def feed_far(ffn):
        results = feed_second(
            norm2, mid, cot, vectors, ffn, back, feed_across, feed_mate, parcels[2:]
        )
        return results, feed_grads(results[1], norm2, cot, results[3])

    (got_near,), (results, sent) = stage([(send_near, "dp", 1)], feed_far, ffn)
    act2, act3, gate2, gate3, mid_grad, grad_low, sums_second, *out_pieces = results
    sent, near = stage(
        [(item, "tensor", 1) for item in sent], lambda *pair: add_low(*pair), keep_near, got_near
    )
    keep_far, send_far = halve_two(*feed_grads(act2, norm2, cot, gate2, *sent))

    def back_part(saved, block, span):
        return lambda grad: attend_back(
            saved, grad, norm1, mixes[block], mixes[block + 1], tables_back, span
        )

    near_steps = Scatter(near, 1)
    (got_far, out_across, *near_got), (mix2, mix3, back_a, bias_far) = stage(
        [(send_far, "dp", 1), (jnp.stack(out_pieces[2:]), "tensor", 2)] + near_steps.transfers(),
        back_part(kept2, 2, every),
        grad_low,
    )
    near_piece = near_steps.finish(near_got)
    far_steps = Scatter(add_low(keep_far, got_far), 1)
    (got, out_got), _ = stage(
        [(mix3, "tensor", 1), mate_transfer(out_pieces, out_across)], lambda: ()
    )
    far_mix = add_low(mix2, got)
    (cross_b, *far_got), (mix0a, mix1a, back_c, bias_c) = stage(
        [(far_mix[1:], "tensor", 2)] + far_steps.transfers(), back_part(kept1, 0, late), grad_low
    )
    far_piece = far_steps.finish(far_got)
    (feed_cross, cross_a, got), (mix0b, mix1b, back_d, bias_d) = stage(
        [(far_piece, "tensor", 2), (far_mix[:1], "tensor", 2), (mix1a, "tensor", 1)],
        back_part(kept0, 0, early),
        grad_low,
    )
    mix_a = add_low(mix0a, got, cross_b)
    feed_piece = add_low(near_piece, feed_cross)
    (got,), _ = stage([(mix1b, "tensor", 1)], lambda: feed_piece)
    mix_b = add_low(mix0b, got, cross_a)
    keep_mix, send_mix = halve(flat(jnp.concatenate([mix_b, mix_a], 0)))
    (mix_got, *feed_got), (table_part, sums_last, *grad_pieces) = stage(
        [(send_mix, "dp", 1)] + upper_transfers(feed_piece),
        lambda mid_grad: finish(
            (back_a, back_c, back_d), base, mid_grad, norm1_gain[None], parcels, table_rows
        ),
        mid_grad,
    )
    bias_near = jnp.concatenate([bias_d, bias_c], 0)

    def by_owner(blocks):
        swapped = jnp.where(rank & 1 == 1, blocks[jnp.array([1, 0, 3, 2])], blocks)
        return jnp.where(rank & 2 == 2, swapped[jnp.array([2, 3, 0, 1])], swapped)

    up_rows = by_owner(jnp.concatenate([sums_first[:2], sums_second[:2]], 0))
    qkv_rows = jnp.stack([bias_near, bias_far])[:, :, 0].reshape(2, heads, 3, 2, HEAD_DIM)
    qkv_rows = qkv_rows.transpose(0, 3, 2, 1, 4).reshape(group, 3, local)
    qkv_rows = by_owner(qkv_rows).transpose(1, 0, 2).reshape(3, width)
    vectors = jnp.concatenate([sums_last[:2], sums_second[2:6], up_rows, qkv_rows], 0)
    vectors = jnp.pad(vectors, ((0, 32 - vectors.shape[0]), (0, 0)))
    small = jnp.concatenate([table_part.astype(bf16), vectors.astype(bf16)], 0)
    core = rank & 1
    count = small.shape[0] // 2
    small_keep = lax.dynamic_slice_in_dim(small, core * count, count, 0)
    small_send = lax.dynamic_slice_in_dim(small, (1 - core) * count, count, 0)
    (got,), ((down_part, up_part), mix_keep) = stage(
        [(small_send, "tensor", 1)],
        lambda pieces: (place(pieces, bf16, "dp", 1, 2), add_low(keep_mix, mix_got)),
        [feed_piece] + feed_got,
    )
    small = add_low(small_keep, got)
    mix_steps = Scatter(mix_keep)
    to_other = jnp.concatenate(grad_pieces[2:] + [small], 0)
    (crossed, down_other, *mix_got), _ = stage(
        [(to_other, "tensor", 2), (flat(down_part), "dp", 1)] + mix_steps.transfers(), lambda: ()
    )
    small = add_low(small, crossed[2 * piece :])
    grad_across = [crossed[:piece], crossed[piece : 2 * piece]]
    mix_piece = mix_steps.finish(mix_got)
    segment = mix_piece.shape[0]
    (grad_got, up_other, *got), down_grad = stage(
        [mate_transfer(grad_pieces, grad_across), (flat(up_part), "dp", 1)]
        + upper_transfers(jnp.concatenate([mix_piece, small], 0)),
        interleave,
        down_part,
        down_other,
    )
    small = add_low(small, *[item[segment:] for item in got])
    mix_part = place([mix_piece] + [item[:segment] for item in got], bf16, "dp", 1)
    (other,), (up_grad, hidden_grad) = stage(
        [(jnp.concatenate([flat(mix_part), small], 0), "dp", 1)],
        lambda part, rows, pieces: (interleave(part, rows), place(pieces, f32, "tensor", 0)),
        up_part,
        up_other,
        four(grad_pieces, grad_across, grad_got),
    )
    size = flat(mix_part).shape[0]
    small = add_low(small, other[size:])
    (other_half,), (mix_grad, hidden_out) = stage(
        [(small, "tensor", 1)],
        lambda part, rows, pieces: (interleave(part, rows), place(pieces, bf16, "tensor", 0)),
        mix_part,
        other,
        four(out_pieces, out_across, out_got),
    )
    small = jnp.where(
        core == 0,
        jnp.concatenate([small, other_half], 0),
        jnp.concatenate([other_half, small], 0),
    ).astype(f32)
    mix_grad = mix_grad.reshape(heads, 4, HEAD_DIM, width)
    qkv_grad = mix_grad[:, :3].transpose(3, 1, 0, 2).reshape(width, 3, local)
    out_grad = mix_grad[:, 3].reshape(local, width)
    at = table_rows
    rows = [small[at + k] for k in range(6)]
    up_bias_grad = lax.dynamic_index_in_dim(small[at + 6 : at + 6 + group], rank, 0, keepdims=False)
    qkv_bias_grad = lax.dynamic_slice_in_dim(
        small[at + 6 + group : at + 9 + group], rank * local, local, 1
    )
    return (
        hidden_out,
        hidden_grad,
        small[:table_rows],
        rows[0],
        rows[1],
        qkv_grad,
        qkv_bias_grad,
        out_grad,
        rows[4],
        rows[2],
        rows[3],
        up_grad,
        up_bias_grad,
        down_grad,
        rows[5],
    )


def solution(mesh):
    rows_placed = P("dp", "tensor", None)
    return jax.shard_map(
        on_device,
        mesh=mesh,
        in_specs=(
            rows_placed,
            P("dp", "tensor"),
            P("dp", "tensor"),
            rows_placed,
            P(),
            P(),
            P(),
            P(None, None, "tensor"),
            P(None, "tensor"),
            P("tensor", None),
            P(),
            P(),
            P(),
            P(None, "tensor"),
            P("tensor"),
            P("tensor", None),
            P(),
        ),
        out_specs=(
            rows_placed,
            rows_placed,
            P(),
            P(),
            P(),
            P(None, None, "tensor"),
            P(None, "tensor"),
            P("tensor", None),
            P(),
            P(),
            P(),
            P(None, "tensor"),
            P("tensor"),
            P("tensor", None),
            P(),
        ),
        check_vma=False,
    )
```

```python
import functools

import jax
import jax.numpy as jnp
from jax import lax
from jax.experimental import pallas as pl
from jax.experimental.pallas import tpu as pltpu
from jax.sharding import PartitionSpec as P

HEAD_DIM = 64
PAIR = 2 * HEAD_DIM
EPSILON = 1e-05
HIGHEST = lax.Precision.HIGHEST
NT = (((1,), (1,)), ((), ()))
TN = (((0,), (0,)), ((), ()))
LOG2E = 1.4426950408889634
TILE = 16
UP_ROW = 10
TABLE_HALF = 64
BIAS_HEADS = 3
SOFT_ROWS = 128
FEED_STEP = 256
bf16 = jnp.bfloat16
f32 = jnp.float32


def params(mebibytes):
    return pltpu.CompilerParams(vmem_limit_bytes=mebibytes * 1024 * 1024)


def cost(microseconds):
    return pl.CostEstimate(
        flops=microseconds * 10**9, bytes_accessed=microseconds * 10**6, transcendentals=0
    )


def dot(left, right):
    return jnp.dot(left, right, preferred_element_type=f32)


def dot_nt(left, right):
    return lax.dot_general(left, right, NT, preferred_element_type=f32)


def dot_tn(left, right):
    return lax.dot_general(left, right, TN, preferred_element_type=f32)


def whole(shape):
    return pl.BlockSpec(shape, lambda i: (0,) * len(shape))


def by_rows(rows, cols):
    return pl.BlockSpec((rows, cols), lambda i: (i, 0))


def by_cols(rows, cols):
    return pl.BlockSpec((rows, cols), lambda i: (0, i))


def swap(array_in, axis, distance):
    size = lax.axis_size(axis)
    return lax.ppermute(array_in, axis, [(i, i ^ distance) for i in range(size)])


def together(items):
    return lax.optimization_barrier(items)


def stage(sends, work, *inputs):
    arrays, inputs = together(([item[0] for item in sends], inputs))
    got = [swap(array, axis, distance) for array, (_, axis, distance) in zip(arrays, sends)]
    return together((got, work(*inputs)))


def add_low(*terms):
    return sum(term.astype(f32) for term in terms).astype(bf16)


def core_sum(mine, other):
    return add_low(mine, swap(other, "tensor", 1))


def halve(rows):
    size = lax.axis_size("dp")
    segment = rows.shape[0] // size
    halves = rows.reshape(size // 2, 2, segment, rows.shape[1])
    mine = lax.axis_index("dp") & 1
    keep = lax.dynamic_index_in_dim(halves, mine, 1, keepdims=False)
    send = lax.dynamic_index_in_dim(halves, 1 - mine, 1, keepdims=False)
    return keep, send


def halve_two(one, two):
    (keep_one, send_one), (keep_two, send_two) = halve(one), halve(two)
    return jnp.stack([keep_one, keep_two]), jnp.stack([send_one, send_two])


def pick(array_in, index):
    return lax.dynamic_index_in_dim(array_in, index, 0, keepdims=False)


class Scatter:
    def __init__(self, current, axis=0):
        self.row = lax.axis_index("dp") >> 1
        self.own, *self.sends = (
            lax.dynamic_index_in_dim(current, self.row ^ j, axis, keepdims=False)
            for j in range(current.shape[axis])
        )

    def transfers(self):
        return [(item, "dp", 2 * j + 2) for j, item in enumerate(self.sends)]

    def finish(self, got):
        return add_low(self.own, *got)


def upper_transfers(segment):
    return [(segment, "dp", 2 * j) for j in range(1, lax.axis_size("dp") // 2)]


def mate_transfer(pieces, crossed):
    return (jnp.stack([pieces[1], crossed[1]]), "tensor", 1)


def four(pieces, crossed, got):
    return [pieces[0], got[0], crossed[0], got[1]]


def normalise(row_data):
    row_mean = jnp.mean(row_data, axis=-1, keepdims=True)
    centred = row_data - row_mean
    row_var = jnp.mean(centred * centred, axis=-1, keepdims=True)
    inverse = lax.rsqrt(row_var + EPSILON)
    return centred * inverse, inverse


def norm_back(scaled, unit, inverse):
    return inverse * (
        scaled
        - jnp.mean(scaled, -1, keepdims=True)
        - unit * jnp.mean(scaled * unit, -1, keepdims=True)
    )


def column_sum(array_in):
    return jnp.sum(array_in, 0, keepdims=True)


def rows_of(*vectors):
    width = vectors[0].shape[1]
    at = lax.broadcasted_iota(jnp.int32, (8, width), 0)
    tile = jnp.zeros((8, width), f32)
    for k, vector in enumerate(vectors):
        tile = jnp.where(at == k, vector, tile)
    return tile


def first_head(rows):
    return lax.broadcasted_iota(jnp.int32, (rows, PAIR), 1) < HEAD_DIM


def turn(values_in, cosines, sines):
    lanes = lax.broadcasted_iota(jnp.int32, values_in.shape, 1)
    lower = (lanes & (HEAD_DIM - 1)) < HEAD_DIM // 2
    other = jnp.where(
        lower,
        pltpu.roll(values_in, PAIR - HEAD_DIM // 2, 1),
        pltpu.roll(values_in, HEAD_DIM // 2, 1),
    )
    return values_in * cosines + other * sines


def unturn(values_in, cosines, sines):
    quarter = HEAD_DIM // 2
    parts = [values_in[k * quarter : (k + 1) * quarter] for k in range(4)]
    out = []
    for low, high in (parts[:2], parts[2:]):
        out += [low * cosines + high * sines, high * cosines - low * sines]
    return jnp.concatenate(out, 0)


def split_three(values_in):
    high = values_in.astype(bf16)
    rest = values_in - high.astype(f32)
    middle = rest.astype(bf16)
    return high, middle, (rest - middle.astype(f32)).astype(bf16)


def parcel_kernel(hidden_ref, ids_ref, flags_ref, bias_ref, up_ref, *outs):
    rank = lax.axis_index("tensor")
    piece, width = hidden_ref.shape[1:]
    at = lax.broadcasted_iota(jnp.int32, (TILE, width), 0)
    tile = jnp.where(at == UP_ROW, up_ref[...].astype(f32), 0.0)
    rest = bias_ref[...]
    for part in range(3):
        high = rest.astype(bf16).astype(f32)
        rest = rest - high
        for k in range(3):
            tile = jnp.where(at == 1 + 3 * part + k, high[k : k + 1], tile)
    for distance, out_ref in enumerate(outs):
        gene = rank ^ distance
        out_ref[:piece] = hidden_ref[gene]
        index = (ids_ref[pl.ds(gene, 1)] + TABLE_HALF * flags_ref[pl.ds(gene, 1)]).astype(f32)
        index = jnp.concatenate([index, jnp.zeros((1, width - piece), f32)], 1)
        out_ref[piece:] = jnp.where(at == 0, index, tile).astype(bf16)


def make_parcels(hidden_in, codon_ids, start_flags, bias, up_bias):
    genes, piece, width = hidden_in.shape
    shape = jax.ShapeDtypeStruct((piece + TILE, width), bf16)
    return pl.pallas_call(
        parcel_kernel,
        out_shape=[shape] * genes,
        name="parcels",
        compiler_params=params(8),
        cost_estimate=cost(2),
    )(hidden_in, codon_ids, start_flags, bias, up_bias)


def onehot_of(tile, table_rows, piece):
    index = tile[0:1, :piece].astype(f32)
    at = lax.broadcasted_iota(jnp.int32, (table_rows, piece), 0).astype(f32)
    return (at == index).astype(bf16)


def embed_kernel(p0, p1, p2, p3, table_ref, gain_ref, shift_ref, base_ref, norm_ref, held):
    step = pl.program_id(0)
    piece = base_ref.shape[0]
    for k, parcel in enumerate((p0, p1, p2, p3)):

        @pl.when(step == k)
        def _():
            held[...] = parcel[...]

    onehot = onehot_of(held[piece:], table_ref.shape[0], piece)
    base = held[:piece].astype(f32)
    for part in split_three(table_ref[...]):
        base = base + dot_tn(onehot, part)
    unit, _ = normalise(base)
    base_ref[...] = base
    norm_ref[...] = (unit * gain_ref[...] + shift_ref[...]).astype(bf16)


def embed(parcels, table, gain, shift):
    rows, width = parcels[0].shape
    piece = rows - TILE
    return pl.pallas_call(
        embed_kernel,
        grid=(len(parcels),),
        in_specs=[whole(parcels[0].shape)] * 4
        + [whole(table.shape), whole(gain.shape), whole(shift.shape)],
        out_specs=[by_rows(piece, width)] * 2,
        out_shape=[
            jax.ShapeDtypeStruct((4 * piece, width), f32),
            jax.ShapeDtypeStruct((4 * piece, width), bf16),
        ],
        scratch_shapes=[pltpu.VMEM((rows, width), bf16)],
        name="embed",
        compiler_params=params(16),
        cost_estimate=cost(4),
    )(*parcels, table, gain, shift)


def pair_rows(a_ref, b_ref, parts):
    return jnp.concatenate([ref[0, part] for part in parts for ref in (a_ref, b_ref)], 0)


def attend_kernel(
    base, norm_ref, a_ref, b_ref, ta_ref, tb_ref, cos_ref, sin_ref,
    q_ref, k_ref, v_ref, context_ref, inverse_ref, exps_ref, attn_ref, biases, scores_ref,
):
    step = pl.program_id(0)
    for head in range(BIAS_HEADS):

        @pl.when(step + base == head)
        def _():
            vectors = []
            lanes = slice(head * PAIR, (head + 1) * PAIR)
            for k in range(3):
                two = []
                for tile in (ta_ref, tb_ref):
                    high = tile[...].astype(f32)[:, lanes]
                    two.append(high[1 + k : 2 + k] + high[4 + k : 5 + k] + high[7 + k : 8 + k])
                vectors.append(jnp.where(first_head(1), two[0], two[1]))
            biases[...] = rows_of(*vectors)

    rows = norm_ref.shape[0]
    product = dot_nt(norm_ref[...], pair_rows(a_ref, b_ref, (0, 1, 2)))
    bias = biases[...]
    cosines, sines = cos_ref[...], sin_ref[...]
    query = turn(product[:, :PAIR] + bias[0:1], cosines, sines).astype(bf16)
    query = query * jnp.asarray(HEAD_DIM**-0.5, bf16)
    keys = turn(product[:, PAIR : 2 * PAIR] + bias[1:2], cosines, sines).astype(bf16)
    values = (product[:, 2 * PAIR :] + bias[2:3]).astype(bf16)
    q_ref[...] = query
    k_ref[...] = keys
    v_ref[...] = values
    values = jnp.concatenate([values, jnp.ones((rows, PAIR), bf16)], 1)
    first = first_head(rows)
    for head in range(2):
        only = jnp.where(first == (head == 0), query, jnp.zeros_like(query))
        scores_ref[head] = dot_nt(only, keys)
    outs = []
    for head in range(2):
        for start in range(0, rows, SOFT_ROWS):
            span = slice(start, start + SOFT_ROWS)
            scores = scores_ref[head, span]
            top = jnp.max(scores, 1, keepdims=True) * LOG2E
            exps_ref[head, span] = jnp.exp2(scores * LOG2E - top).astype(bf16)
        outs.append(dot(exps_ref[head], values))
    inverse = 1.0 / jnp.where(first, outs[0][:, PAIR:], outs[1][:, PAIR:])
    context = (jnp.where(first, outs[0][:, :PAIR], outs[1][:, :PAIR]) * inverse).astype(bf16)
    inverse_ref[...] = inverse
    context_ref[...] = context
    more = dot(context, pair_rows(a_ref, b_ref, (3,)))

    @pl.when(step == 0)
    def _():
        attn_ref[...] = more

    @pl.when(step != 0)
    def _():
        attn_ref[...] += more


def attend(norm, a, b, tile_a, tile_b, tables, heads):
    rows, width = norm.shape
    base, pairs = heads
    low = jax.ShapeDtypeStruct((rows, pairs * PAIR), bf16)
    return pl.pallas_call(
        functools.partial(attend_kernel, base),
        grid=(pairs,),
        in_specs=[whole(norm.shape)]
        + [pl.BlockSpec((1,) + a.shape[1:], lambda i: (i + base, 0, 0, 0))] * 2
        + [tile_spec_of(tile_a)] * 2
        + [whole((rows, PAIR))] * 2,
        out_specs=[by_cols(rows, PAIR)] * 5
        + [pl.BlockSpec((2, rows, rows), lambda i: (i, 0, 0)), whole((rows, width))],
        out_shape=[low] * 4
        + [
            jax.ShapeDtypeStruct((rows, pairs * PAIR), f32),
            jax.ShapeDtypeStruct((2 * pairs, rows, rows), bf16),
            jax.ShapeDtypeStruct((rows, width), f32),
        ],
        scratch_shapes=[pltpu.VMEM((8, PAIR), f32), pltpu.VMEM((2, rows, rows), f32)],
        name="attend",
        compiler_params=params(44),
        cost_estimate=cost(8 * pairs),
    )(norm, a, b, tile_a, tile_b, *tables)


def attend_back_kernel(
    q_ref, k_ref, v_ref, context_ref, inverse_ref, exps_ref, grad_ref, norm_ref,
    a_ref, b_ref, cos_ref, sin_ref, out_a, out_b, back_ref, bias_ref, probs_ref, scores_ref,
):
    step = pl.program_id(0)
    rows = q_ref.shape[0]
    values = v_ref[...]
    first = first_head(rows)
    grad = dot_nt(grad_ref[...], pair_rows(a_ref, b_ref, (3,))) * inverse_ref[...]
    terms = grad * context_ref[...].astype(f32)
    inners = [
        jnp.sum(jnp.where(first == (head == 0), terms, 0.0), 1, keepdims=True) for head in range(2)
    ]
    grad = grad.astype(bf16)
    for head in range(2):
        only = jnp.where(first == (head == 0), grad, jnp.zeros_like(grad))
        probs_ref[head] = dot_nt(only, values)
    grad_turned, query_turned, keys_turned = grad.T, q_ref[...].T, k_ref[...].T
    turned = [[], [], []]
    for head in range(2):
        part = slice(head * HEAD_DIM, (head + 1) * HEAD_DIM)
        turned[2].append(dot(grad_turned[part], exps_ref[head]))
        for start in range(0, rows, SOFT_ROWS):
            span = slice(start, start + SOFT_ROWS)
            low = exps_ref[head, span].astype(f32) * (probs_ref[head, span] - inners[head][span])
            scores_ref[head, span] = low.astype(bf16)
        turned[0].append(dot_nt(keys_turned[part], scores_ref[head]))
        turned[1].append(dot(query_turned[part], scores_ref[head]))
    dq, dk, dv = (jnp.concatenate(item, 0) for item in turned)
    dq = unturn(dq * HEAD_DIM**-0.5, cos_ref[...], sin_ref[...])
    dk = unturn(dk, cos_ref[...], sin_ref[...])
    left = jnp.concatenate([dq, dk, dv], 0).astype(bf16)
    more = dot_tn(left, pair_rows(a_ref, b_ref, (0, 1, 2)))

    @pl.when(step == 0)
    def _():
        back_ref[...] = more

    @pl.when(step != 0)
    def _():
        back_ref[...] += more

    bias_ref[0] = dot_nt(jnp.ones((8, rows), bf16), left)
    inputs = dot(left, norm_ref[...]).astype(bf16)
    outputs = dot_tn(context_ref[...], grad_ref[...]).astype(bf16)
    for k in range(4):
        result = outputs if k == 3 else inputs[k * PAIR : (k + 1) * PAIR]
        out_a[0, k] = result[:HEAD_DIM]
        out_b[0, k] = result[HEAD_DIM:]


def attend_back(kept, grad, norm, a, b, tables, heads):
    query, keys, values, context, inverse, exps = kept
    rows, width = norm.shape
    base, count = heads
    shape = (count,) + a.shape[1:]
    columns = by_cols(rows, PAIR)
    weights = pl.BlockSpec((1,) + a.shape[1:], lambda i: (i + base, 0, 0, 0))
    return pl.pallas_call(
        attend_back_kernel,
        grid=(count,),
        in_specs=[columns] * 5
        + [pl.BlockSpec((2, rows, rows), lambda i: (i, 0, 0))]
        + [whole(norm.shape)] * 2
        + [weights] * 2
        + [whole(tables[0].shape)] * 2,
        out_specs=[pl.BlockSpec((1,) + a.shape[1:], lambda i: (i, 0, 0, 0))] * 2
        + [whole((rows, width)), pl.BlockSpec((1, 8, 3 * PAIR), lambda i: (i, 0, 0))],
        out_shape=[jax.ShapeDtypeStruct(shape, bf16)] * 2
        + [
            jax.ShapeDtypeStruct((rows, width), f32),
            jax.ShapeDtypeStruct((count, 8, 3 * PAIR), f32),
        ],
        scratch_shapes=[pltpu.VMEM((2, rows, rows), f32), pltpu.VMEM((2, rows, rows), bf16)],
        name="attend_back",
        compiler_params=params(50),
        cost_estimate=cost(9 * count),
    )(query, keys, values, context, inverse, exps, grad, norm, a, b, *tables)


def gelu_parts(gate):
    bell = jnp.exp2(gate * gate * (-0.5 * LOG2E))
    span = 1.0 + jnp.abs(gate) * (0.3275911 * 0.5**0.5)
    guess = pl.reciprocal(span, approx=True)
    near = guess * (2.0 - span * guess)
    tail = 1.061405429 * 0.5
    for factor in (-1.453152027, 1.421413741, -0.284496736, 0.254829592):
        tail = tail * near + factor * 0.5
    tail = tail * near * bell
    return jnp.where(gate >= 0, 1.0 - tail, tail), bell * 0.3989422804014327


def feed_block(norm, cot, up_ref, down_ref, tile, act_ref, gate_ref):
    chunk = 256
    units = up_ref.shape[1]
    spans = [slice(start, start + chunk) for start in range(0, units, chunk)]

    def first_products(span):
        bias = tile[UP_ROW : UP_ROW + 1, span].astype(f32)
        return dot(norm, up_ref[:, span]) + bias, dot_nt(cot, down_ref[span])

    sums = []
    ahead = first_products(spans[0])
    for at, span in enumerate(spans):
        gate, grad = ahead
        if at + 1 < len(spans):
            ahead = first_products(spans[at + 1])
        share, density = gelu_parts(gate)
        low = (grad * (share + gate * density)).astype(bf16)
        act_ref[:, span] = (gate * share).astype(bf16)
        gate_ref[:, span] = low
        sums.append(column_sum(low.astype(f32)))
    ffn = dot(act_ref[...], down_ref[...])
    back = dot_nt(gate_ref[...], up_ref[...])
    return ffn, back, jnp.concatenate(sums, 1)


def add_sums(ref, tile):
    @pl.when(pl.program_id(0) == 0)
    def _():
        ref[...] = tile

    @pl.when(pl.program_id(0) != 0)
    def _():
        ref[...] += tile


def feed_first_kernel(
    attn_a, attn_b, attn_c, base_ref, cot_ref, vec_ref, ua, ub, da, db, ta, tb,
    mid_ref, norm_ref, act_a, act_b, gate_a, gate_b, ffn_ref, back_ref, sums_ref,
):
    out_bias, gain, shift = (vec_ref[k : k + 1] for k in range(3))
    attn = attn_a[...] + attn_b[...] + attn_c[...]
    mid = base_ref[...] + (attn + out_bias)
    unit, _ = normalise(mid)
    norm = (unit * gain + shift).astype(bf16)
    mid_ref[...] = mid
    norm_ref[...] = norm
    cot = cot_ref[...]
    ffn, back, sum_a = feed_block(norm, cot, ua, da, ta[...], act_a, gate_a)
    more, back_more, sum_b = feed_block(norm, cot, ub, db, tb[...], act_b, gate_b)
    ffn_ref[...] = ffn + more
    back_ref[...] = back + back_more
    add_sums(sums_ref, rows_of(sum_a, sum_b))


def feed_second_kernel(
    norm_ref, mid_ref, cot_ref, vec_ref, ffn_ref, back_ref, one, two, ta, tb,
    act_a, act_b, gate_a, gate_b, mid_grad_ref, low_ref, sums_ref, *pieces,
):
    down_bias, gain = vec_ref[3:4], vec_ref[1:2]
    norm, cot = norm_ref[...], cot_ref[...]
    ffn, back, sum_a = feed_block(norm, cot, one.at[0], one.at[1], ta[...], act_a, gate_a)
    more, back_more, sum_b = feed_block(norm, cot, two.at[0], two.at[1], tb[...], act_b, gate_b)
    mid = mid_ref[...]
    out = (mid + (ffn_ref[...] + (ffn + more) + down_bias)).astype(bf16)
    rows = pieces[0].shape[0]
    back = back_ref[...] + (back + back_more)
    unit, inverse = normalise(mid)
    high = cot.astype(f32)
    grad = high + norm_back(back * gain, unit, inverse)
    low = grad.astype(bf16)
    mid_grad_ref[...] = grad
    low_ref[...] = low
    per_step = mid.shape[0] // rows
    for k, piece in enumerate(pieces):

        @pl.when(pl.program_id(0) == k // per_step)
        def _():
            piece[...] = out[k % per_step * rows : (k % per_step + 1) * rows]

    add_sums(
        sums_ref,
        rows_of(
            sum_a,
            sum_b,
            column_sum(back * unit),
            column_sum(back),
            column_sum(low.astype(f32)),
            column_sum(high),
        ),
    )


def tile_spec_of(parcel):
    at = parcel.shape[0] // TILE - 1
    return pl.BlockSpec((TILE, parcel.shape[1]), lambda i: (at, 0))


def feed_first(attns, base, cot, vectors, ups, downs, parcels):
    rows, width = base.shape
    units = ups[0].shape[1]
    piece = parcels[0].shape[0] - TILE
    step = FEED_STEP
    low = jax.ShapeDtypeStruct((rows, units), bf16)
    high = jax.ShapeDtypeStruct((rows, width), f32)
    return pl.pallas_call(
        feed_first_kernel,
        grid=(rows // step,),
        in_specs=[by_rows(step, width)] * 5
        + [whole(vectors.shape)]
        + [whole(ups[0].shape)] * 2
        + [whole(downs[0].shape)] * 2
        + [tile_spec_of(parcels[0])] * 2,
        out_specs=[by_rows(step, width)] * 2
        + [by_rows(step, units)] * 4
        + [by_rows(step, width)] * 2
        + [whole((8, width))],
        out_shape=[high, jax.ShapeDtypeStruct((rows, width), bf16)]
        + [low] * 4
        + [high, high, jax.ShapeDtypeStruct((8, width), f32)],
        name="feed_first",
        compiler_params=params(30),
        cost_estimate=cost(18),
    )(*attns, base, cot, vectors, *ups, *downs, *parcels)


def feed_second(norm, mid, cot, vectors, ffn, back, one, two, parcels):
    rows, width = mid.shape
    units = one.shape[2]
    piece = parcels[0].shape[0] - TILE
    step = FEED_STEP
    low = jax.ShapeDtypeStruct((rows, units), bf16)
    return pl.pallas_call(
        feed_second_kernel,
        grid=(rows // step,),
        in_specs=[by_rows(step, width)] * 3
        + [whole(vectors.shape)]
        + [by_rows(step, width)] * 2
        + [whole(one.shape)] * 2
        + [tile_spec_of(parcels[0])] * 2,
        out_specs=[by_rows(step, units)] * 4
        + [by_rows(step, width)] * 2
        + [whole((8, width))]
        + [whole((piece, width))] * (rows // piece),
        out_shape=[low] * 4
        + [
            jax.ShapeDtypeStruct((rows, width), f32),
            jax.ShapeDtypeStruct((rows, width), bf16),
            jax.ShapeDtypeStruct((8, width), f32),
        ]
        + [jax.ShapeDtypeStruct((piece, width), bf16)] * (rows // piece),
        name="feed_second",
        compiler_params=params(30),
        cost_estimate=cost(20),
    )(norm, mid, cot, vectors, ffn, back, one, two, *parcels)


def feed_grad_kernel(act_ref, norm_ref, cot_ref, gate_ref, down_ref, up_ref):
    down_ref[...] = dot_tn(act_ref[...], cot_ref[...]).astype(bf16)
    up_ref[...] = dot_tn(norm_ref[...], gate_ref[...]).astype(bf16)


def feed_grads(act, norm, cot, gate):
    units, width = act.shape[1], norm.shape[1]
    return pl.pallas_call(
        feed_grad_kernel,
        out_shape=[
            jax.ShapeDtypeStruct((units, width), bf16),
            jax.ShapeDtypeStruct((width, units), bf16),
        ],
        name="feed_grads",
        compiler_params=params(16),
        cost_estimate=cost(3),
    )(act, norm, cot, gate)


def finish_kernel(count, *refs):
    backs, refs = refs[:count], refs[count:]
    base_ref, mid_grad_ref, gain_ref, t0, t1, t2, t3, table_ref, sums_ref, *pieces = refs
    step = pl.program_id(0)
    piece = base_ref.shape[0]
    back = sum(ref[...] for ref in backs)
    unit, inverse = normalise(base_ref[...])
    grad = mid_grad_ref[...] + norm_back(back * gain_ref[...], unit, inverse)
    low = grad.astype(bf16)
    tile = t0[...]
    for k, other in enumerate((t1, t2, t3)):
        tile = jnp.where(step == k + 1, other[...], tile)
    onehot = onehot_of(tile, table_ref.shape[0], piece)
    total = 0.0
    for part in split_three(grad):
        total = total + dot(onehot, part)
    add_sums(table_ref, total)
    add_sums(sums_ref, rows_of(column_sum(back * unit), column_sum(back)))
    for k, out_ref in enumerate(pieces):

        @pl.when(step == k)
        def _():
            out_ref[...] = low


def finish(backs, base, mid_grad, gain, parcels, table_rows):
    rows, width = base.shape
    step = parcels[0].shape[0] - TILE
    return pl.pallas_call(
        functools.partial(finish_kernel, len(backs)),
        grid=(rows // step,),
        in_specs=[by_rows(step, width)] * (len(backs) + 2)
        + [whole(gain.shape)]
        + [tile_spec_of(parcels[0])] * 4,
        out_specs=[whole((table_rows, width)), whole((8, width))]
        + [whole((step, width))] * (rows // step),
        out_shape=[
            jax.ShapeDtypeStruct((table_rows, width), f32),
            jax.ShapeDtypeStruct((8, width), f32),
        ]
        + [jax.ShapeDtypeStruct((step, width), bf16)] * (rows // step),
        name="finish",
        compiler_params=params(16),
        cost_estimate=cost(5),
    )(*backs, base, mid_grad, gain, *parcels)


def place_kernel(axis, shift, count, *refs):
    pieces, outs = refs[:count], refs[count:]
    rank = lax.axis_index(axis) >> shift
    for distance, piece in enumerate(pieces):
        for which, out_ref in enumerate(outs):
            part = piece[which] if len(outs) > 1 else piece[...]
            out_ref[rank ^ distance] = part.astype(out_ref.dtype)


def place(pieces, dtype, axis, shift, arrays=1):
    count = len(pieces)
    shape = pieces[0].shape[1:] if arrays > 1 else pieces[0].shape
    outs = pl.pallas_call(
        functools.partial(place_kernel, axis, shift, count),
        out_shape=[jax.ShapeDtypeStruct((count,) + shape, dtype)] * arrays,
        name="place",
        compiler_params=params(12),
        cost_estimate=cost(2),
    )(*pieces)
    return outs if arrays > 1 else outs[0]


def interleave_kernel(mine_ref, other_ref, out_ref):
    bit = lax.axis_index("dp") & 1
    for k in range(mine_ref.shape[0]):
        out_ref[2 * k + bit] = mine_ref[k].astype(out_ref.dtype)
        out_ref[2 * k + 1 - bit] = other_ref[k].astype(out_ref.dtype)


def interleave(mine, other):
    count, segment, width = mine.shape
    out = pl.pallas_call(
        interleave_kernel,
        out_shape=jax.ShapeDtypeStruct((2 * count, segment, width), f32),
        name="interleave",
        compiler_params=params(12),
        cost_estimate=cost(2),
    )(mine, other[: count * segment].reshape(mine.shape))
    return out.reshape(2 * count * segment, width)


def on_device(
    hidden_in,
    codon_ids,
    start_flags,
    cotangent,
    codon_table,
    norm1_gain,
    norm1_bias,
    qkv_weight,
    qkv_bias,
    out_weight,
    out_bias,
    norm2_gain,
    norm2_bias,
    up_weight,
    up_bias,
    down_weight,
    down_bias,
):
    gene_count, piece, width = hidden_in.shape
    group = lax.axis_size("tensor")
    rank = lax.axis_index("tensor")
    local = qkv_weight.shape[2]
    heads = local // HEAD_DIM
    table_rows = codon_table.shape[0]

    spread_bias = jnp.broadcast_to(
        qkv_bias.reshape(3, heads, 1, HEAD_DIM), (3, heads, 2, HEAD_DIM)
    ).reshape(3, 2 * local)
    spread_bias = jnp.pad(spread_bias, ((0, 5), (0, width - 2 * local)))
    own = make_parcels(hidden_in, codon_ids, start_flags, spread_bias, up_bias[None])
    turned = qkv_weight.transpose(1, 2, 0).reshape(3, heads, HEAD_DIM, width)
    mixed = jnp.concatenate(
        [turned.transpose(1, 0, 2, 3), out_weight.reshape(heads, 1, HEAD_DIM, width)], 1
    )
    blocks = (mixed.reshape(4 * local, width), up_weight, down_weight)
    bit = lax.axis_index("dp") & 1
    half = width // 2

    def half_of(block):
        return lax.dynamic_slice_in_dim(block, bit * half, half, 0)

    def join(one, two):
        return jnp.where(
            bit == 0, jnp.concatenate([one, two], -2), jnp.concatenate([two, one], -2)
        )

    def as_mix(block):
        return block.reshape(heads, 4, HEAD_DIM, width)

    def flat(item):
        return item.reshape(-1, width)

    own_cot = [pick(cotangent, rank ^ r) for r in range(group)]
    cot_stack = jnp.stack(own_cot[2:])
    up_half = half_of(blocks[1])

    frequencies = 10000.0 ** (-jnp.arange(HEAD_DIM // 2, dtype=f32) * 2.0 / HEAD_DIM)
    positions = jnp.concatenate(
        [((rank ^ r) * piece + jnp.arange(piece)).astype(f32) for r in range(group)]
    )
    angles = positions[:, None] * frequencies[None, :]
    cosines, sines = jnp.cos(angles), jnp.sin(angles)
    tables = (jnp.concatenate([cosines] * 4, 1), jnp.concatenate([-sines, sines] * 2, 1))
    tables_back = (cosines.T, sines.T)

    def local_work():
        return tables, tables_back, half_of(blocks[0]), up_half, own_cot, cot_stack

    got, (tables, tables_back, mix_half, up_half, own_cot, cot_stack) = stage(
        [(own[r], "tensor", r) for r in (2, 3, 1)], local_work
    )
    parcels = [own[0], got[2], got[0], got[1]]
    (mix_mate,) = together((swap(blocks[0], "tensor", 1),))
    mixes = [as_mix(blocks[0]), as_mix(mix_mate)]
    early, late, every = (0, 1), (1, heads - 1), (0, heads)

    def first_heads(parcels):
        base, norm1 = embed(parcels, codon_table, norm1_gain[None], norm1_bias[None])
        return base, norm1, attend(norm1, *mixes[:2], *parcels[:2], tables, early)

    got, (base, norm1, (*kept0, attn0)) = stage(
        [(mix_half, "tensor", 2), (blocks[1], "tensor", 1), (blocks[2], "tensor", 1)],
        first_heads,
        parcels,
    )
    mix_half, *mates = got
    (mix_other, cot_across), (*kept1, attn1) = stage(
        [(mix_half, "dp", 1), (cot_stack, "tensor", 2)],
        lambda norm: attend(norm, *mixes[:2], *parcels[:2], tables, late),
        norm1,
    )
    across_mix = join(mix_half, mix_other)
    (across_mate, got), _ = stage(
        [(across_mix, "tensor", 1), mate_transfer(own_cot, cot_across)], lambda: ()
    )
    mixes += [as_mix(across_mix), as_mix(across_mate)]
    cot = jnp.concatenate(four(own_cot, cot_across, got), 0)
    part = width // 4
    (up_half, down_part), (*kept2, attn2) = stage(
        [(up_half, "tensor", 2), (down_weight[:part], "tensor", 2)],
        lambda norm: attend(norm, *mixes[2:], *parcels[2:], tables, every),
        norm1,
    )
    vectors = jnp.stack([out_bias, norm2_gain, norm2_bias, down_bias])

    def feed_near(base, cot):
        results = feed_first(
            (attn0, attn1, attn2), base, cot, vectors,
            (up_weight, mates[0]), (down_weight, mates[1]), parcels[:2],
        )
        return results, feed_grads(results[3], results[1], cot, results[5])

    (up_other, down_rest), (results, sent) = stage(
        [(up_half, "dp", 1), (down_weight[part:], "tensor", 2)], feed_near, base, cot
    )
    mid, norm2, act0, act1, gate0, gate1, ffn, back, sums_first = results

    def feed_join(one, two, down_one, down_two):
        across = jnp.stack([join(one, two), jnp.concatenate([down_one, down_two], 0)])
        return feed_grads(act0, norm2, cot, gate0), across

    got, (near, feed_across) = stage(
        [(item, "tensor", 1) for item in sent],
        feed_join, up_half, up_other, down_part, down_rest,
    )
    (feed_mate,), (keep_near, send_near) = stage(
        [(feed_across, "tensor", 1)],
        lambda near, got: halve_two(add_low(near[0], got[0]), add_low(near[1], got[1])),
        near,
        got,
    )

    def feed_far(ffn):
        results = feed_second(
            norm2, mid, cot, vectors, ffn, back, feed_across, feed_mate, parcels[2:]
        )
        sent = feed_grads(results[1], norm2, cot, results[3])
        return results, sent, feed_grads(results[0], norm2, cot, results[2])

    (got_near,), (results, sent, far) = stage([(send_near, "dp", 1)], feed_far, ffn)
    act2, act3, gate2, gate3, mid_grad, grad_low, sums_second, *out_pieces = results
    got, near = stage(
        [(item, "tensor", 1) for item in sent], lambda *pair: add_low(*pair), keep_near, got_near
    )
    keep_far, send_far = halve_two(add_low(far[0], got[0]), add_low(far[1], got[1]))

    def back_part(saved, block, span):
        return lambda grad: attend_back(
            saved, grad, norm1, mixes[block], mixes[block + 1], tables_back, span
        )

    near_steps = Scatter(near, 1)
    (got_far, out_across, *near_got), (mix2, mix3, back_a, bias_far) = stage(
        [(send_far, "dp", 1), (jnp.stack(out_pieces[2:]), "tensor", 2)] + near_steps.transfers(),
        back_part(kept2, 2, every),
        grad_low,
    )
    near_piece = near_steps.finish(near_got)
    far_steps = Scatter(add_low(keep_far, got_far), 1)
    (got, out_got), _ = stage(
        [(mix3, "tensor", 1), mate_transfer(out_pieces, out_across)], lambda: ()
    )
    far_mix = add_low(mix2, got)
    (cross_b, *far_got), (mix0a, mix1a, back_c, bias_c) = stage(
        [(far_mix[1:], "tensor", 2)] + far_steps.transfers(), back_part(kept1, 0, late), grad_low
    )
    far_piece = far_steps.finish(far_got)
    (feed_cross, cross_a, got), (mix0b, mix1b, back_d, bias_d) = stage(
        [(far_piece, "tensor", 2), (far_mix[:1], "tensor", 2), (mix1a, "tensor", 1)],
        back_part(kept0, 0, early),
        grad_low,
    )
    mix_a = add_low(mix0a, got, cross_b)
    feed_piece = add_low(near_piece, feed_cross)
    (got,), _ = stage([(mix1b, "tensor", 1)], lambda: feed_piece)
    mix_b = add_low(mix0b, got, cross_a)
    keep_mix, send_mix = halve(flat(jnp.concatenate([mix_b, mix_a], 0)))
    (mix_got, *feed_got), (table_part, sums_last, *grad_pieces) = stage(
        [(send_mix, "dp", 1)] + upper_transfers(feed_piece),
        lambda mid_grad: finish(
            (back_a, back_c, back_d), base, mid_grad, norm1_gain[None], parcels, table_rows
        ),
        mid_grad,
    )
    bias_near = jnp.concatenate([bias_d, bias_c], 0)

    def by_owner(blocks):
        swapped = jnp.where(rank & 1 == 1, blocks[jnp.array([1, 0, 3, 2])], blocks)
        return jnp.where(rank & 2 == 2, swapped[jnp.array([2, 3, 0, 1])], swapped)

    up_rows = by_owner(jnp.concatenate([sums_first[:2], sums_second[:2]], 0))
    qkv_rows = jnp.stack([bias_near, bias_far])[:, :, 0].reshape(2, heads, 3, 2, HEAD_DIM)
    qkv_rows = qkv_rows.transpose(0, 3, 2, 1, 4).reshape(group, 3, local)
    qkv_rows = by_owner(qkv_rows).transpose(1, 0, 2).reshape(3, width)
    vectors = jnp.concatenate([sums_last[:2], sums_second[2:6], up_rows, qkv_rows], 0)
    vectors = jnp.pad(vectors, ((0, 32 - vectors.shape[0]), (0, 0)))
    small = jnp.concatenate([table_part.astype(bf16), vectors.astype(bf16)], 0)
    core = rank & 1
    count = small.shape[0] // 2
    small_keep = lax.dynamic_slice_in_dim(small, core * count, count, 0)
    small_send = lax.dynamic_slice_in_dim(small, (1 - core) * count, count, 0)
    (got,), ((down_part, up_part), mix_keep) = stage(
        [(small_send, "tensor", 1)],
        lambda pieces: (place(pieces, bf16, "dp", 1, 2), add_low(keep_mix, mix_got)),
        [feed_piece] + feed_got,
    )
    small = add_low(small_keep, got)
    mix_steps = Scatter(mix_keep)
    to_other = jnp.concatenate([grad_pieces[2], small], 0)
    (crossed, down_other, *mix_got), _ = stage(
        [(to_other, "tensor", 2), (flat(down_part), "dp", 1)] + mix_steps.transfers(), lambda: ()
    )
    small = add_low(small, crossed[piece:])
    mix_piece = mix_steps.finish(mix_got)
    (last, up_other, *mix_got), down_grad = stage(
        [(grad_pieces[3], "tensor", 2), (jnp.concatenate([flat(up_part), small], 0), "dp", 1)]
        + upper_transfers(mix_piece),
        interleave,
        down_part,
        down_other,
    )
    size = flat(up_part).shape[0]
    small = add_low(small, up_other[size:])
    mix_part = place([mix_piece] + mix_got, bf16, "dp", 1)
    grad_across = [crossed[:piece], last]
    (other, grad_got, *got), (up_grad, hidden_out) = stage(
        [(flat(mix_part), "dp", 1), mate_transfer(grad_pieces, grad_across)]
        + upper_transfers(small),
        lambda part, rows, pieces: (interleave(part, rows), place(pieces, bf16, "tensor", 0)),
        up_part,
        up_other,
        four(out_pieces, out_across, out_got),
    )
    small = add_low(small, *got)
    (other_half,), (mix_grad, hidden_grad) = stage(
        [(small, "tensor", 1)],
        lambda part, rows, pieces: (interleave(part, rows), place(pieces, f32, "tensor", 0)),
        mix_part,
        other,
        four(grad_pieces, grad_across, grad_got),
    )
    small = jnp.where(
        core == 0,
        jnp.concatenate([small, other_half], 0),
        jnp.concatenate([other_half, small], 0),
    ).astype(f32)
    mix_grad = mix_grad.reshape(heads, 4, HEAD_DIM, width)
    qkv_grad = mix_grad[:, :3].transpose(3, 1, 0, 2).reshape(width, 3, local)
    out_grad = mix_grad[:, 3].reshape(local, width)
    at = table_rows
    rows = [small[at + k] for k in range(6)]
    up_bias_grad = lax.dynamic_index_in_dim(small[at + 6 : at + 6 + group], rank, 0, keepdims=False)
    qkv_bias_grad = lax.dynamic_slice_in_dim(
        small[at + 6 + group : at + 9 + group], rank * local, local, 1
    )
    return (
        hidden_out,
        hidden_grad,
        small[:table_rows],
        rows[0],
        rows[1],
        qkv_grad,
        qkv_bias_grad,
        out_grad,
        rows[4],
        rows[2],
        rows[3],
        up_grad,
        up_bias_grad,
        down_grad,
        rows[5],
    )


def solution(mesh):
    rows_placed = P("dp", "tensor", None)
    return jax.shard_map(
        on_device,
        mesh=mesh,
        in_specs=(
            rows_placed,
            P("dp", "tensor"),
            P("dp", "tensor"),
            rows_placed,
            P(),
            P(),
            P(),
            P(None, None, "tensor"),
            P(None, "tensor"),
            P("tensor", None),
            P(),
            P(),
            P(),
            P(None, "tensor"),
            P("tensor"),
            P("tensor", None),
            P(),
        ),
        out_specs=(
            rows_placed,
            rows_placed,
            P(),
            P(),
            P(),
            P(None, None, "tensor"),
            P(None, "tensor"),
            P("tensor", None),
            P(),
            P(),
            P(),
            P(None, "tensor"),
            P("tensor"),
            P("tensor", None),
            P(),
        ),
        check_vma=False,
    )
```

```python
import functools

import jax
import jax.numpy as jnp
from jax import lax
from jax.experimental import pallas as pl
from jax.experimental.pallas import tpu as pltpu
from jax.sharding import PartitionSpec as P

HEAD_DIM = 64
PAIR = 2 * HEAD_DIM
EPSILON = 1e-05
HIGHEST = lax.Precision.HIGHEST
NT = (((1,), (1,)), ((), ()))
TN = (((0,), (0,)), ((), ()))
LOG2E = 1.4426950408889634
TILE = 16
UP_ROW = 10
TABLE_HALF = 64
BIAS_HEADS = 3
SOFT_ROWS = 128
FEED_STEP = 256
bf16 = jnp.bfloat16
f32 = jnp.float32


def params(mebibytes):
    return pltpu.CompilerParams(vmem_limit_bytes=mebibytes * 1024 * 1024)


def cost(microseconds):
    return pl.CostEstimate(
        flops=microseconds * 10**9, bytes_accessed=microseconds * 10**6, transcendentals=0
    )


def dot(left, right):
    return jnp.dot(left, right, preferred_element_type=f32)


def dot_nt(left, right):
    return lax.dot_general(left, right, NT, preferred_element_type=f32)


def dot_tn(left, right):
    return lax.dot_general(left, right, TN, preferred_element_type=f32)


def whole(shape):
    return pl.BlockSpec(shape, lambda i: (0,) * len(shape))


def by_rows(rows, cols):
    return pl.BlockSpec((rows, cols), lambda i: (i, 0))


def by_cols(rows, cols):
    return pl.BlockSpec((rows, cols), lambda i: (0, i))


def swap(array_in, axis, distance):
    size = lax.axis_size(axis)
    return lax.ppermute(array_in, axis, [(i, i ^ distance) for i in range(size)])


def together(items):
    return lax.optimization_barrier(items)


def stage(sends, work, *inputs):
    arrays, inputs = together(([item[0] for item in sends], inputs))
    got = [swap(array, axis, distance) for array, (_, axis, distance) in zip(arrays, sends)]
    return together((got, work(*inputs)))


def add_low(*terms):
    return sum(term.astype(f32) for term in terms).astype(bf16)


def core_sum(mine, other):
    return add_low(mine, swap(other, "tensor", 1))


def halve(rows):
    size = lax.axis_size("dp")
    segment = rows.shape[0] // size
    halves = rows.reshape(size // 2, 2, segment, rows.shape[1])
    mine = lax.axis_index("dp") & 1
    keep = lax.dynamic_index_in_dim(halves, mine, 1, keepdims=False)
    send = lax.dynamic_index_in_dim(halves, 1 - mine, 1, keepdims=False)
    return keep, send


def halve_heads(blocks):
    heads, width = blocks.shape[0], blocks.shape[-1]
    size = lax.axis_size("dp")
    mine = lax.axis_index("dp") & 1
    halves = blocks.reshape(heads, size // 2, 2, -1, width)
    return [
        lax.dynamic_index_in_dim(halves, which, 2, keepdims=False)
        .transpose(1, 0, 2, 3)
        .reshape(size // 2, -1, width)
        for which in (mine, 1 - mine)
    ]


def halve_two(one, two):
    (keep_one, send_one), (keep_two, send_two) = halve(one), halve(two)
    return jnp.stack([keep_one, keep_two]), jnp.stack([send_one, send_two])


def pick(array_in, index):
    return lax.dynamic_index_in_dim(array_in, index, 0, keepdims=False)


class Scatter:
    def __init__(self, current, axis=0):
        self.row = lax.axis_index("dp") >> 1
        self.own, *self.sends = (
            lax.dynamic_index_in_dim(current, self.row ^ j, axis, keepdims=False)
            for j in range(current.shape[axis])
        )

    def transfers(self):
        return [(item, "dp", 2 * j + 2) for j, item in enumerate(self.sends)]

    def finish(self, got):
        return add_low(self.own, *got)


def upper_transfers(segment):
    return [(segment, "dp", 2 * j) for j in range(1, lax.axis_size("dp") // 2)]


def mate_transfer(pieces, crossed):
    return (jnp.stack([pieces[1], crossed[1]]), "tensor", 1)


def four(pieces, crossed, got):
    return [pieces[0], got[0], crossed[0], got[1]]


def normalise(row_data):
    row_mean = jnp.mean(row_data, axis=-1, keepdims=True)
    centred = row_data - row_mean
    row_var = jnp.mean(centred * centred, axis=-1, keepdims=True)
    inverse = lax.rsqrt(row_var + EPSILON)
    return centred * inverse, inverse


def norm_back(scaled, unit, inverse):
    return inverse * (
        scaled
        - jnp.mean(scaled, -1, keepdims=True)
        - unit * jnp.mean(scaled * unit, -1, keepdims=True)
    )


def column_sum(array_in):
    return jnp.sum(array_in, 0, keepdims=True)


def rows_of(*vectors):
    width = vectors[0].shape[1]
    at = lax.broadcasted_iota(jnp.int32, (8, width), 0)
    tile = jnp.zeros((8, width), f32)
    for k, vector in enumerate(vectors):
        tile = jnp.where(at == k, vector, tile)
    return tile


def first_head(rows):
    return lax.broadcasted_iota(jnp.int32, (rows, PAIR), 1) < HEAD_DIM


def turn(values_in, cosines, sines):
    lanes = lax.broadcasted_iota(jnp.int32, values_in.shape, 1)
    lower = (lanes & (HEAD_DIM - 1)) < HEAD_DIM // 2
    other = jnp.where(
        lower,
        pltpu.roll(values_in, PAIR - HEAD_DIM // 2, 1),
        pltpu.roll(values_in, HEAD_DIM // 2, 1),
    )
    return values_in * cosines + other * sines


def unturn(values_in, cosines, sines):
    quarter = HEAD_DIM // 2
    parts = [values_in[k * quarter : (k + 1) * quarter] for k in range(4)]
    out = []
    for low, high in (parts[:2], parts[2:]):
        out += [low * cosines + high * sines, high * cosines - low * sines]
    return jnp.concatenate(out, 0)


def split_three(values_in):
    high = values_in.astype(bf16)
    rest = values_in - high.astype(f32)
    middle = rest.astype(bf16)
    return high, middle, (rest - middle.astype(f32)).astype(bf16)


def parcel_kernel(hidden_ref, ids_ref, flags_ref, bias_ref, up_ref, *outs):
    rank = lax.axis_index("tensor")
    piece, width = hidden_ref.shape[1:]
    at = lax.broadcasted_iota(jnp.int32, (TILE, width), 0)
    tile = jnp.where(at == UP_ROW, up_ref[...].astype(f32), 0.0)
    rest = bias_ref[...]
    for part in range(3):
        high = rest.astype(bf16).astype(f32)
        rest = rest - high
        for k in range(3):
            tile = jnp.where(at == 1 + 3 * part + k, high[k : k + 1], tile)
    for distance, out_ref in enumerate(outs):
        gene = rank ^ distance
        out_ref[:piece] = hidden_ref[gene]
        index = (ids_ref[pl.ds(gene, 1)] + TABLE_HALF * flags_ref[pl.ds(gene, 1)]).astype(f32)
        index = jnp.concatenate([index, jnp.zeros((1, width - piece), f32)], 1)
        out_ref[piece:] = jnp.where(at == 0, index, tile).astype(bf16)


def make_parcels(hidden_in, codon_ids, start_flags, bias, up_bias):
    genes, piece, width = hidden_in.shape
    shape = jax.ShapeDtypeStruct((piece + TILE, width), bf16)
    return pl.pallas_call(
        parcel_kernel,
        out_shape=[shape] * genes,
        name="parcels",
        compiler_params=params(48),
        cost_estimate=cost(2),
    )(hidden_in, codon_ids, start_flags, bias, up_bias)


def onehot_of(tile, table_rows, piece):
    index = tile[0:1, :piece].astype(f32)
    at = lax.broadcasted_iota(jnp.int32, (table_rows, piece), 0).astype(f32)
    return (at == index).astype(bf16)


def embed_kernel(p0, p1, p2, p3, table_ref, gain_ref, shift_ref, base_ref, norm_ref, held):
    step = pl.program_id(0)
    piece = base_ref.shape[0]
    for k, parcel in enumerate((p0, p1, p2, p3)):

        @pl.when(step == k)
        def _():
            held[...] = parcel[...]

    onehot = onehot_of(held[piece:], table_ref.shape[0], piece)
    base = held[:piece].astype(f32)
    for part in split_three(table_ref[...]):
        base = base + dot_tn(onehot, part)
    unit, _ = normalise(base)
    base_ref[...] = base
    norm_ref[...] = (unit * gain_ref[...] + shift_ref[...]).astype(bf16)


def embed(parcels, table, gain, shift):
    rows, width = parcels[0].shape
    piece = rows - TILE
    return pl.pallas_call(
        embed_kernel,
        grid=(len(parcels),),
        in_specs=[whole(parcels[0].shape)] * 4
        + [whole(table.shape), whole(gain.shape), whole(shift.shape)],
        out_specs=[by_rows(piece, width)] * 2,
        out_shape=[
            jax.ShapeDtypeStruct((4 * piece, width), f32),
            jax.ShapeDtypeStruct((4 * piece, width), bf16),
        ],
        scratch_shapes=[pltpu.VMEM((rows, width), bf16)],
        name="embed",
        compiler_params=params(48),
        cost_estimate=cost(4),
    )(*parcels, table, gain, shift)


def pair_rows(a_ref, b_ref, parts):
    return jnp.concatenate([ref[0, part] for part in parts for ref in (a_ref, b_ref)], 0)


def attend_kernel(
    base, norm_ref, a_ref, b_ref, ta_ref, tb_ref, cos_ref, sin_ref,
    q_ref, k_ref, v_ref, context_ref, inverse_ref, exps_ref, attn_ref, biases, scores_ref,
):
    step = pl.program_id(0)
    for head in range(BIAS_HEADS):

        @pl.when(step + base == head)
        def _():
            vectors = []
            lanes = slice(head * PAIR, (head + 1) * PAIR)
            for k in range(3):
                two = []
                for tile in (ta_ref, tb_ref):
                    high = tile[...].astype(f32)[:, lanes]
                    two.append(high[1 + k : 2 + k] + high[4 + k : 5 + k] + high[7 + k : 8 + k])
                vectors.append(jnp.where(first_head(1), two[0], two[1]))
            biases[...] = rows_of(*vectors)

    rows = norm_ref.shape[0]
    product = dot_nt(norm_ref[...], pair_rows(a_ref, b_ref, (0, 1, 2)))
    bias = biases[...]
    cosines, sines = cos_ref[...], sin_ref[...]
    query = turn(product[:, :PAIR] + bias[0:1], cosines, sines).astype(bf16)
    query = query * jnp.asarray(HEAD_DIM**-0.5, bf16)
    keys = turn(product[:, PAIR : 2 * PAIR] + bias[1:2], cosines, sines).astype(bf16)
    values = (product[:, 2 * PAIR :] + bias[2:3]).astype(bf16)
    q_ref[...] = query
    k_ref[...] = keys
    v_ref[...] = values
    values = jnp.concatenate([values, jnp.ones((rows, PAIR), bf16)], 1)
    first = first_head(rows)
    for head in range(2):
        only = jnp.where(first == (head == 0), query, jnp.zeros_like(query))
        scores_ref[head] = dot_nt(only, keys)
    outs = []
    for head in range(2):
        for start in range(0, rows, SOFT_ROWS):
            span = slice(start, start + SOFT_ROWS)
            scores = scores_ref[head, span]
            top = jnp.max(scores, 1, keepdims=True) * LOG2E
            exps_ref[head, span] = jnp.exp2(scores * LOG2E - top).astype(bf16)
        outs.append(dot(exps_ref[head], values))
    inverse = 1.0 / jnp.where(first, outs[0][:, PAIR:], outs[1][:, PAIR:])
    context = (jnp.where(first, outs[0][:, :PAIR], outs[1][:, :PAIR]) * inverse).astype(bf16)
    inverse_ref[...] = inverse
    context_ref[...] = context
    more = dot(context, pair_rows(a_ref, b_ref, (3,)))

    @pl.when(step == 0)
    def _():
        attn_ref[...] = more

    @pl.when(step != 0)
    def _():
        attn_ref[...] += more


def attend(norm, a, b, tile_a, tile_b, tables, heads):
    rows, width = norm.shape
    base, pairs = heads
    low = jax.ShapeDtypeStruct((rows, pairs * PAIR), bf16)
    return pl.pallas_call(
        functools.partial(attend_kernel, base),
        grid=(pairs,),
        in_specs=[whole(norm.shape)]
        + [pl.BlockSpec((1,) + a.shape[1:], lambda i: (i + base, 0, 0, 0))] * 2
        + [tile_spec_of(tile_a)] * 2
        + [whole((rows, PAIR))] * 2,
        out_specs=[by_cols(rows, PAIR)] * 5
        + [pl.BlockSpec((2, rows, rows), lambda i: (i, 0, 0)), whole((rows, width))],
        out_shape=[low] * 4
        + [
            jax.ShapeDtypeStruct((rows, pairs * PAIR), f32),
            jax.ShapeDtypeStruct((2 * pairs, rows, rows), bf16),
            jax.ShapeDtypeStruct((rows, width), f32),
        ],
        scratch_shapes=[pltpu.VMEM((8, PAIR), f32), pltpu.VMEM((2, rows, rows), f32)],
        name="attend",
        compiler_params=params(44),
        cost_estimate=cost(8 * pairs),
    )(norm, a, b, tile_a, tile_b, *tables)


def attend_back_kernel(
    q_ref, k_ref, v_ref, context_ref, inverse_ref, exps_ref, grad_ref, norm_ref,
    a_ref, b_ref, cos_ref, sin_ref, out_a, out_b, back_ref, bias_ref, probs_ref, scores_ref,
):
    step = pl.program_id(0)
    rows = q_ref.shape[0]
    values = v_ref[...]
    first = first_head(rows)
    grad = dot_nt(grad_ref[...], pair_rows(a_ref, b_ref, (3,))) * inverse_ref[...]
    terms = grad * context_ref[...].astype(f32)
    inners = [
        jnp.sum(jnp.where(first == (head == 0), terms, 0.0), 1, keepdims=True) for head in range(2)
    ]
    grad = grad.astype(bf16)
    for head in range(2):
        only = jnp.where(first == (head == 0), grad, jnp.zeros_like(grad))
        probs_ref[head] = dot_nt(only, values)
    grad_turned, query_turned, keys_turned = grad.T, q_ref[...].T, k_ref[...].T
    turned = [[], [], []]
    for head in range(2):
        part = slice(head * HEAD_DIM, (head + 1) * HEAD_DIM)
        turned[2].append(dot(grad_turned[part], exps_ref[head]))
        for start in range(0, rows, SOFT_ROWS):
            span = slice(start, start + SOFT_ROWS)
            low = exps_ref[head, span].astype(f32) * (probs_ref[head, span] - inners[head][span])
            scores_ref[head, span] = low.astype(bf16)
        turned[0].append(dot_nt(keys_turned[part], scores_ref[head]))
        turned[1].append(dot(query_turned[part], scores_ref[head]))
    dq, dk, dv = (jnp.concatenate(item, 0) for item in turned)
    dq = unturn(dq * HEAD_DIM**-0.5, cos_ref[...], sin_ref[...])
    dk = unturn(dk, cos_ref[...], sin_ref[...])
    left = jnp.concatenate([dq, dk, dv], 0).astype(bf16)
    more = dot_tn(left, pair_rows(a_ref, b_ref, (0, 1, 2)))

    @pl.when(step == 0)
    def _():
        back_ref[...] = more

    @pl.when(step != 0)
    def _():
        back_ref[...] += more

    bias_ref[0] = dot_nt(jnp.ones((8, rows), bf16), left)
    inputs = dot(left, norm_ref[...]).astype(bf16)
    outputs = dot_tn(context_ref[...], grad_ref[...]).astype(bf16)
    for k in range(4):
        result = outputs if k == 3 else inputs[k * PAIR : (k + 1) * PAIR]
        out_a[0, k] = result[:HEAD_DIM]
        out_b[0, k] = result[HEAD_DIM:]


def attend_back(kept, grad, norm, a, b, tables, heads):
    query, keys, values, context, inverse, exps = kept
    rows, width = norm.shape
    base, count = heads
    shape = (count,) + a.shape[1:]
    columns = by_cols(rows, PAIR)
    weights = pl.BlockSpec((1,) + a.shape[1:], lambda i: (i + base, 0, 0, 0))
    return pl.pallas_call(
        attend_back_kernel,
        grid=(count,),
        in_specs=[columns] * 5
        + [pl.BlockSpec((2, rows, rows), lambda i: (i, 0, 0))]
        + [whole(norm.shape)] * 2
        + [weights] * 2
        + [whole(tables[0].shape)] * 2,
        out_specs=[pl.BlockSpec((1,) + a.shape[1:], lambda i: (i, 0, 0, 0))] * 2
        + [whole((rows, width)), pl.BlockSpec((1, 8, 3 * PAIR), lambda i: (i, 0, 0))],
        out_shape=[jax.ShapeDtypeStruct(shape, bf16)] * 2
        + [
            jax.ShapeDtypeStruct((rows, width), f32),
            jax.ShapeDtypeStruct((count, 8, 3 * PAIR), f32),
        ],
        scratch_shapes=[pltpu.VMEM((2, rows, rows), f32), pltpu.VMEM((2, rows, rows), bf16)],
        name="attend_back",
        compiler_params=params(50),
        cost_estimate=cost(9 * count),
    )(query, keys, values, context, inverse, exps, grad, norm, a, b, *tables)


def gelu_parts(gate):
    bell = jnp.exp2(gate * gate * (-0.5 * LOG2E))
    span = 1.0 + jnp.abs(gate) * (0.3275911 * 0.5**0.5)
    guess = pl.reciprocal(span, approx=True)
    near = guess * (2.0 - span * guess)
    tail = 1.061405429 * 0.5
    for factor in (-1.453152027, 1.421413741, -0.284496736, 0.254829592):
        tail = tail * near + factor * 0.5
    tail = tail * near * bell
    return jnp.where(gate >= 0, 1.0 - tail, tail), bell * 0.3989422804014327


def feed_block(norm, cot, up_ref, down_ref, tile, act_ref, gate_ref):
    chunk = 256
    units = up_ref.shape[1]
    spans = [slice(start, start + chunk) for start in range(0, units, chunk)]

    def first_products(span):
        bias = tile[UP_ROW : UP_ROW + 1, span].astype(f32)
        return dot(norm, up_ref[:, span]) + bias, dot_nt(cot, down_ref[span])

    sums = []
    ahead = first_products(spans[0])
    for at, span in enumerate(spans):
        gate, grad = ahead
        if at + 1 < len(spans):
            ahead = first_products(spans[at + 1])
        share, density = gelu_parts(gate)
        low = (grad * (share + gate * density)).astype(bf16)
        act_ref[:, span] = (gate * share).astype(bf16)
        gate_ref[:, span] = low
        sums.append(column_sum(low.astype(f32)))
    ffn = dot(act_ref[...], down_ref[...])
    back = dot_nt(gate_ref[...], up_ref[...])
    return ffn, back, jnp.concatenate(sums, 1)


def add_sums(ref, tile):
    @pl.when(pl.program_id(0) == 0)
    def _():
        ref[...] = tile

    @pl.when(pl.program_id(0) != 0)
    def _():
        ref[...] += tile


def feed_first_kernel(
    attn_a, attn_b, attn_c, base_ref, cot_ref, vec_ref, ua, ub, da, db, ta, tb,
    mid_ref, norm_ref, act_a, act_b, gate_a, gate_b, ffn_ref, back_ref, sums_ref,
):
    out_bias, gain, shift = (vec_ref[k : k + 1] for k in range(3))
    attn = attn_a[...] + attn_b[...] + attn_c[...]
    mid = base_ref[...] + (attn + out_bias)
    unit, _ = normalise(mid)
    norm = (unit * gain + shift).astype(bf16)
    mid_ref[...] = mid
    norm_ref[...] = norm
    cot = cot_ref[...]
    ffn, back, sum_a = feed_block(norm, cot, ua, da, ta[...], act_a, gate_a)
    more, back_more, sum_b = feed_block(norm, cot, ub, db, tb[...], act_b, gate_b)
    ffn_ref[...] = ffn + more
    back_ref[...] = back + back_more
    add_sums(sums_ref, rows_of(sum_a, sum_b))


def feed_second_kernel(
    norm_ref, mid_ref, cot_ref, vec_ref, ffn_ref, back_ref, one, two, ta, tb,
    act_a, act_b, gate_a, gate_b, mid_grad_ref, low_ref, sums_ref, *pieces,
):
    down_bias, gain = vec_ref[3:4], vec_ref[1:2]
    norm, cot = norm_ref[...], cot_ref[...]
    ffn, back, sum_a = feed_block(norm, cot, one.at[0], one.at[1], ta[...], act_a, gate_a)
    more, back_more, sum_b = feed_block(norm, cot, two.at[0], two.at[1], tb[...], act_b, gate_b)
    mid = mid_ref[...]
    out = (mid + (ffn_ref[...] + (ffn + more) + down_bias)).astype(bf16)
    rows = pieces[0].shape[0]
    back = back_ref[...] + (back + back_more)
    unit, inverse = normalise(mid)
    high = cot.astype(f32)
    grad = high + norm_back(back * gain, unit, inverse)
    low = grad.astype(bf16)
    mid_grad_ref[...] = grad
    low_ref[...] = low
    per_step = mid.shape[0] // rows
    for k, piece in enumerate(pieces):

        @pl.when(pl.program_id(0) == k // per_step)
        def _():
            piece[...] = out[k % per_step * rows : (k % per_step + 1) * rows]

    add_sums(
        sums_ref,
        rows_of(
            sum_a,
            sum_b,
            column_sum(back * unit),
            column_sum(back),
            column_sum(low.astype(f32)),
            column_sum(high),
        ),
    )


def tile_spec_of(parcel):
    at = parcel.shape[0] // TILE - 1
    return pl.BlockSpec((TILE, parcel.shape[1]), lambda i: (at, 0))


def feed_first(attns, base, cot, vectors, ups, downs, parcels):
    rows, width = base.shape
    units = ups[0].shape[1]
    piece = parcels[0].shape[0] - TILE
    step = FEED_STEP
    low = jax.ShapeDtypeStruct((rows, units), bf16)
    high = jax.ShapeDtypeStruct((rows, width), f32)
    return pl.pallas_call(
        feed_first_kernel,
        grid=(rows // step,),
        in_specs=[by_rows(step, width)] * 5
        + [whole(vectors.shape)]
        + [whole(ups[0].shape)] * 2
        + [whole(downs[0].shape)] * 2
        + [tile_spec_of(parcels[0])] * 2,
        out_specs=[by_rows(step, width)] * 2
        + [by_rows(step, units)] * 4
        + [by_rows(step, width)] * 2
        + [whole((8, width))],
        out_shape=[high, jax.ShapeDtypeStruct((rows, width), bf16)]
        + [low] * 4
        + [high, high, jax.ShapeDtypeStruct((8, width), f32)],
        name="feed_first",
        compiler_params=params(24),
        cost_estimate=cost(18),
    )(*attns, base, cot, vectors, *ups, *downs, *parcels)


def feed_second(norm, mid, cot, vectors, ffn, back, one, two, parcels):
    rows, width = mid.shape
    units = one.shape[2]
    piece = parcels[0].shape[0] - TILE
    step = FEED_STEP
    low = jax.ShapeDtypeStruct((rows, units), bf16)
    return pl.pallas_call(
        feed_second_kernel,
        grid=(rows // step,),
        in_specs=[by_rows(step, width)] * 3
        + [whole(vectors.shape)]
        + [by_rows(step, width)] * 2
        + [whole(one.shape)] * 2
        + [tile_spec_of(parcels[0])] * 2,
        out_specs=[by_rows(step, units)] * 4
        + [by_rows(step, width)] * 2
        + [whole((8, width))]
        + [whole((piece, width))] * (rows // piece),
        out_shape=[low] * 4
        + [
            jax.ShapeDtypeStruct((rows, width), f32),
            jax.ShapeDtypeStruct((rows, width), bf16),
            jax.ShapeDtypeStruct((8, width), f32),
        ]
        + [jax.ShapeDtypeStruct((piece, width), bf16)] * (rows // piece),
        name="feed_second",
        compiler_params=params(24),
        cost_estimate=cost(20),
    )(norm, mid, cot, vectors, ffn, back, one, two, *parcels)


def feed_grad_kernel(act_ref, norm_ref, cot_ref, gate_ref, down_ref, up_ref):
    down_ref[...] = dot_tn(act_ref[...], cot_ref[...]).astype(bf16)
    up_ref[...] = dot_tn(norm_ref[...], gate_ref[...]).astype(bf16)


def feed_grads(act, norm, cot, gate):
    units, width = act.shape[1], norm.shape[1]
    return pl.pallas_call(
        feed_grad_kernel,
        out_shape=[
            jax.ShapeDtypeStruct((units, width), bf16),
            jax.ShapeDtypeStruct((width, units), bf16),
        ],
        name="feed_grads",
        compiler_params=params(16),
        cost_estimate=cost(3),
    )(act, norm, cot, gate)


def finish_kernel(count, *refs):
    backs, refs = refs[:count], refs[count:]
    base_ref, mid_grad_ref, gain_ref, t0, t1, t2, t3, table_ref, sums_ref, *pieces = refs
    step = pl.program_id(0)
    piece = base_ref.shape[0]
    back = sum(ref[...] for ref in backs)
    unit, inverse = normalise(base_ref[...])
    grad = mid_grad_ref[...] + norm_back(back * gain_ref[...], unit, inverse)
    low = grad.astype(bf16)
    tile = t0[...]
    for k, other in enumerate((t1, t2, t3)):
        tile = jnp.where(step == k + 1, other[...], tile)
    onehot = onehot_of(tile, table_ref.shape[0], piece)
    total = 0.0
    for part in split_three(grad):
        total = total + dot(onehot, part)
    add_sums(table_ref, total)
    add_sums(sums_ref, rows_of(column_sum(back * unit), column_sum(back)))
    for k, out_ref in enumerate(pieces):

        @pl.when(step == k)
        def _():
            out_ref[...] = low


def finish(backs, base, mid_grad, gain, parcels, table_rows):
    rows, width = base.shape
    step = parcels[0].shape[0] - TILE
    return pl.pallas_call(
        functools.partial(finish_kernel, len(backs)),
        grid=(rows // step,),
        in_specs=[by_rows(step, width)] * (len(backs) + 2)
        + [whole(gain.shape)]
        + [tile_spec_of(parcels[0])] * 4,
        out_specs=[whole((table_rows, width)), whole((8, width))]
        + [whole((step, width))] * (rows // step),
        out_shape=[
            jax.ShapeDtypeStruct((table_rows, width), f32),
            jax.ShapeDtypeStruct((8, width), f32),
        ]
        + [jax.ShapeDtypeStruct((step, width), bf16)] * (rows // step),
        name="finish",
        compiler_params=params(60),
        cost_estimate=cost(5),
    )(*backs, base, mid_grad, gain, *parcels)


def place_kernel(axis, shift, count, *refs):
    pieces, outs = refs[:count], refs[count:]
    rank = lax.axis_index(axis) >> shift
    for distance, piece in enumerate(pieces):
        for which, out_ref in enumerate(outs):
            part = piece[which] if len(outs) > 1 else piece[...]
            out_ref[rank ^ distance] = part.astype(out_ref.dtype)


def place(pieces, dtype, axis, shift, arrays=1):
    count = len(pieces)
    shape = pieces[0].shape[1:] if arrays > 1 else pieces[0].shape
    outs = pl.pallas_call(
        functools.partial(place_kernel, axis, shift, count),
        out_shape=[jax.ShapeDtypeStruct((count,) + shape, dtype)] * arrays,
        name="place",
        compiler_params=params(12),
        cost_estimate=cost(2),
    )(*pieces)
    return outs if arrays > 1 else outs[0]


def interleave_kernel(mine_ref, other_ref, out_ref):
    bit = lax.axis_index("dp") & 1
    for k in range(mine_ref.shape[0]):
        out_ref[2 * k + bit] = mine_ref[k].astype(out_ref.dtype)
        out_ref[2 * k + 1 - bit] = other_ref[k].astype(out_ref.dtype)


def interleave(mine, other):
    count, segment, width = mine.shape
    out = pl.pallas_call(
        interleave_kernel,
        out_shape=jax.ShapeDtypeStruct((2 * count, segment, width), f32),
        name="interleave",
        compiler_params=params(12),
        cost_estimate=cost(2),
    )(mine, other[: count * segment].reshape(mine.shape))
    return out.reshape(2 * count * segment, width)


def on_device(
    hidden_in,
    codon_ids,
    start_flags,
    cotangent,
    codon_table,
    norm1_gain,
    norm1_bias,
    qkv_weight,
    qkv_bias,
    out_weight,
    out_bias,
    norm2_gain,
    norm2_bias,
    up_weight,
    up_bias,
    down_weight,
    down_bias,
):
    gene_count, piece, width = hidden_in.shape
    group = lax.axis_size("tensor")
    rank = lax.axis_index("tensor")
    local = qkv_weight.shape[2]
    heads = local // HEAD_DIM
    table_rows = codon_table.shape[0]

    spread_bias = jnp.broadcast_to(
        qkv_bias.reshape(3, heads, 1, HEAD_DIM), (3, heads, 2, HEAD_DIM)
    ).reshape(3, 2 * local)
    spread_bias = jnp.pad(spread_bias, ((0, 5), (0, width - 2 * local)))
    own = make_parcels(hidden_in, codon_ids, start_flags, spread_bias, up_bias[None])
    turned = qkv_weight.transpose(1, 2, 0).reshape(3, heads, HEAD_DIM, width)
    mixed = jnp.concatenate(
        [turned.transpose(1, 0, 2, 3), out_weight.reshape(heads, 1, HEAD_DIM, width)], 1
    )
    blocks = (mixed.reshape(4 * local, width), up_weight, down_weight)
    bit = lax.axis_index("dp") & 1
    half = width // 2

    def half_of(block):
        return lax.dynamic_slice_in_dim(block, bit * half, half, 0)

    def join(one, two):
        return jnp.where(
            bit == 0, jnp.concatenate([one, two], -2), jnp.concatenate([two, one], -2)
        )

    def as_mix(block):
        return block.reshape(heads, 4, HEAD_DIM, width)

    def flat(item):
        return item.reshape(-1, width)

    own_cot = [pick(cotangent, rank ^ r) for r in range(group)]
    cot_stack = jnp.stack(own_cot[2:])
    up_half = half_of(blocks[1])

    frequencies = 10000.0 ** (-jnp.arange(HEAD_DIM // 2, dtype=f32) * 2.0 / HEAD_DIM)
    positions = jnp.concatenate(
        [((rank ^ r) * piece + jnp.arange(piece)).astype(f32) for r in range(group)]
    )
    angles = positions[:, None] * frequencies[None, :]
    cosines, sines = jnp.cos(angles), jnp.sin(angles)
    tables = (jnp.concatenate([cosines] * 4, 1), jnp.concatenate([-sines, sines] * 2, 1))
    tables_back = (cosines.T, sines.T)

    def local_work():
        return tables, tables_back, half_of(blocks[0]), up_half, own_cot, cot_stack

    got, (tables, tables_back, mix_half, up_half, own_cot, cot_stack) = stage(
        [(own[r], "tensor", r) for r in (2, 3, 1)], local_work
    )
    parcels = [own[0], got[2], got[0], got[1]]
    (mix_mate,) = together((swap(blocks[0], "tensor", 1),))
    mixes = [as_mix(blocks[0]), as_mix(mix_mate)]
    early, late, every = (0, 1), (1, heads - 1), (0, heads)

    def first_heads(parcels):
        base, norm1 = embed(parcels, codon_table, norm1_gain[None], norm1_bias[None])
        return base, norm1, attend(norm1, *mixes[:2], *parcels[:2], tables, early)

    got, (base, norm1, (*kept0, attn0)) = stage(
        [(mix_half, "tensor", 2), (blocks[1], "tensor", 1), (blocks[2], "tensor", 1)],
        first_heads,
        parcels,
    )
    mix_half, *mates = got
    (mix_other, cot_across), (*kept1, attn1) = stage(
        [(mix_half, "dp", 1), (cot_stack, "tensor", 2)],
        lambda norm: attend(norm, *mixes[:2], *parcels[:2], tables, late),
        norm1,
    )
    across_mix = join(mix_half, mix_other)
    (across_mate, got), _ = stage(
        [(across_mix, "tensor", 1), mate_transfer(own_cot, cot_across)], lambda: ()
    )
    mixes += [as_mix(across_mix), as_mix(across_mate)]
    cot = jnp.concatenate(four(own_cot, cot_across, got), 0)
    part = width // 4
    (up_half, down_part), (*kept2, attn2) = stage(
        [(up_half, "tensor", 2), (down_weight[:part], "tensor", 2)],
        lambda norm: attend(norm, *mixes[2:], *parcels[2:], tables, every),
        norm1,
    )
    vectors = jnp.stack([out_bias, norm2_gain, norm2_bias, down_bias])

    def feed_near(base, cot):
        results = feed_first(
            (attn0, attn1, attn2), base, cot, vectors,
            (up_weight, mates[0]), (down_weight, mates[1]), parcels[:2],
        )
        return results, feed_grads(results[3], results[1], cot, results[5])

    (up_other, down_rest), (results, sent) = stage(
        [(up_half, "dp", 1), (down_weight[part:], "tensor", 2)], feed_near, base, cot
    )
    mid, norm2, act0, act1, gate0, gate1, ffn, back, sums_first = results

    def feed_join(one, two, down_one, down_two):
        across = jnp.stack([join(one, two), jnp.concatenate([down_one, down_two], 0)])
        return feed_grads(act0, norm2, cot, gate0), across

    got, (near, feed_across) = stage(
        [(item, "tensor", 1) for item in sent],
        feed_join, up_half, up_other, down_part, down_rest,
    )
    (feed_mate,), (keep_near, send_near) = stage(
        [(feed_across, "tensor", 1)],
        lambda near, got: halve_two(add_low(near[0], got[0]), add_low(near[1], got[1])),
        near,
        got,
    )

    def feed_far(ffn):
        results = feed_second(
            norm2, mid, cot, vectors, ffn, back, feed_across, feed_mate, parcels[2:]
        )
        sent = feed_grads(results[1], norm2, cot, results[3])
        return results, sent, feed_grads(results[0], norm2, cot, results[2])

    (got_near,), (results, sent, far) = stage([(send_near, "dp", 1)], feed_far, ffn)
    act2, act3, gate2, gate3, mid_grad, grad_low, sums_second, *out_pieces = results
    got, near = stage(
        [(item, "tensor", 1) for item in sent], lambda *pair: add_low(*pair), keep_near, got_near
    )
    keep_far, send_far = halve_two(add_low(far[0], got[0]), add_low(far[1], got[1]))

    def back_part(saved, block, span):
        return lambda grad: attend_back(
            saved, grad, norm1, mixes[block], mixes[block + 1], tables_back, span
        )

    near_steps = Scatter(near, 1)
    (*near_got, got_far, out_across), (mix2, mix3, back_a, bias_far) = stage(
        near_steps.transfers() + [(send_far, "dp", 1), (jnp.stack(out_pieces[2:]), "tensor", 2)],
        back_part(kept2, 2, every),
        grad_low,
    )
    far_steps = Scatter(add_low(keep_far, got_far), 1)
    (got,), _ = stage([(mix3, "tensor", 1)], lambda sends: sends, far_steps.sends)
    far_mix = add_low(mix2, got)
    (*far_got, cross, out_got), (mix0a, mix1a, back_c, bias_c) = stage(
        far_steps.transfers()
        + [(far_mix, "tensor", 2), mate_transfer(out_pieces, out_across)],
        back_part(kept1, 0, late),
        grad_low,
    )
    near_piece = near_steps.finish(near_got)
    far_piece = far_steps.finish(far_got)
    (feed_cross, got), (mix0b, mix1b, back_d, bias_d) = stage(
        [(far_piece, "tensor", 2), (mix1a, "tensor", 1)], back_part(kept0, 0, early), grad_low
    )
    feed_piece = add_low(near_piece, feed_cross)
    mix_keep, mix_send = halve_heads(
        jnp.concatenate(
            [add_low(mix0b, cross[:1]), add_low(mix0a, got, cross[1:]), mix1b], 0
        )
    )
    (*feed_got, mix_got), (table_part, sums_last, *grad_pieces) = stage(
        upper_transfers(feed_piece) + [(mix_send, "dp", 1)],
        lambda mid_grad: finish(
            (back_a, back_c, back_d), base, mid_grad, norm1_gain[None], parcels, table_rows
        ),
        mid_grad,
    )
    bias_near = jnp.concatenate([bias_d, bias_c], 0)

    def by_owner(blocks):
        swapped = jnp.where(rank & 1 == 1, blocks[jnp.array([1, 0, 3, 2])], blocks)
        return jnp.where(rank & 2 == 2, swapped[jnp.array([2, 3, 0, 1])], swapped)

    up_rows = by_owner(jnp.concatenate([sums_first[:2], sums_second[:2]], 0))
    qkv_rows = jnp.stack([bias_near, bias_far])[:, :, 0].reshape(2, heads, 3, 2, HEAD_DIM)
    qkv_rows = qkv_rows.transpose(0, 3, 2, 1, 4).reshape(group, 3, local)
    qkv_rows = by_owner(qkv_rows).transpose(1, 0, 2).reshape(3, width)
    vectors = jnp.concatenate([sums_last[:2], sums_second[2:6], up_rows, qkv_rows], 0)
    vectors = jnp.pad(vectors, ((0, 32 - vectors.shape[0]), (0, 0)))
    small = jnp.concatenate([table_part.astype(bf16), vectors.astype(bf16)], 0)
    core = rank & 1
    count = small.shape[0] // 2
    small_keep = lax.dynamic_slice_in_dim(small, core * count, count, 0)
    small_send = lax.dynamic_slice_in_dim(small, (1 - core) * count, count, 0)
    segment = mix_keep.shape[1] // (heads + 1)
    mix_sum = add_low(mix_keep, mix_got)
    mate_share = mix_sum[:, -segment:]
    (got, mate_got), (down_part, up_part) = stage(
        [(small_send, "tensor", 1), (mate_share, "tensor", 1)],
        lambda pieces: place(pieces, bf16, "dp", 1, 2),
        [feed_piece] + feed_got,
    )
    small = add_low(small_keep, got)
    mix_own = add_low(mix_sum[:, :segment], mate_got)
    mix_steps = Scatter(jnp.concatenate([mix_own, mix_sum[:, segment:-segment]], 1))
    to_other = jnp.concatenate(grad_pieces[2:] + [small], 0)
    (*mix_got, crossed, down_other), _ = stage(
        mix_steps.transfers() + [(to_other, "tensor", 2), (flat(down_part), "dp", 1)], lambda: ()
    )
    small = add_low(small, crossed[2 * piece :])
    mix_piece = mix_steps.finish(mix_got)
    grad_across = [crossed[:piece], crossed[piece : 2 * piece]]
    (*mix_got, up_other, grad_got), down_grad = stage(
        upper_transfers(mix_piece)
        + [
            (jnp.concatenate([flat(up_part), small], 0), "dp", 1),
            mate_transfer(grad_pieces, grad_across),
        ],
        interleave,
        down_part,
        down_other,
    )
    size = flat(up_part).shape[0]
    small = add_low(small, up_other[size:])
    mix_part = place([mix_piece] + mix_got, bf16, "dp", 1)
    (*got, other), (up_grad, hidden_out, hidden_grad) = stage(
        upper_transfers(small) + [(flat(mix_part), "dp", 1)],
        lambda part, rows, out, grad: (
            interleave(part, rows),
            place(out, bf16, "tensor", 0),
            place(grad, f32, "tensor", 0),
        ),
        up_part,
        up_other,
        four(out_pieces, out_across, out_got),
        four(grad_pieces, grad_across, grad_got),
    )
    small = add_low(small, *got)
    (other_half,), mix_grad = stage(
        [(small, "tensor", 1)], interleave, mix_part, other
    )
    small = jnp.where(
        core == 0,
        jnp.concatenate([small, other_half], 0),
        jnp.concatenate([other_half, small], 0),
    ).astype(f32)
    owners = lax.axis_size("dp") // 4
    mix_grad = mix_grad.reshape(4, owners, heads, HEAD_DIM // owners, width)
    qkv_grad = mix_grad[:3].transpose(4, 0, 2, 1, 3).reshape(width, 3, local)
    out_grad = mix_grad[3].transpose(1, 0, 2, 3).reshape(local, width)
    at = table_rows
    rows = [small[at + k] for k in range(6)]
    up_bias_grad = lax.dynamic_index_in_dim(small[at + 6 : at + 6 + group], rank, 0, keepdims=False)
    qkv_bias_grad = lax.dynamic_slice_in_dim(
        small[at + 6 + group : at + 9 + group], rank * local, local, 1
    )
    return (
        hidden_out,
        hidden_grad,
        small[:table_rows],
        rows[0],
        rows[1],
        qkv_grad,
        qkv_bias_grad,
        out_grad,
        rows[4],
        rows[2],
        rows[3],
        up_grad,
        up_bias_grad,
        down_grad,
        rows[5],
    )


def solution(mesh):
    rows_placed = P("dp", "tensor", None)
    return jax.shard_map(
        on_device,
        mesh=mesh,
        in_specs=(
            rows_placed,
            P("dp", "tensor"),
            P("dp", "tensor"),
            rows_placed,
            P(),
            P(),
            P(),
            P(None, None, "tensor"),
            P(None, "tensor"),
            P("tensor", None),
            P(),
            P(),
            P(),
            P(None, "tensor"),
            P("tensor"),
            P("tensor", None),
            P(),
        ),
        out_specs=(
            rows_placed,
            rows_placed,
            P(),
            P(),
            P(),
            P(None, None, "tensor"),
            P(None, "tensor"),
            P("tensor", None),
            P(),
            P(),
            P(),
            P(None, "tensor"),
            P("tensor"),
            P("tensor", None),
            P(),
        ),
        check_vma=False,
    )
```

```python
import functools

import jax
import jax.numpy as jnp
from jax import lax
from jax.experimental import pallas as pl
from jax.experimental.pallas import tpu as pltpu
from jax.sharding import PartitionSpec as P

HEAD_DIM = 64
PAIR = 2 * HEAD_DIM
EPSILON = 1e-05
HIGHEST = lax.Precision.HIGHEST
NT = (((1,), (1,)), ((), ()))
TN = (((0,), (0,)), ((), ()))
LOG2E = 1.4426950408889634
TILE = 16
UP_ROW = 10
BIAS_HEADS = 3
SOFT_ROWS = 128
FEED_STEP = 256
bf16 = jnp.bfloat16
f32 = jnp.float32


def params(mebibytes):
    return pltpu.CompilerParams(vmem_limit_bytes=mebibytes * 1024 * 1024)


def cost(microseconds):
    return pl.CostEstimate(
        flops=microseconds * 10**9, bytes_accessed=microseconds * 10**6, transcendentals=0
    )


def dot(left, right):
    return jnp.dot(left, right, preferred_element_type=f32)


def dot_nt(left, right):
    return lax.dot_general(left, right, NT, preferred_element_type=f32)


def dot_tn(left, right):
    return lax.dot_general(left, right, TN, preferred_element_type=f32)


def whole(shape):
    return pl.BlockSpec(shape, lambda i: (0,) * len(shape))


def by_rows(rows, cols):
    return pl.BlockSpec((rows, cols), lambda i: (i, 0))


def by_cols(rows, cols):
    return pl.BlockSpec((rows, cols), lambda i: (0, i))


def swap(array_in, axis, distance):
    size = lax.axis_size(axis)
    return lax.ppermute(array_in, axis, [(i, i ^ distance) for i in range(size)])


def together(items):
    return lax.optimization_barrier(items)


def stage(sends, work, *inputs):
    arrays, inputs = together(([item[0] for item in sends], inputs))
    got = [swap(array, axis, distance) for array, (_, axis, distance) in zip(arrays, sends)]
    return together((got, work(*inputs)))


def add_low(*terms):
    return sum(term.astype(f32) for term in terms).astype(bf16)


def core_sum(mine, other):
    return add_low(mine, swap(other, "tensor", 1))


def halve(rows):
    size = lax.axis_size("dp")
    segment = rows.shape[0] // size
    halves = rows.reshape(size // 2, 2, segment, rows.shape[1])
    mine = lax.axis_index("dp") & 1
    keep = lax.dynamic_index_in_dim(halves, mine, 1, keepdims=False)
    send = lax.dynamic_index_in_dim(halves, 1 - mine, 1, keepdims=False)
    return keep, send


def halve_heads(blocks):
    heads, width = blocks.shape[0], blocks.shape[-1]
    size = lax.axis_size("dp")
    mine = lax.axis_index("dp") & 1
    halves = blocks.reshape(heads, size // 2, 2, -1, width)
    return [
        lax.dynamic_index_in_dim(halves, which, 2, keepdims=False)
        .transpose(1, 0, 2, 3)
        .reshape(size // 2, -1, width)
        for which in (mine, 1 - mine)
    ]


def add_halve_kernel(one, got_one, two, got_two, keep_ref, send_ref):
    mine = lax.axis_index("dp") & 1
    for which, (left, right) in enumerate(((one, got_one), (two, got_two))):
        for k in range(keep_ref.shape[1]):
            for index, out_ref in ((mine, keep_ref), (1 - mine, send_ref)):
                out_ref[which, k] = add_low(left[k, index], right[k, index])


def add_halve(one, got_one, two, got_two):
    size = lax.axis_size("dp")
    rows, width = one.shape
    shape = jax.ShapeDtypeStruct((2, size // 2, rows // size, width), bf16)
    return pl.pallas_call(
        add_halve_kernel,
        out_shape=[shape] * 2,
        name="add_halve",
        compiler_params=params(16),
        cost_estimate=cost(2),
    )(*(item.reshape((size // 2, 2) + shape.shape[2:]) for item in (one, got_one, two, got_two)))


def pick(array_in, index):
    return lax.dynamic_index_in_dim(array_in, index, 0, keepdims=False)


class Scatter:
    def __init__(self, current, axis=0):
        self.row = lax.axis_index("dp") >> 1
        self.own, *self.sends = (
            lax.dynamic_index_in_dim(current, self.row ^ j, axis, keepdims=False)
            for j in range(current.shape[axis])
        )

    def transfers(self):
        return [(item, "dp", 2 * j + 2) for j, item in enumerate(self.sends)]

    def finish(self, got):
        return add_low(self.own, *got)


def upper_transfers(segment):
    return [(segment, "dp", 2 * j) for j in range(1, lax.axis_size("dp") // 2)]


def mate_transfer(pieces, crossed):
    return (jnp.stack([pieces[1], crossed[1]]), "tensor", 1)


def four(pieces, crossed, got):
    return [pieces[0], got[0], crossed[0], got[1]]


def normalise(row_data):
    row_mean = jnp.mean(row_data, axis=-1, keepdims=True)
    centred = row_data - row_mean
    row_var = jnp.mean(centred * centred, axis=-1, keepdims=True)
    inverse = lax.rsqrt(row_var + EPSILON)
    return centred * inverse, inverse


def norm_back(scaled, unit, inverse):
    return inverse * (
        scaled
        - jnp.mean(scaled, -1, keepdims=True)
        - unit * jnp.mean(scaled * unit, -1, keepdims=True)
    )


def column_sum(array_in):
    return jnp.sum(array_in, 0, keepdims=True)


def rows_of(*vectors):
    width = vectors[0].shape[1]
    at = lax.broadcasted_iota(jnp.int32, (8, width), 0)
    tile = jnp.zeros((8, width), f32)
    for k, vector in enumerate(vectors):
        tile = jnp.where(at == k, vector, tile)
    return tile


def first_head(rows):
    return lax.broadcasted_iota(jnp.int32, (rows, PAIR), 1) < HEAD_DIM


def unturn(values_in, cosines, sines):
    quarter = HEAD_DIM // 2
    parts = [values_in[k * quarter : (k + 1) * quarter] for k in range(4)]
    out = []
    for low, high in (parts[:2], parts[2:]):
        out += [low * cosines + high * sines, high * cosines - low * sines]
    return jnp.concatenate(out, 0)


def split_three(values_in):
    high = values_in.astype(bf16)
    rest = values_in - high.astype(f32)
    middle = rest.astype(bf16)
    return high, middle, (rest - middle.astype(f32)).astype(bf16)


def parcel_kernel(half, hidden_ref, ids_ref, flags_ref, bias_ref, up_ref, *outs):
    rank = lax.axis_index("tensor")
    piece, width = hidden_ref.shape[1:]
    at = lax.broadcasted_iota(jnp.int32, (TILE, width), 0)
    tile = jnp.where(at == UP_ROW, up_ref[...].astype(f32), 0.0)
    rest = bias_ref[...]
    for part in range(3):
        high = rest.astype(bf16).astype(f32)
        rest = rest - high
        for k in range(3):
            tile = jnp.where(at == 1 + 3 * part + k, high[k : k + 1], tile)
    for distance, out_ref in enumerate(outs):
        gene = rank ^ distance
        out_ref[:piece] = hidden_ref[gene]
        index = (ids_ref[pl.ds(gene, 1)] + half * flags_ref[pl.ds(gene, 1)]).astype(f32)
        index = jnp.concatenate([index, jnp.zeros((1, width - piece), f32)], 1)
        out_ref[piece:] = jnp.where(at == 0, index, tile).astype(bf16)


def make_parcels(hidden_in, codon_ids, start_flags, bias, up_bias, half):
    genes, piece, width = hidden_in.shape
    shape = jax.ShapeDtypeStruct((piece + TILE, width), bf16)
    return pl.pallas_call(
        functools.partial(parcel_kernel, half),
        out_shape=[shape] * genes,
        name="parcels",
        compiler_params=params(48),
        cost_estimate=cost(2),
    )(hidden_in, codon_ids, start_flags, bias, up_bias)


def onehot_of(tile, table_rows, piece):
    index = tile[0:1, :piece].astype(f32)
    at = lax.broadcasted_iota(jnp.int32, (table_rows, piece), 0).astype(f32)
    return (at == index).astype(bf16)


def embed_kernel(p0, p1, p2, p3, table_ref, gain_ref, shift_ref, base_ref, norm_ref, held):
    step = pl.program_id(0)
    piece = base_ref.shape[0]
    for k, parcel in enumerate((p0, p1, p2, p3)):

        @pl.when(step == k)
        def _():
            held[...] = parcel[...]

    onehot = onehot_of(held[piece:], table_ref.shape[0], piece)
    base = held[:piece].astype(f32)
    for part in split_three(table_ref[...]):
        base = base + dot_tn(onehot, part)
    unit, _ = normalise(base)
    base_ref[...] = base
    norm_ref[...] = (unit * gain_ref[...] + shift_ref[...]).astype(bf16)


def embed(parcels, table, gain, shift):
    rows, width = parcels[0].shape
    piece = rows - TILE
    return pl.pallas_call(
        embed_kernel,
        grid=(len(parcels),),
        in_specs=[whole(parcels[0].shape)] * 4
        + [whole(table.shape), whole(gain.shape), whole(shift.shape)],
        out_specs=[by_rows(piece, width)] * 2,
        out_shape=[
            jax.ShapeDtypeStruct((4 * piece, width), f32),
            jax.ShapeDtypeStruct((4 * piece, width), bf16),
        ],
        scratch_shapes=[pltpu.VMEM((rows, width), bf16)],
        name="embed",
        compiler_params=params(48),
        cost_estimate=cost(4),
    )(*parcels, table, gain, shift)


def pair_rows(a_ref, b_ref, parts):
    return jnp.concatenate([ref[0, part] for part in parts for ref in (a_ref, b_ref)], 0)


def attend_kernel(
    base, norm_ref, a_ref, b_ref, ta_ref, tb_ref, cos_ref, sin_ref,
    kept_ref, inverse_ref, exps_ref, attn_ref, biases, scores_ref,
):
    step = pl.program_id(0)
    for head in range(BIAS_HEADS):

        @pl.when(step + base == head)
        def _():
            vectors = []
            lanes = slice(head * PAIR, (head + 1) * PAIR)
            for k in range(3):
                two = []
                for tile in (ta_ref, tb_ref):
                    high = tile[...].astype(f32)[:, lanes]
                    two.append(high[1 + k : 2 + k] + high[4 + k : 5 + k] + high[7 + k : 8 + k])
                vectors.append(jnp.where(first_head(1), two[0], two[1]))
            biases[...] = rows_of(*vectors)

    rows = norm_ref.shape[0]
    product = dot_nt(pair_rows(a_ref, b_ref, (0, 1, 2)), norm_ref[...])
    bias = biases[...].T
    cosines, sines = cos_ref[...], -sin_ref[...]
    query = unturn(product[:PAIR] + bias[:, 0:1], cosines, sines).astype(bf16)
    query = query * jnp.asarray(HEAD_DIM**-0.5, bf16)
    keys = unturn(product[PAIR : 2 * PAIR] + bias[:, 1:2], cosines, sines).astype(bf16)
    values = (product[2 * PAIR :] + bias[:, 2:3]).astype(bf16)
    kept_ref[0] = query
    kept_ref[1] = keys
    kept_ref[2] = values
    parts = [slice(head * HEAD_DIM, (head + 1) * HEAD_DIM) for head in range(2)]
    for head, part in enumerate(parts):
        scores_ref[head] = dot_tn(keys[part], query[part])
    ones = jnp.ones((16, rows), bf16)
    contexts, inverses = [], []
    for head, part in enumerate(parts):
        spans = [slice(start, start + SOFT_ROWS) for start in range(0, rows, SOFT_ROWS)]
        top = None
        for span in spans:
            more = jnp.max(scores_ref[head, span], 0, keepdims=True)
            top = more if top is None else jnp.maximum(top, more)
        top = top * LOG2E
        for span in spans:
            exps_ref[head, span] = jnp.exp2(scores_ref[head, span] * LOG2E - top).astype(bf16)
        out = dot(jnp.concatenate([values[part], ones], 0), exps_ref[head])
        inverse = 1.0 / out[HEAD_DIM : HEAD_DIM + 1]
        contexts.append(out[:HEAD_DIM] * inverse)
        inverses.append(inverse)
    context = jnp.concatenate(contexts, 0).astype(bf16)
    inverse_ref[...] = rows_of(*inverses)
    kept_ref[3] = context
    more = dot_tn(context, pair_rows(a_ref, b_ref, (3,)))

    @pl.when(step == 0)
    def _():
        attn_ref[...] = more

    @pl.when(step != 0)
    def _():
        attn_ref[...] += more


def attend(norm, a, b, tile_a, tile_b, tables, heads):
    rows, width = norm.shape
    base, pairs = heads
    return pl.pallas_call(
        functools.partial(attend_kernel, base),
        grid=(pairs,),
        in_specs=[whole(norm.shape)]
        + [pl.BlockSpec((1,) + a.shape[1:], lambda i: (i + base, 0, 0, 0))] * 2
        + [tile_spec_of(tile_a)] * 2
        + [whole(tables[0].shape)] * 2,
        out_specs=[pl.BlockSpec((4, PAIR, rows), lambda i: (0, i, 0)), by_rows(8, rows)]
        + [pl.BlockSpec((2, rows, rows), lambda i: (i, 0, 0)), whole((rows, width))],
        out_shape=[
            jax.ShapeDtypeStruct((4, pairs * PAIR, rows), bf16),
            jax.ShapeDtypeStruct((8 * pairs, rows), f32),
            jax.ShapeDtypeStruct((2 * pairs, rows, rows), bf16),
            jax.ShapeDtypeStruct((rows, width), f32),
        ],
        scratch_shapes=[pltpu.VMEM((8, PAIR), f32), pltpu.VMEM((2, rows, rows), f32)],
        name="attend",
        compiler_params=params(44),
        cost_estimate=cost(8 * pairs),
    )(norm, a, b, tile_a, tile_b, *tables)


def attend_back_kernel(
    kept_ref, inverse_ref, exps_ref, grad_ref, norm_ref,
    a_ref, b_ref, cos_ref, sin_ref, out_a, out_b, back_ref, bias_ref, probs_ref, scores_ref,
):
    step = pl.program_id(0)
    rows = kept_ref.shape[2]
    query, keys, values, context = (kept_ref[k] for k in range(4))
    grad = dot_nt(pair_rows(a_ref, b_ref, (3,)), grad_ref[...])
    parts = [slice(head * HEAD_DIM, (head + 1) * HEAD_DIM) for head in range(2)]
    grads, inners = [], []
    for head, part in enumerate(parts):
        scaled = grad[part] * inverse_ref[head : head + 1]
        inners.append(column_sum(scaled * context[part].astype(f32)))
        grads.append(scaled.astype(bf16))
        probs_ref[head] = dot_tn(values[part], grads[head])
    turned = [[], [], []]
    for head, part in enumerate(parts):
        turned[2].append(dot_nt(grads[head], exps_ref[head]))
        for start in range(0, rows, SOFT_ROWS):
            span = slice(start, start + SOFT_ROWS)
            low = exps_ref[head, span].astype(f32) * (probs_ref[head, span] - inners[head])
            scores_ref[head, span] = low.astype(bf16)
        turned[0].append(dot(keys[part], scores_ref[head]))
        turned[1].append(dot_nt(query[part], scores_ref[head]))
    dq, dk, dv = (jnp.concatenate(item, 0) for item in turned)
    dq = unturn(dq * HEAD_DIM**-0.5, cos_ref[...], sin_ref[...])
    dk = unturn(dk, cos_ref[...], sin_ref[...])
    left = jnp.concatenate([dq, dk, dv], 0).astype(bf16)
    more = dot_tn(left, pair_rows(a_ref, b_ref, (0, 1, 2)))

    @pl.when(step == 0)
    def _():
        back_ref[...] = more

    @pl.when(step != 0)
    def _():
        back_ref[...] += more

    bias_ref[0] = dot_nt(jnp.ones((8, rows), bf16), left)
    inputs = dot(left, norm_ref[...]).astype(bf16)
    outputs = dot(context, grad_ref[...]).astype(bf16)
    for k in range(4):
        result = outputs if k == 3 else inputs[k * PAIR : (k + 1) * PAIR]
        out_a[0, k] = result[:HEAD_DIM]
        out_b[0, k] = result[HEAD_DIM:]


def attend_back(kept, grad, norm, a, b, tables, heads):
    saved, inverse, exps = kept
    rows, width = norm.shape
    base, count = heads
    shape = (count,) + a.shape[1:]
    columns = pl.BlockSpec((4, PAIR, rows), lambda i: (0, i, 0))
    weights = pl.BlockSpec((1,) + a.shape[1:], lambda i: (i + base, 0, 0, 0))
    return pl.pallas_call(
        attend_back_kernel,
        grid=(count,),
        in_specs=[columns, by_rows(8, rows)]
        + [pl.BlockSpec((2, rows, rows), lambda i: (i, 0, 0))]
        + [whole(norm.shape)] * 2
        + [weights] * 2
        + [whole(tables[0].shape)] * 2,
        out_specs=[pl.BlockSpec((1,) + a.shape[1:], lambda i: (i, 0, 0, 0))] * 2
        + [whole((rows, width)), pl.BlockSpec((1, 8, 3 * PAIR), lambda i: (i, 0, 0))],
        out_shape=[jax.ShapeDtypeStruct(shape, bf16)] * 2
        + [
            jax.ShapeDtypeStruct((rows, width), f32),
            jax.ShapeDtypeStruct((count, 8, 3 * PAIR), f32),
        ],
        scratch_shapes=[pltpu.VMEM((2, rows, rows), f32), pltpu.VMEM((2, rows, rows), bf16)],
        name="attend_back",
        compiler_params=params(50),
        cost_estimate=cost(9 * count),
    )(saved, inverse, exps, grad, norm, a, b, *tables)


def gelu_parts(gate):
    bell = jnp.exp2(gate * gate * (-0.5 * LOG2E))
    span = 1.0 + jnp.abs(gate) * (0.3275911 * 0.5**0.5)
    guess = pl.reciprocal(span, approx=True)
    near = guess * (2.0 - span * guess)
    tail = 1.061405429 * 0.5
    for factor in (-1.453152027, 1.421413741, -0.284496736, 0.254829592):
        tail = tail * near + factor * 0.5
    tail = tail * near * bell
    return jnp.where(gate >= 0, 1.0 - tail, tail), bell * 0.3989422804014327


def feed_block(norm, cot, up_ref, down_ref, tile, act_ref, gate_ref):
    chunk = 256
    units = up_ref.shape[1]
    spans = [slice(start, start + chunk) for start in range(0, units, chunk)]

    def first_products(span):
        bias = tile[UP_ROW : UP_ROW + 1, span].astype(f32)
        return dot(norm, up_ref[:, span]) + bias, dot_nt(cot, down_ref[span])

    sums = []
    ahead = first_products(spans[0])
    for at, span in enumerate(spans):
        gate, grad = ahead
        if at + 1 < len(spans):
            ahead = first_products(spans[at + 1])
        share, density = gelu_parts(gate)
        low = (grad * (share + gate * density)).astype(bf16)
        act_ref[:, span] = (gate * share).astype(bf16)
        gate_ref[:, span] = low
        sums.append(column_sum(low.astype(f32)))
    ffn = dot(act_ref[...], down_ref[...])
    back = dot_nt(gate_ref[...], up_ref[...])
    return ffn, back, jnp.concatenate(sums, 1)


def add_sums(ref, tile):
    @pl.when(pl.program_id(0) == 0)
    def _():
        ref[...] = tile

    @pl.when(pl.program_id(0) != 0)
    def _():
        ref[...] += tile


def feed_first_kernel(
    attn_a, attn_b, attn_c, base_ref, cot_ref, vec_ref, ua, ub, da, db, ta, tb,
    mid_ref, norm_ref, act_a, act_b, gate_a, gate_b, ffn_ref, back_ref, sums_ref,
):
    out_bias, gain, shift = (vec_ref[k : k + 1] for k in range(3))
    attn = attn_a[...] + attn_b[...] + attn_c[...]
    mid = base_ref[...] + (attn + out_bias)
    unit, _ = normalise(mid)
    norm = (unit * gain + shift).astype(bf16)
    mid_ref[...] = mid
    norm_ref[...] = norm
    cot = cot_ref[...]
    ffn, back, sum_a = feed_block(norm, cot, ua, da, ta[...], act_a, gate_a)
    more, back_more, sum_b = feed_block(norm, cot, ub, db, tb[...], act_b, gate_b)
    ffn_ref[...] = ffn + more
    back_ref[...] = back + back_more
    add_sums(sums_ref, rows_of(sum_a, sum_b))


def feed_second_kernel(
    norm_ref, mid_ref, cot_ref, vec_ref, ffn_ref, back_ref, one, two, ta, tb,
    act_a, act_b, gate_a, gate_b, mid_grad_ref, low_ref, sums_ref, *pieces,
):
    down_bias, gain = vec_ref[3:4], vec_ref[1:2]
    norm, cot = norm_ref[...], cot_ref[...]
    ffn, back, sum_a = feed_block(norm, cot, one.at[0], one.at[1], ta[...], act_a, gate_a)
    more, back_more, sum_b = feed_block(norm, cot, two.at[0], two.at[1], tb[...], act_b, gate_b)
    mid = mid_ref[...]
    out = (mid + (ffn_ref[...] + (ffn + more) + down_bias)).astype(bf16)
    rows = pieces[0].shape[0]
    back = back_ref[...] + (back + back_more)
    unit, inverse = normalise(mid)
    high = cot.astype(f32)
    grad = high + norm_back(back * gain, unit, inverse)
    low = grad.astype(bf16)
    mid_grad_ref[...] = grad
    low_ref[...] = low
    per_step = mid.shape[0] // rows
    for k, piece in enumerate(pieces):

        @pl.when(pl.program_id(0) == k // per_step)
        def _():
            piece[...] = out[k % per_step * rows : (k % per_step + 1) * rows]

    add_sums(
        sums_ref,
        rows_of(
            sum_a,
            sum_b,
            column_sum(back * unit),
            column_sum(back),
            column_sum(low.astype(f32)),
            column_sum(high),
        ),
    )


def tile_spec_of(parcel):
    at = parcel.shape[0] // TILE - 1
    return pl.BlockSpec((TILE, parcel.shape[1]), lambda i: (at, 0))


def feed_first(attns, base, cot, vectors, ups, downs, parcels):
    rows, width = base.shape
    units = ups[0].shape[1]
    piece = parcels[0].shape[0] - TILE
    step = FEED_STEP
    low = jax.ShapeDtypeStruct((rows, units), bf16)
    high = jax.ShapeDtypeStruct((rows, width), f32)
    return pl.pallas_call(
        feed_first_kernel,
        grid=(rows // step,),
        in_specs=[by_rows(step, width)] * 5
        + [whole(vectors.shape)]
        + [whole(ups[0].shape)] * 2
        + [whole(downs[0].shape)] * 2
        + [tile_spec_of(parcels[0])] * 2,
        out_specs=[by_rows(step, width)] * 2
        + [by_rows(step, units)] * 4
        + [by_rows(step, width)] * 2
        + [whole((8, width))],
        out_shape=[high, jax.ShapeDtypeStruct((rows, width), bf16)]
        + [low] * 4
        + [high, high, jax.ShapeDtypeStruct((8, width), f32)],
        name="feed_first",
        compiler_params=params(24),
        cost_estimate=cost(18),
    )(*attns, base, cot, vectors, *ups, *downs, *parcels)


def feed_second(norm, mid, cot, vectors, ffn, back, one, two, parcels):
    rows, width = mid.shape
    units = one.shape[2]
    piece = parcels[0].shape[0] - TILE
    step = FEED_STEP
    low = jax.ShapeDtypeStruct((rows, units), bf16)
    return pl.pallas_call(
        feed_second_kernel,
        grid=(rows // step,),
        in_specs=[by_rows(step, width)] * 3
        + [whole(vectors.shape)]
        + [by_rows(step, width)] * 2
        + [whole(one.shape)] * 2
        + [tile_spec_of(parcels[0])] * 2,
        out_specs=[by_rows(step, units)] * 4
        + [by_rows(step, width)] * 2
        + [whole((8, width))]
        + [whole((piece, width))] * (rows // piece),
        out_shape=[low] * 4
        + [
            jax.ShapeDtypeStruct((rows, width), f32),
            jax.ShapeDtypeStruct((rows, width), bf16),
            jax.ShapeDtypeStruct((8, width), f32),
        ]
        + [jax.ShapeDtypeStruct((piece, width), bf16)] * (rows // piece),
        name="feed_second",
        compiler_params=params(24),
        cost_estimate=cost(20),
    )(norm, mid, cot, vectors, ffn, back, one, two, *parcels)


def feed_grad_kernel(act_ref, norm_ref, cot_ref, gate_ref, down_ref, up_ref):
    down_ref[...] = dot_tn(act_ref[...], cot_ref[...]).astype(bf16)
    up_ref[...] = dot_tn(norm_ref[...], gate_ref[...]).astype(bf16)


def feed_grads(act, norm, cot, gate):
    units, width = act.shape[1], norm.shape[1]
    return pl.pallas_call(
        feed_grad_kernel,
        out_shape=[
            jax.ShapeDtypeStruct((units, width), bf16),
            jax.ShapeDtypeStruct((width, units), bf16),
        ],
        name="feed_grads",
        compiler_params=params(16),
        cost_estimate=cost(3),
    )(act, norm, cot, gate)


def finish_kernel(count, *refs):
    backs, refs = refs[:count], refs[count:]
    base_ref, mid_grad_ref, gain_ref, t0, t1, t2, t3, table_ref, sums_ref, *pieces = refs
    step = pl.program_id(0)
    piece = base_ref.shape[0]
    back = sum(ref[...] for ref in backs)
    unit, inverse = normalise(base_ref[...])
    grad = mid_grad_ref[...] + norm_back(back * gain_ref[...], unit, inverse)
    low = grad.astype(bf16)
    tile = t0[...]
    for k, other in enumerate((t1, t2, t3)):
        tile = jnp.where(step == k + 1, other[...], tile)
    onehot = onehot_of(tile, table_ref.shape[0], piece)
    total = 0.0
    for part in split_three(grad):
        total = total + dot(onehot, part)
    add_sums(table_ref, total)
    add_sums(sums_ref, rows_of(column_sum(back * unit), column_sum(back)))
    for k, out_ref in enumerate(pieces):

        @pl.when(step == k)
        def _():
            out_ref[...] = low


def finish(backs, base, mid_grad, gain, parcels, table_rows):
    rows, width = base.shape
    step = parcels[0].shape[0] - TILE
    return pl.pallas_call(
        functools.partial(finish_kernel, len(backs)),
        grid=(rows // step,),
        in_specs=[by_rows(step, width)] * (len(backs) + 2)
        + [whole(gain.shape)]
        + [tile_spec_of(parcels[0])] * 4,
        out_specs=[whole((table_rows, width)), whole((8, width))]
        + [whole((step, width))] * (rows // step),
        out_shape=[
            jax.ShapeDtypeStruct((table_rows, width), f32),
            jax.ShapeDtypeStruct((8, width), f32),
        ]
        + [jax.ShapeDtypeStruct((step, width), bf16)] * (rows // step),
        name="finish",
        compiler_params=params(60),
        cost_estimate=cost(5),
    )(*backs, base, mid_grad, gain, *parcels)


def place_kernel(axis, shift, count, *refs):
    pieces, outs = refs[:count], refs[count:]
    rank = lax.axis_index(axis) >> shift
    for distance, piece in enumerate(pieces):
        for which, out_ref in enumerate(outs):
            part = piece[which] if len(outs) > 1 else piece[...]
            out_ref[rank ^ distance] = part.astype(out_ref.dtype)


def place(pieces, dtype, axis, shift, arrays=1):
    count = len(pieces)
    shape = pieces[0].shape[1:] if arrays > 1 else pieces[0].shape
    outs = pl.pallas_call(
        functools.partial(place_kernel, axis, shift, count),
        out_shape=[jax.ShapeDtypeStruct((count,) + shape, dtype)] * arrays,
        name="place",
        compiler_params=params(12),
        cost_estimate=cost(2),
    )(*pieces)
    return outs if arrays > 1 else outs[0]


def interleave_kernel(mine_ref, other_ref, out_ref):
    bit = lax.axis_index("dp") & 1
    for k in range(mine_ref.shape[0]):
        out_ref[2 * k + bit] = mine_ref[k].astype(out_ref.dtype)
        out_ref[2 * k + 1 - bit] = other_ref[k].astype(out_ref.dtype)


def interleave(mine, other):
    count, segment, width = mine.shape
    out = pl.pallas_call(
        interleave_kernel,
        out_shape=jax.ShapeDtypeStruct((2 * count, segment, width), f32),
        name="interleave",
        compiler_params=params(12),
        cost_estimate=cost(2),
    )(mine, other[: count * segment].reshape(mine.shape))
    return out.reshape(2 * count * segment, width)


def on_device(
    hidden_in,
    codon_ids,
    start_flags,
    cotangent,
    codon_table,
    norm1_gain,
    norm1_bias,
    qkv_weight,
    qkv_bias,
    out_weight,
    out_bias,
    norm2_gain,
    norm2_bias,
    up_weight,
    up_bias,
    down_weight,
    down_bias,
):
    gene_count, piece, width = hidden_in.shape
    group = lax.axis_size("tensor")
    rank = lax.axis_index("tensor")
    local = qkv_weight.shape[2]
    heads = local // HEAD_DIM
    table_rows = codon_table.shape[0]

    spread_bias = jnp.broadcast_to(
        qkv_bias.reshape(3, heads, 1, HEAD_DIM), (3, heads, 2, HEAD_DIM)
    ).reshape(3, 2 * local)
    spread_bias = jnp.pad(spread_bias, ((0, 5), (0, width - 2 * local)))
    own = make_parcels(
        hidden_in, codon_ids, start_flags, spread_bias, up_bias[None], table_rows // 2
    )
    turned = qkv_weight.transpose(1, 2, 0).reshape(3, heads, HEAD_DIM, width)
    mixed = jnp.concatenate(
        [turned.transpose(1, 0, 2, 3), out_weight.reshape(heads, 1, HEAD_DIM, width)], 1
    )
    blocks = (mixed.reshape(4 * local, width), up_weight, down_weight)
    bit = lax.axis_index("dp") & 1
    half = width // 2

    def half_of(block):
        return lax.dynamic_slice_in_dim(block, bit * half, half, 0)

    def join(one, two):
        return jnp.where(
            bit == 0, jnp.concatenate([one, two], -2), jnp.concatenate([two, one], -2)
        )

    def as_mix(block):
        return block.reshape(heads, 4, HEAD_DIM, width)

    def flat(item):
        return item.reshape(-1, width)

    own_cot = [pick(cotangent, rank ^ r) for r in range(group)]
    cot_stack = jnp.stack(own_cot[2:])
    up_half = half_of(blocks[1])
    quarter = width // 4
    down_first, down_last = down_weight[:quarter], down_weight[quarter:]

    frequencies = 10000.0 ** (-jnp.arange(HEAD_DIM // 2, dtype=f32) * 2.0 / HEAD_DIM)
    positions = jnp.concatenate(
        [((rank ^ r) * piece + jnp.arange(piece)).astype(f32) for r in range(group)]
    )
    angles = frequencies[:, None] * positions[None, :]
    tables = (jnp.cos(angles), jnp.sin(angles))

    def local_work():
        return tables, half_of(blocks[0]), up_half, own_cot, cot_stack, down_first, down_last

    got, (tables, mix_half, up_half, own_cot, cot_stack, down_first, down_last) = stage(
        [(own[r], "tensor", r) for r in (2, 3, 1)], local_work
    )
    parcels = [own[0], got[2], got[0], got[1]]
    (mix_mate,) = together((swap(blocks[0], "tensor", 1),))
    mixes = [as_mix(blocks[0]), as_mix(mix_mate)]
    early, late, every = (0, 1), (1, heads - 1), (0, heads)

    def first_heads(parcels):
        base, norm1 = embed(parcels, codon_table, norm1_gain[None], norm1_bias[None])
        return base, norm1, attend(norm1, *mixes[:2], *parcels[:2], tables, early)

    got, (base, norm1, (*kept0, attn0)) = stage(
        [(mix_half, "tensor", 2), (blocks[1], "tensor", 1), (blocks[2], "tensor", 1)],
        first_heads,
        parcels,
    )
    mix_half, *mates = got
    (mix_other, cot_across), (*kept1, attn1) = stage(
        [(mix_half, "dp", 1), (cot_stack, "tensor", 2)],
        lambda norm: attend(norm, *mixes[:2], *parcels[:2], tables, late),
        norm1,
    )
    across_mix = join(mix_half, mix_other)
    (across_mate, got), _ = stage(
        [(across_mix, "tensor", 1), mate_transfer(own_cot, cot_across)], lambda: ()
    )
    mixes += [as_mix(across_mix), as_mix(across_mate)]
    cot = jnp.concatenate(four(own_cot, cot_across, got), 0)
    (up_half, down_part), (*kept2, attn2) = stage(
        [(up_half, "tensor", 2), (down_first, "tensor", 2)],
        lambda norm: attend(norm, *mixes[2:], *parcels[2:], tables, every),
        norm1,
    )
    vectors = jnp.stack([out_bias, norm2_gain, norm2_bias, down_bias])

    def feed_near(base, cot):
        results = feed_first(
            (attn0, attn1, attn2), base, cot, vectors,
            (up_weight, mates[0]), (down_weight, mates[1]), parcels[:2],
        )
        return results, feed_grads(results[3], results[1], cot, results[5])

    (up_other, down_rest), (results, sent) = stage(
        [(up_half, "dp", 1), (down_last, "tensor", 2)], feed_near, base, cot
    )
    mid, norm2, act0, act1, gate0, gate1, ffn, back, sums_first = results

    def feed_join(one, two, down_one, down_two):
        across = jnp.stack([join(one, two), jnp.concatenate([down_one, down_two], 0)])
        return feed_grads(act0, norm2, cot, gate0), across

    got, (near, feed_across) = stage(
        [(item, "tensor", 1) for item in sent],
        feed_join, up_half, up_other, down_part, down_rest,
    )
    (feed_mate,), (keep_near, send_near) = stage(
        [(feed_across, "tensor", 1)],
        lambda near, got: add_halve(near[0], got[0], near[1], got[1]),
        near,
        got,
    )

    def feed_far(ffn):
        results = feed_second(
            norm2, mid, cot, vectors, ffn, back, feed_across, feed_mate, parcels[2:]
        )
        sent = feed_grads(results[1], norm2, cot, results[3])
        return results, sent, feed_grads(results[0], norm2, cot, results[2])

    (got_near,), (results, sent, far) = stage([(send_near, "dp", 1)], feed_far, ffn)
    act2, act3, gate2, gate3, mid_grad, grad_low, sums_second, *out_pieces = results
    got, near = stage(
        [(item, "tensor", 1) for item in sent], lambda *pair: add_low(*pair), keep_near, got_near
    )
    keep_far, send_far = add_halve(far[0], got[0], far[1], got[1])

    def back_part(saved, block, span):
        return lambda grad: attend_back(
            saved, grad, norm1, mixes[block], mixes[block + 1], tables, span
        )

    near_steps = Scatter(near, 1)
    (*near_got, got_far, out_across), (mix2, mix3, back_a, bias_far) = stage(
        near_steps.transfers() + [(send_far, "dp", 1), (jnp.stack(out_pieces[2:]), "tensor", 2)],
        back_part(kept2, 2, every),
        grad_low,
    )
    far_steps = Scatter(add_low(keep_far, got_far), 1)
    (got,), _ = stage([(mix3, "tensor", 1)], lambda sends: sends, far_steps.sends)
    far_mix = add_low(mix2, got)
    (*far_got, cross, out_got), (mix0a, mix1a, back_c, bias_c) = stage(
        far_steps.transfers()
        + [(far_mix, "tensor", 2), mate_transfer(out_pieces, out_across)],
        back_part(kept1, 0, late),
        grad_low,
    )
    near_piece = near_steps.finish(near_got)
    far_piece = far_steps.finish(far_got)
    (feed_cross, got), (mix0b, mix1b, back_d, bias_d) = stage(
        [(far_piece, "tensor", 2), (mix1a, "tensor", 1)], back_part(kept0, 0, early), grad_low
    )
    feed_piece = add_low(near_piece, feed_cross)
    mix_keep, mix_send = halve_heads(
        jnp.concatenate(
            [add_low(mix0b, cross[:1]), add_low(mix0a, got, cross[1:]), mix1b], 0
        )
    )
    (*feed_got, mix_got), (table_part, sums_last, *grad_pieces) = stage(
        upper_transfers(feed_piece) + [(mix_send, "dp", 1)],
        lambda mid_grad: finish(
            (back_a, back_c, back_d), base, mid_grad, norm1_gain[None], parcels, table_rows
        ),
        mid_grad,
    )
    bias_near = jnp.concatenate([bias_d, bias_c], 0)

    def by_owner(blocks):
        swapped = jnp.where(rank & 1 == 1, blocks[jnp.array([1, 0, 3, 2])], blocks)
        return jnp.where(rank & 2 == 2, swapped[jnp.array([2, 3, 0, 1])], swapped)

    up_rows = by_owner(jnp.concatenate([sums_first[:2], sums_second[:2]], 0))
    qkv_rows = jnp.stack([bias_near, bias_far])[:, :, 0].reshape(2, heads, 3, 2, HEAD_DIM)
    qkv_rows = qkv_rows.transpose(0, 3, 2, 1, 4).reshape(group, 3, local)
    qkv_rows = by_owner(qkv_rows).transpose(1, 0, 2).reshape(3, width)
    vectors = jnp.concatenate([sums_last[:2], sums_second[2:6], up_rows, qkv_rows], 0)
    vectors = jnp.pad(vectors, ((0, 32 - vectors.shape[0]), (0, 0)))
    small = jnp.concatenate([table_part.astype(bf16), vectors.astype(bf16)], 0)
    core = rank & 1
    count = small.shape[0] // 2
    small_keep = lax.dynamic_slice_in_dim(small, core * count, count, 0)
    small_send = lax.dynamic_slice_in_dim(small, (1 - core) * count, count, 0)
    segment = mix_keep.shape[1] // (heads + 1)
    mix_sum = add_low(mix_keep, mix_got)
    mate_share = mix_sum[:, -segment:]
    (got, mate_got), (down_part, up_part) = stage(
        [(small_send, "tensor", 1), (mate_share, "tensor", 1)],
        lambda pieces: place(pieces, bf16, "dp", 1, 2),
        [feed_piece] + feed_got,
    )
    small = add_low(small_keep, got)
    mix_own = add_low(mix_sum[:, :segment], mate_got)
    mix_steps = Scatter(jnp.concatenate([mix_own, mix_sum[:, segment:-segment]], 1))
    to_other = jnp.concatenate(grad_pieces[2:] + [small], 0)
    (*mix_got, crossed, down_other), _ = stage(
        mix_steps.transfers() + [(to_other, "tensor", 2), (flat(down_part), "dp", 1)], lambda: ()
    )
    small = add_low(small, crossed[2 * piece :])
    mix_piece = mix_steps.finish(mix_got)
    grad_across = [crossed[:piece], crossed[piece : 2 * piece]]
    (*mix_got, up_other, grad_got), down_grad = stage(
        upper_transfers(mix_piece)
        + [
            (jnp.concatenate([flat(up_part), small], 0), "dp", 1),
            mate_transfer(grad_pieces, grad_across),
        ],
        interleave,
        down_part,
        down_other,
    )
    size = flat(up_part).shape[0]
    small = add_low(small, up_other[size:])
    mix_part = place([mix_piece] + mix_got, bf16, "dp", 1)
    (*got, other), (up_grad, hidden_out, hidden_grad) = stage(
        upper_transfers(small) + [(flat(mix_part), "dp", 1)],
        lambda part, rows, out, grad: (
            interleave(part, rows),
            place(out, bf16, "tensor", 0),
            place(grad, f32, "tensor", 0),
        ),
        up_part,
        up_other,
        four(out_pieces, out_across, out_got),
        four(grad_pieces, grad_across, grad_got),
    )
    small = add_low(small, *got)
    (other_half,), mix_grad = stage(
        [(small, "tensor", 1)], interleave, mix_part, other
    )
    small = jnp.where(
        core == 0,
        jnp.concatenate([small, other_half], 0),
        jnp.concatenate([other_half, small], 0),
    ).astype(f32)
    owners = lax.axis_size("dp") // 4
    mix_grad = mix_grad.reshape(4, owners, heads, HEAD_DIM // owners, width)
    qkv_grad = mix_grad[:3].transpose(4, 0, 2, 1, 3).reshape(width, 3, local)
    out_grad = mix_grad[3].transpose(1, 0, 2, 3).reshape(local, width)
    at = table_rows
    rows = [small[at + k] for k in range(6)]
    up_bias_grad = lax.dynamic_index_in_dim(small[at + 6 : at + 6 + group], rank, 0, keepdims=False)
    qkv_bias_grad = lax.dynamic_slice_in_dim(
        small[at + 6 + group : at + 9 + group], rank * local, local, 1
    )
    return (
        hidden_out,
        hidden_grad,
        small[:table_rows],
        rows[0],
        rows[1],
        qkv_grad,
        qkv_bias_grad,
        out_grad,
        rows[4],
        rows[2],
        rows[3],
        up_grad,
        up_bias_grad,
        down_grad,
        rows[5],
    )


def solution(mesh):
    rows_placed = P("dp", "tensor", None)
    return jax.shard_map(
        on_device,
        mesh=mesh,
        in_specs=(
            rows_placed,
            P("dp", "tensor"),
            P("dp", "tensor"),
            rows_placed,
            P(),
            P(),
            P(),
            P(None, None, "tensor"),
            P(None, "tensor"),
            P("tensor", None),
            P(),
            P(),
            P(),
            P(None, "tensor"),
            P("tensor"),
            P("tensor", None),
            P(),
        ),
        out_specs=(
            rows_placed,
            rows_placed,
            P(),
            P(),
            P(),
            P(None, None, "tensor"),
            P(None, "tensor"),
            P("tensor", None),
            P(),
            P(),
            P(),
            P(None, "tensor"),
            P("tensor"),
            P("tensor", None),
            P(),
        ),
        check_vma=False,
    )
```

```python
import functools

import jax
import jax.numpy as jnp
from jax import lax
from jax.experimental import pallas as pl
from jax.experimental.pallas import tpu as pltpu
from jax.sharding import PartitionSpec as P

HEAD_DIM = 64
PAIR = 2 * HEAD_DIM
EPSILON = 1e-05
HIGHEST = lax.Precision.HIGHEST
NT = (((1,), (1,)), ((), ()))
TN = (((0,), (0,)), ((), ()))
LOG2E = 1.4426950408889634
TILE = 16
UP_ROW = 10
BIAS_HEADS = 3
SOFT_ROWS = 128
FEED_STEP = 256
bf16 = jnp.bfloat16
f32 = jnp.float32


def params(mebibytes):
    return pltpu.CompilerParams(vmem_limit_bytes=mebibytes * 1024 * 1024)


def cost(microseconds):
    return pl.CostEstimate(
        flops=microseconds * 10**9, bytes_accessed=microseconds * 10**6, transcendentals=0
    )


def dot(left, right):
    return jnp.dot(left, right, preferred_element_type=f32)


def dot_nt(left, right):
    return lax.dot_general(left, right, NT, preferred_element_type=f32)


def dot_tn(left, right):
    return lax.dot_general(left, right, TN, preferred_element_type=f32)


def whole(shape):
    return pl.BlockSpec(shape, lambda i: (0,) * len(shape))


def by_rows(rows, cols):
    return pl.BlockSpec((rows, cols), lambda i: (i, 0))


def by_cols(rows, cols):
    return pl.BlockSpec((rows, cols), lambda i: (0, i))


def swap(array_in, axis, distance):
    size = lax.axis_size(axis)
    return lax.ppermute(array_in, axis, [(i, i ^ distance) for i in range(size)])


def together(items):
    return lax.optimization_barrier(items)


def stage(sends, work, *inputs):
    arrays, inputs = together(([item[0] for item in sends], inputs))
    got = [swap(array, axis, distance) for array, (_, axis, distance) in zip(arrays, sends)]
    return together((got, work(*inputs)))


def add_low(*terms):
    return sum(term.astype(f32) for term in terms).astype(bf16)


def core_sum(mine, other):
    return add_low(mine, swap(other, "tensor", 1))


def halve(rows):
    size = lax.axis_size("dp")
    segment = rows.shape[0] // size
    halves = rows.reshape(size // 2, 2, segment, rows.shape[1])
    mine = lax.axis_index("dp") & 1
    keep = lax.dynamic_index_in_dim(halves, mine, 1, keepdims=False)
    send = lax.dynamic_index_in_dim(halves, 1 - mine, 1, keepdims=False)
    return keep, send


def halve_heads(blocks):
    heads, width = blocks.shape[0], blocks.shape[-1]
    size = lax.axis_size("dp")
    mine = lax.axis_index("dp") & 1
    halves = blocks.reshape(heads, size // 2, 2, -1, width)
    return [
        lax.dynamic_index_in_dim(halves, which, 2, keepdims=False)
        .transpose(1, 0, 2, 3)
        .reshape(size // 2, -1, width)
        for which in (mine, 1 - mine)
    ]


def add_halve_kernel(one, got_one, two, got_two, keep_ref, send_ref):
    mine = lax.axis_index("dp") & 1
    for which, (left, right) in enumerate(((one, got_one), (two, got_two))):
        for k in range(keep_ref.shape[1]):
            for index, out_ref in ((mine, keep_ref), (1 - mine, send_ref)):
                out_ref[which, k] = add_low(left[k, index], right[k, index])


def add_halve(one, got_one, two, got_two):
    size = lax.axis_size("dp")
    rows, width = one.shape
    shape = jax.ShapeDtypeStruct((2, size // 2, rows // size, width), bf16)
    return pl.pallas_call(
        add_halve_kernel,
        out_shape=[shape] * 2,
        name="add_halve",
        compiler_params=params(16),
        cost_estimate=cost(2),
    )(*(item.reshape((size // 2, 2) + shape.shape[2:]) for item in (one, got_one, two, got_two)))


def pick(array_in, index):
    return lax.dynamic_index_in_dim(array_in, index, 0, keepdims=False)


class Scatter:
    def __init__(self, current, axis=0):
        self.row = lax.axis_index("dp") >> 1
        self.own, *self.sends = (
            lax.dynamic_index_in_dim(current, self.row ^ j, axis, keepdims=False)
            for j in range(current.shape[axis])
        )

    def transfers(self):
        return [(item, "dp", 2 * j + 2) for j, item in enumerate(self.sends)]

    def finish(self, got):
        return add_low(self.own, *got)


def upper_transfers(segment):
    return [(segment, "dp", 2 * j) for j in range(1, lax.axis_size("dp") // 2)]


def mate_transfer(pieces, crossed):
    return (jnp.stack([pieces[1], crossed[1]]), "tensor", 1)


def four(pieces, crossed, got):
    return [pieces[0], got[0], crossed[0], got[1]]


def normalise(row_data):
    row_mean = jnp.mean(row_data, axis=-1, keepdims=True)
    centred = row_data - row_mean
    row_var = jnp.mean(centred * centred, axis=-1, keepdims=True)
    inverse = lax.rsqrt(row_var + EPSILON)
    return centred * inverse, inverse


def norm_back(scaled, unit, inverse):
    return inverse * (
        scaled
        - jnp.mean(scaled, -1, keepdims=True)
        - unit * jnp.mean(scaled * unit, -1, keepdims=True)
    )


def column_sum(array_in):
    return jnp.sum(array_in, 0, keepdims=True)


def rows_of(*vectors):
    width = vectors[0].shape[1]
    at = lax.broadcasted_iota(jnp.int32, (8, width), 0)
    tile = jnp.zeros((8, width), f32)
    for k, vector in enumerate(vectors):
        tile = jnp.where(at == k, vector, tile)
    return tile


def first_head(rows):
    return lax.broadcasted_iota(jnp.int32, (rows, PAIR), 1) < HEAD_DIM


def unturn(values_in, cosines, sines):
    quarter = HEAD_DIM // 2
    parts = [values_in[k * quarter : (k + 1) * quarter] for k in range(4)]
    out = []
    for low, high in (parts[:2], parts[2:]):
        out += [low * cosines + high * sines, high * cosines - low * sines]
    return jnp.concatenate(out, 0)


def split_three(values_in):
    high = values_in.astype(bf16)
    rest = values_in - high.astype(f32)
    middle = rest.astype(bf16)
    return high, middle, (rest - middle.astype(f32)).astype(bf16)


def parcel_kernel(half, hidden_ref, ids_ref, flags_ref, bias_ref, up_ref, *outs):
    rank = lax.axis_index("tensor")
    piece, width = hidden_ref.shape[1:]
    at = lax.broadcasted_iota(jnp.int32, (TILE, width), 0)
    tile = jnp.where(at == UP_ROW, up_ref[...].astype(f32), 0.0)
    rest = bias_ref[...]
    for part in range(3):
        high = rest.astype(bf16).astype(f32)
        rest = rest - high
        for k in range(3):
            tile = jnp.where(at == 1 + 3 * part + k, high[k : k + 1], tile)
    for distance, out_ref in enumerate(outs):
        gene = rank ^ distance
        out_ref[:piece] = hidden_ref[gene]
        index = (ids_ref[pl.ds(gene, 1)] + half * flags_ref[pl.ds(gene, 1)]).astype(f32)
        index = jnp.concatenate([index, jnp.zeros((1, width - piece), f32)], 1)
        out_ref[piece:] = jnp.where(at == 0, index, tile).astype(bf16)


def make_parcels(hidden_in, codon_ids, start_flags, bias, up_bias, half):
    genes, piece, width = hidden_in.shape
    shape = jax.ShapeDtypeStruct((piece + TILE, width), bf16)
    return pl.pallas_call(
        functools.partial(parcel_kernel, half),
        out_shape=[shape] * genes,
        name="parcels",
        compiler_params=params(48),
        cost_estimate=cost(2),
    )(hidden_in, codon_ids, start_flags, bias, up_bias)


def onehot_of(tile, table_rows, piece):
    index = tile[0:1, :piece].astype(f32)
    at = lax.broadcasted_iota(jnp.int32, (table_rows, piece), 0).astype(f32)
    return (at == index).astype(bf16)


def embed_kernel(p0, p1, p2, p3, table_ref, gain_ref, shift_ref, base_ref, norm_ref, held):
    step = pl.program_id(0)
    piece = base_ref.shape[0]
    for k, parcel in enumerate((p0, p1, p2, p3)):

        @pl.when(step == k)
        def _():
            held[...] = parcel[...]

    onehot = onehot_of(held[piece:], table_ref.shape[0], piece)
    base = held[:piece].astype(f32)
    for part in split_three(table_ref[...]):
        base = base + dot_tn(onehot, part)
    unit, _ = normalise(base)
    base_ref[...] = base
    norm_ref[...] = (unit * gain_ref[...] + shift_ref[...]).astype(bf16)


def embed(parcels, table, gain, shift):
    rows, width = parcels[0].shape
    piece = rows - TILE
    return pl.pallas_call(
        embed_kernel,
        grid=(len(parcels),),
        in_specs=[whole(parcels[0].shape)] * 4
        + [whole(table.shape), whole(gain.shape), whole(shift.shape)],
        out_specs=[by_rows(piece, width)] * 2,
        out_shape=[
            jax.ShapeDtypeStruct((4 * piece, width), f32),
            jax.ShapeDtypeStruct((4 * piece, width), bf16),
        ],
        scratch_shapes=[pltpu.VMEM((rows, width), bf16)],
        name="embed",
        compiler_params=params(48),
        cost_estimate=cost(4),
    )(*parcels, table, gain, shift)


def pair_rows(a_ref, b_ref, parts):
    return jnp.concatenate([ref[0, part] for part in parts for ref in (a_ref, b_ref)], 0)


def attend_kernel(
    base, norm_ref, a_ref, b_ref, ta_ref, tb_ref, cos_ref, sin_ref,
    kept_ref, inverse_ref, exps_ref, attn_ref, biases, scores_ref,
):
    step = pl.program_id(0)
    for head in range(BIAS_HEADS):

        @pl.when(step + base == head)
        def _():
            vectors = []
            lanes = slice(head * PAIR, (head + 1) * PAIR)
            for k in range(3):
                two = []
                for tile in (ta_ref, tb_ref):
                    high = tile[...].astype(f32)[:, lanes]
                    two.append(high[1 + k : 2 + k] + high[4 + k : 5 + k] + high[7 + k : 8 + k])
                vectors.append(jnp.where(first_head(1), two[0], two[1]))
            biases[...] = rows_of(*vectors)

    rows = norm_ref.shape[0]
    product = dot_nt(pair_rows(a_ref, b_ref, (0, 1, 2)), norm_ref[...])
    bias = biases[...].T
    cosines, sines = cos_ref[...], -sin_ref[...]
    query = unturn(product[:PAIR] + bias[:, 0:1], cosines, sines).astype(bf16)
    query = query * jnp.asarray(HEAD_DIM**-0.5, bf16)
    keys = unturn(product[PAIR : 2 * PAIR] + bias[:, 1:2], cosines, sines).astype(bf16)
    values = (product[2 * PAIR :] + bias[:, 2:3]).astype(bf16)
    kept_ref[0] = query
    kept_ref[1] = keys
    kept_ref[2] = values
    parts = [slice(head * HEAD_DIM, (head + 1) * HEAD_DIM) for head in range(2)]
    for head, part in enumerate(parts):
        scores_ref[head] = dot_tn(keys[part], query[part])
    ones = jnp.ones((16, rows), bf16)
    contexts, inverses = [], []
    for head, part in enumerate(parts):
        spans = [slice(start, start + SOFT_ROWS) for start in range(0, rows, SOFT_ROWS)]
        top = None
        for span in spans:
            more = jnp.max(scores_ref[head, span], 0, keepdims=True)
            top = more if top is None else jnp.maximum(top, more)
        top = top * LOG2E
        for span in spans:
            exps_ref[head, span] = jnp.exp2(scores_ref[head, span] * LOG2E - top).astype(bf16)
        out = dot(jnp.concatenate([values[part], ones], 0), exps_ref[head])
        inverse = 1.0 / out[HEAD_DIM : HEAD_DIM + 1]
        contexts.append(out[:HEAD_DIM] * inverse)
        inverses.append(inverse)
    context = jnp.concatenate(contexts, 0).astype(bf16)
    inverse_ref[...] = rows_of(*inverses)
    kept_ref[3] = context
    more = dot_tn(context, pair_rows(a_ref, b_ref, (3,)))

    @pl.when(step == 0)
    def _():
        attn_ref[...] = more

    @pl.when(step != 0)
    def _():
        attn_ref[...] += more


def attend(norm, a, b, tile_a, tile_b, tables, heads):
    rows, width = norm.shape
    base, pairs = heads
    return pl.pallas_call(
        functools.partial(attend_kernel, base),
        grid=(pairs,),
        in_specs=[whole(norm.shape)]
        + [pl.BlockSpec((1,) + a.shape[1:], lambda i: (i + base, 0, 0, 0))] * 2
        + [tile_spec_of(tile_a)] * 2
        + [whole(tables[0].shape)] * 2,
        out_specs=[pl.BlockSpec((4, PAIR, rows), lambda i: (0, i, 0)), by_rows(8, rows)]
        + [pl.BlockSpec((2, rows, rows), lambda i: (i, 0, 0)), whole((rows, width))],
        out_shape=[
            jax.ShapeDtypeStruct((4, pairs * PAIR, rows), bf16),
            jax.ShapeDtypeStruct((8 * pairs, rows), f32),
            jax.ShapeDtypeStruct((2 * pairs, rows, rows), bf16),
            jax.ShapeDtypeStruct((rows, width), f32),
        ],
        scratch_shapes=[pltpu.VMEM((8, PAIR), f32), pltpu.VMEM((2, rows, rows), f32)],
        name="attend",
        compiler_params=params(44),
        cost_estimate=cost(8 * pairs),
    )(norm, a, b, tile_a, tile_b, *tables)


def attend_back_kernel(
    kept_ref, inverse_ref, exps_ref, grad_ref, norm_ref,
    a_ref, b_ref, cos_ref, sin_ref, out_a, out_b, back_ref, bias_ref, probs_ref, scores_ref,
):
    step = pl.program_id(0)
    rows = kept_ref.shape[2]
    query, keys, values, context = (kept_ref[k] for k in range(4))
    grad = dot_nt(pair_rows(a_ref, b_ref, (3,)), grad_ref[...])
    parts = [slice(head * HEAD_DIM, (head + 1) * HEAD_DIM) for head in range(2)]
    grads, inners = [], []
    for head, part in enumerate(parts):
        scaled = grad[part] * inverse_ref[head : head + 1]
        inners.append(column_sum(scaled * context[part].astype(f32)))
        grads.append(scaled.astype(bf16))
        probs_ref[head] = dot_tn(values[part], grads[head])
    turned = [[], [], []]
    for head, part in enumerate(parts):
        turned[2].append(dot_nt(grads[head], exps_ref[head]))
        for start in range(0, rows, SOFT_ROWS):
            span = slice(start, start + SOFT_ROWS)
            low = exps_ref[head, span].astype(f32) * (probs_ref[head, span] - inners[head])
            scores_ref[head, span] = low.astype(bf16)
        turned[0].append(dot(keys[part], scores_ref[head]))
        turned[1].append(dot_nt(query[part], scores_ref[head]))
    dq, dk, dv = (jnp.concatenate(item, 0) for item in turned)
    dq = unturn(dq * HEAD_DIM**-0.5, cos_ref[...], sin_ref[...])
    dk = unturn(dk, cos_ref[...], sin_ref[...])
    left = jnp.concatenate([dq, dk, dv], 0).astype(bf16)
    more = dot_tn(left, pair_rows(a_ref, b_ref, (0, 1, 2)))

    @pl.when(step == 0)
    def _():
        back_ref[...] = more

    @pl.when(step != 0)
    def _():
        back_ref[...] += more

    bias_ref[0] = dot_nt(jnp.ones((8, rows), bf16), left)
    inputs = dot(left, norm_ref[...]).astype(bf16)
    outputs = dot(context, grad_ref[...]).astype(bf16)
    for k in range(4):
        result = outputs if k == 3 else inputs[k * PAIR : (k + 1) * PAIR]
        out_a[0, k] = result[:HEAD_DIM]
        out_b[0, k] = result[HEAD_DIM:]


def attend_back(kept, grad, norm, a, b, tables, heads):
    saved, inverse, exps = kept
    rows, width = norm.shape
    base, count = heads
    shape = (count,) + a.shape[1:]
    columns = pl.BlockSpec((4, PAIR, rows), lambda i: (0, i, 0))
    weights = pl.BlockSpec((1,) + a.shape[1:], lambda i: (i + base, 0, 0, 0))
    return pl.pallas_call(
        attend_back_kernel,
        grid=(count,),
        in_specs=[columns, by_rows(8, rows)]
        + [pl.BlockSpec((2, rows, rows), lambda i: (i, 0, 0))]
        + [whole(norm.shape)] * 2
        + [weights] * 2
        + [whole(tables[0].shape)] * 2,
        out_specs=[pl.BlockSpec((1,) + a.shape[1:], lambda i: (i, 0, 0, 0))] * 2
        + [whole((rows, width)), pl.BlockSpec((1, 8, 3 * PAIR), lambda i: (i, 0, 0))],
        out_shape=[jax.ShapeDtypeStruct(shape, bf16)] * 2
        + [
            jax.ShapeDtypeStruct((rows, width), f32),
            jax.ShapeDtypeStruct((count, 8, 3 * PAIR), f32),
        ],
        scratch_shapes=[pltpu.VMEM((2, rows, rows), f32), pltpu.VMEM((2, rows, rows), bf16)],
        name="attend_back",
        compiler_params=params(50),
        cost_estimate=cost(9 * count),
    )(saved, inverse, exps, grad, norm, a, b, *tables)


def gelu_parts(gate):
    bell = jnp.exp2(gate * gate * (-0.5 * LOG2E))
    span = 1.0 + jnp.abs(gate) * (0.3275911 * 0.5**0.5)
    guess = pl.reciprocal(span, approx=True)
    near = guess * (2.0 - span * guess)
    tail = 1.061405429 * 0.5
    for factor in (-1.453152027, 1.421413741, -0.284496736, 0.254829592):
        tail = tail * near + factor * 0.5
    tail = tail * near * bell
    return jnp.where(gate >= 0, 1.0 - tail, tail), bell * 0.3989422804014327


def feed_block(norm, cot, up_ref, down_ref, tile, act_ref, gate_ref):
    chunk = 256
    units = up_ref.shape[1]
    spans = [slice(start, start + chunk) for start in range(0, units, chunk)]

    def first_products(span):
        bias = tile[UP_ROW : UP_ROW + 1, span].astype(f32)
        return dot(norm, up_ref[:, span]) + bias, dot_nt(cot, down_ref[span])

    sums = []
    ahead = first_products(spans[0])
    for at, span in enumerate(spans):
        gate, grad = ahead
        if at + 1 < len(spans):
            ahead = first_products(spans[at + 1])
        share, density = gelu_parts(gate)
        low = (grad * (share + gate * density)).astype(bf16)
        act_ref[:, span] = (gate * share).astype(bf16)
        gate_ref[:, span] = low
        sums.append(column_sum(low.astype(f32)))
    ffn = dot(act_ref[...], down_ref[...])
    back = dot_nt(gate_ref[...], up_ref[...])
    return ffn, back, jnp.concatenate(sums, 1)


def add_sums(ref, tile):
    @pl.when(pl.program_id(0) == 0)
    def _():
        ref[...] = tile

    @pl.when(pl.program_id(0) != 0)
    def _():
        ref[...] += tile


def feed_first_kernel(
    attn_a, attn_b, attn_c, base_ref, cot_ref, vec_ref, ua, ub, da, db, ta, tb,
    mid_ref, norm_ref, act_a, act_b, gate_a, gate_b, ffn_ref, back_ref, sums_ref,
):
    out_bias, gain, shift = (vec_ref[k : k + 1] for k in range(3))
    attn = attn_a[...] + attn_b[...] + attn_c[...]
    mid = base_ref[...] + (attn + out_bias)
    unit, _ = normalise(mid)
    norm = (unit * gain + shift).astype(bf16)
    mid_ref[...] = mid
    norm_ref[...] = norm
    cot = cot_ref[...]
    ffn, back, sum_a = feed_block(norm, cot, ua, da, ta[...], act_a, gate_a)
    more, back_more, sum_b = feed_block(norm, cot, ub, db, tb[...], act_b, gate_b)
    ffn_ref[...] = ffn + more
    back_ref[...] = back + back_more
    add_sums(sums_ref, rows_of(sum_a, sum_b))


def feed_second_kernel(
    norm_ref, mid_ref, cot_ref, vec_ref, ffn_ref, back_ref, one, two, ta, tb,
    act_a, act_b, gate_a, gate_b, mid_grad_ref, low_ref, sums_ref, *pieces,
):
    down_bias, gain = vec_ref[3:4], vec_ref[1:2]
    norm, cot = norm_ref[...], cot_ref[...]
    ffn, back, sum_a = feed_block(norm, cot, one.at[0], one.at[1], ta[...], act_a, gate_a)
    more, back_more, sum_b = feed_block(norm, cot, two.at[0], two.at[1], tb[...], act_b, gate_b)
    mid = mid_ref[...]
    out = (mid + (ffn_ref[...] + (ffn + more) + down_bias)).astype(bf16)
    rows = pieces[0].shape[0]
    back = back_ref[...] + (back + back_more)
    unit, inverse = normalise(mid)
    high = cot.astype(f32)
    grad = high + norm_back(back * gain, unit, inverse)
    low = grad.astype(bf16)
    mid_grad_ref[...] = grad
    low_ref[...] = low
    per_step = mid.shape[0] // rows
    for k, piece in enumerate(pieces):

        @pl.when(pl.program_id(0) == k // per_step)
        def _():
            piece[...] = out[k % per_step * rows : (k % per_step + 1) * rows]

    add_sums(
        sums_ref,
        rows_of(
            sum_a,
            sum_b,
            column_sum(back * unit),
            column_sum(back),
            column_sum(low.astype(f32)),
            column_sum(high),
        ),
    )


def tile_spec_of(parcel):
    at = parcel.shape[0] // TILE - 1
    return pl.BlockSpec((TILE, parcel.shape[1]), lambda i: (at, 0))


def feed_first(attns, base, cot, vectors, ups, downs, parcels):
    rows, width = base.shape
    units = ups[0].shape[1]
    piece = parcels[0].shape[0] - TILE
    step = FEED_STEP
    low = jax.ShapeDtypeStruct((rows, units), bf16)
    high = jax.ShapeDtypeStruct((rows, width), f32)
    return pl.pallas_call(
        feed_first_kernel,
        grid=(rows // step,),
        in_specs=[by_rows(step, width)] * 5
        + [whole(vectors.shape)]
        + [whole(ups[0].shape)] * 2
        + [whole(downs[0].shape)] * 2
        + [tile_spec_of(parcels[0])] * 2,
        out_specs=[by_rows(step, width)] * 2
        + [by_rows(step, units)] * 4
        + [by_rows(step, width)] * 2
        + [whole((8, width))],
        out_shape=[high, jax.ShapeDtypeStruct((rows, width), bf16)]
        + [low] * 4
        + [high, high, jax.ShapeDtypeStruct((8, width), f32)],
        name="feed_first",
        compiler_params=params(24),
        cost_estimate=cost(18),
    )(*attns, base, cot, vectors, *ups, *downs, *parcels)


def feed_second(norm, mid, cot, vectors, ffn, back, one, two, parcels):
    rows, width = mid.shape
    units = one.shape[2]
    piece = parcels[0].shape[0] - TILE
    step = FEED_STEP
    low = jax.ShapeDtypeStruct((rows, units), bf16)
    return pl.pallas_call(
        feed_second_kernel,
        grid=(rows // step,),
        in_specs=[by_rows(step, width)] * 3
        + [whole(vectors.shape)]
        + [by_rows(step, width)] * 2
        + [whole(one.shape)] * 2
        + [tile_spec_of(parcels[0])] * 2,
        out_specs=[by_rows(step, units)] * 4
        + [by_rows(step, width)] * 2
        + [whole((8, width))]
        + [whole((piece, width))] * (rows // piece),
        out_shape=[low] * 4
        + [
            jax.ShapeDtypeStruct((rows, width), f32),
            jax.ShapeDtypeStruct((rows, width), bf16),
            jax.ShapeDtypeStruct((8, width), f32),
        ]
        + [jax.ShapeDtypeStruct((piece, width), bf16)] * (rows // piece),
        name="feed_second",
        compiler_params=params(24),
        cost_estimate=cost(20),
    )(norm, mid, cot, vectors, ffn, back, one, two, *parcels)


def feed_grad_kernel(act_ref, norm_ref, cot_ref, gate_ref, down_ref, up_ref):
    down_ref[...] = dot_tn(act_ref[...], cot_ref[...]).astype(bf16)
    up_ref[...] = dot_tn(norm_ref[...], gate_ref[...]).astype(bf16)


def feed_grads(act, norm, cot, gate):
    units, width = act.shape[1], norm.shape[1]
    return pl.pallas_call(
        feed_grad_kernel,
        out_shape=[
            jax.ShapeDtypeStruct((units, width), bf16),
            jax.ShapeDtypeStruct((width, units), bf16),
        ],
        name="feed_grads",
        compiler_params=params(16),
        cost_estimate=cost(3),
    )(act, norm, cot, gate)


def finish_kernel(count, *refs):
    backs, refs = refs[:count], refs[count:]
    base_ref, mid_grad_ref, gain_ref, t0, t1, t2, t3, table_ref, sums_ref, *pieces = refs
    step = pl.program_id(0)
    piece = base_ref.shape[0]
    back = sum(ref[...] for ref in backs)
    unit, inverse = normalise(base_ref[...])
    grad = mid_grad_ref[...] + norm_back(back * gain_ref[...], unit, inverse)
    low = grad.astype(bf16)
    tile = t0[...]
    for k, other in enumerate((t1, t2, t3)):
        tile = jnp.where(step == k + 1, other[...], tile)
    onehot = onehot_of(tile, table_ref.shape[0], piece)
    total = 0.0
    for part in split_three(grad):
        total = total + dot(onehot, part)
    add_sums(table_ref, total)
    add_sums(sums_ref, rows_of(column_sum(back * unit), column_sum(back)))
    for k, out_ref in enumerate(pieces):

        @pl.when(step == k)
        def _():
            out_ref[...] = low


def finish(backs, base, mid_grad, gain, parcels, table_rows):
    rows, width = base.shape
    step = parcels[0].shape[0] - TILE
    return pl.pallas_call(
        functools.partial(finish_kernel, len(backs)),
        grid=(rows // step,),
        in_specs=[by_rows(step, width)] * (len(backs) + 2)
        + [whole(gain.shape)]
        + [tile_spec_of(parcels[0])] * 4,
        out_specs=[whole((table_rows, width)), whole((8, width))]
        + [whole((step, width))] * (rows // step),
        out_shape=[
            jax.ShapeDtypeStruct((table_rows, width), f32),
            jax.ShapeDtypeStruct((8, width), f32),
        ]
        + [jax.ShapeDtypeStruct((step, width), bf16)] * (rows // step),
        name="finish",
        compiler_params=params(60),
        cost_estimate=cost(5),
    )(*backs, base, mid_grad, gain, *parcels)


def place_kernel(axis, shift, count, *refs):
    pieces, outs = refs[:count], refs[count:]
    rank = lax.axis_index(axis) >> shift
    for distance, piece in enumerate(pieces):
        for which, out_ref in enumerate(outs):
            part = piece[which] if len(outs) > 1 else piece[...]
            out_ref[rank ^ distance] = part.astype(out_ref.dtype)


def place(pieces, dtype, axis, shift, arrays=1):
    count = len(pieces)
    shape = pieces[0].shape[1:] if arrays > 1 else pieces[0].shape
    outs = pl.pallas_call(
        functools.partial(place_kernel, axis, shift, count),
        out_shape=[jax.ShapeDtypeStruct((count,) + shape, dtype)] * arrays,
        name="place",
        compiler_params=params(12),
        cost_estimate=cost(2),
    )(*pieces)
    return outs if arrays > 1 else outs[0]


def interleave_kernel(mine_ref, other_ref, out_ref):
    bit = lax.axis_index("dp") & 1
    segment = out_ref.shape[1]
    for k in range(mine_ref.shape[0]):
        if len(other_ref.shape) == 3:
            other = other_ref[k]
        else:
            other = other_ref[k * segment : (k + 1) * segment]
        out_ref[2 * k + bit] = mine_ref[k].astype(out_ref.dtype)
        out_ref[2 * k + 1 - bit] = other.astype(out_ref.dtype)


def interleave(mine, other):
    count, segment, width = mine.shape
    rows = count * segment
    if segment % TILE == 0:
        other_spec = whole((rows, width))
    else:
        other = other[:rows].reshape(mine.shape)
        other_spec = whole(mine.shape)
    out = pl.pallas_call(
        interleave_kernel,
        grid=(1,),
        in_specs=[whole(mine.shape), other_spec],
        out_specs=whole((2 * count, segment, width)),
        out_shape=jax.ShapeDtypeStruct((2 * count, segment, width), f32),
        name="interleave",
        compiler_params=params(12),
        cost_estimate=cost(2),
    )(mine, other)
    return out.reshape(2 * rows, width)


def on_device(
    hidden_in,
    codon_ids,
    start_flags,
    cotangent,
    codon_table,
    norm1_gain,
    norm1_bias,
    qkv_weight,
    qkv_bias,
    out_weight,
    out_bias,
    norm2_gain,
    norm2_bias,
    up_weight,
    up_bias,
    down_weight,
    down_bias,
):
    gene_count, piece, width = hidden_in.shape
    group = lax.axis_size("tensor")
    rank = lax.axis_index("tensor")
    local = qkv_weight.shape[2]
    heads = local // HEAD_DIM
    table_rows = codon_table.shape[0]

    spread_bias = jnp.broadcast_to(
        qkv_bias.reshape(3, heads, 1, HEAD_DIM), (3, heads, 2, HEAD_DIM)
    ).reshape(3, 2 * local)
    spread_bias = jnp.pad(spread_bias, ((0, 5), (0, width - 2 * local)))
    own = make_parcels(
        hidden_in, codon_ids, start_flags, spread_bias, up_bias[None], table_rows // 2
    )
    turned = qkv_weight.transpose(1, 2, 0).reshape(3, heads, HEAD_DIM, width)
    mixed = jnp.concatenate(
        [turned.transpose(1, 0, 2, 3), out_weight.reshape(heads, 1, HEAD_DIM, width)], 1
    )
    blocks = (mixed.reshape(4 * local, width), up_weight, down_weight)
    bit = lax.axis_index("dp") & 1
    half = width // 2

    def half_of(block):
        return lax.dynamic_slice_in_dim(block, bit * half, half, 0)

    def join(one, two):
        return jnp.where(
            bit == 0, jnp.concatenate([one, two], -2), jnp.concatenate([two, one], -2)
        )

    def as_mix(block):
        return block.reshape(heads, 4, HEAD_DIM, width)

    def flat(item):
        return item.reshape(-1, width)

    own_cot = [pick(cotangent, rank ^ r) for r in range(group)]
    cot_stack = jnp.stack(own_cot[2:])
    up_half = half_of(blocks[1])
    quarter = width // 4
    down_first, down_last = down_weight[:quarter], down_weight[quarter:]

    frequencies = 10000.0 ** (-jnp.arange(HEAD_DIM // 2, dtype=f32) * 2.0 / HEAD_DIM)
    positions = jnp.concatenate(
        [((rank ^ r) * piece + jnp.arange(piece)).astype(f32) for r in range(group)]
    )
    angles = frequencies[:, None] * positions[None, :]
    tables = (jnp.cos(angles), jnp.sin(angles))

    def local_work():
        return tables, half_of(blocks[0]), up_half, own_cot, cot_stack, down_first, down_last

    got, (tables, mix_half, up_half, own_cot, cot_stack, down_first, down_last) = stage(
        [(own[r], "tensor", r) for r in (2, 3, 1)], local_work
    )
    parcels = [own[0], got[2], got[0], got[1]]
    (mix_mate,) = together((swap(blocks[0], "tensor", 1),))
    mixes = [as_mix(blocks[0]), as_mix(mix_mate)]
    early, late, every = (0, 1), (1, heads - 1), (0, heads)

    def first_heads(parcels):
        base, norm1 = embed(parcels, codon_table, norm1_gain[None], norm1_bias[None])
        return base, norm1, attend(norm1, *mixes[:2], *parcels[:2], tables, early)

    got, (base, norm1, (*kept0, attn0)) = stage(
        [(mix_half, "tensor", 2), (blocks[1], "tensor", 1), (blocks[2], "tensor", 1)],
        first_heads,
        parcels,
    )
    mix_half, *mates = got
    (mix_other, cot_across), (*kept1, attn1) = stage(
        [(mix_half, "dp", 1), (cot_stack, "tensor", 2)],
        lambda norm: attend(norm, *mixes[:2], *parcels[:2], tables, late),
        norm1,
    )
    across_mix = join(mix_half, mix_other)
    (across_mate, got), _ = stage(
        [(across_mix, "tensor", 1), mate_transfer(own_cot, cot_across)], lambda: ()
    )
    mixes += [as_mix(across_mix), as_mix(across_mate)]
    cot = jnp.concatenate(four(own_cot, cot_across, got), 0)
    (up_half, down_part), (*kept2, attn2) = stage(
        [(up_half, "tensor", 2), (down_first, "tensor", 2)],
        lambda norm: attend(norm, *mixes[2:], *parcels[2:], tables, every),
        norm1,
    )
    vectors = jnp.stack([out_bias, norm2_gain, norm2_bias, down_bias])

    def feed_near(base, cot):
        results = feed_first(
            (attn0, attn1, attn2), base, cot, vectors,
            (up_weight, mates[0]), (down_weight, mates[1]), parcels[:2],
        )
        return results, feed_grads(results[3], results[1], cot, results[5])

    (up_other, down_rest), (results, sent) = stage(
        [(up_half, "dp", 1), (down_last, "tensor", 2)], feed_near, base, cot
    )
    mid, norm2, act0, act1, gate0, gate1, ffn, back, sums_first = results

    def feed_join(one, two, down_one, down_two):
        across = jnp.stack([join(one, two), jnp.concatenate([down_one, down_two], 0)])
        return feed_grads(act0, norm2, cot, gate0), across

    got, (near, feed_across) = stage(
        [(item, "tensor", 1) for item in sent],
        feed_join, up_half, up_other, down_part, down_rest,
    )
    (feed_mate,), (keep_near, send_near) = stage(
        [(feed_across, "tensor", 1)],
        lambda near, got: add_halve(near[0], got[0], near[1], got[1]),
        near,
        got,
    )

    def feed_far(ffn):
        results = feed_second(
            norm2, mid, cot, vectors, ffn, back, feed_across, feed_mate, parcels[2:]
        )
        sent = feed_grads(results[1], norm2, cot, results[3])
        return results, sent, feed_grads(results[0], norm2, cot, results[2])

    (got_near,), (results, sent, far) = stage([(send_near, "dp", 1)], feed_far, ffn)
    act2, act3, gate2, gate3, mid_grad, grad_low, sums_second, *out_pieces = results
    got, near = stage(
        [(item, "tensor", 1) for item in sent], lambda *pair: add_low(*pair), keep_near, got_near
    )
    keep_far, send_far = add_halve(far[0], got[0], far[1], got[1])

    def back_part(saved, block, span):
        return lambda grad: attend_back(
            saved, grad, norm1, mixes[block], mixes[block + 1], tables, span
        )

    near_steps = Scatter(near, 1)
    (*near_got, got_far, out_across), (mix2, mix3, back_a, bias_far) = stage(
        near_steps.transfers() + [(send_far, "dp", 1), (jnp.stack(out_pieces[2:]), "tensor", 2)],
        back_part(kept2, 2, every),
        grad_low,
    )
    far_steps = Scatter(add_low(keep_far, got_far), 1)
    (got,), _ = stage([(mix3, "tensor", 1)], lambda sends: sends, far_steps.sends)
    far_mix = add_low(mix2, got)
    (*far_got, cross, out_got), (mix0a, mix1a, back_c, bias_c) = stage(
        far_steps.transfers()
        + [(far_mix, "tensor", 2), mate_transfer(out_pieces, out_across)],
        back_part(kept1, 0, late),
        grad_low,
    )
    near_piece = near_steps.finish(near_got)
    far_piece = far_steps.finish(far_got)
    (feed_cross, got), (mix0b, mix1b, back_d, bias_d) = stage(
        [(far_piece, "tensor", 2), (mix1a, "tensor", 1)], back_part(kept0, 0, early), grad_low
    )
    feed_piece = add_low(near_piece, feed_cross)
    mix_keep, mix_send = halve_heads(
        jnp.concatenate(
            [add_low(mix0b, cross[:1]), add_low(mix0a, got, cross[1:]), mix1b], 0
        )
    )
    (*feed_got, mix_got), (table_part, sums_last, *grad_pieces) = stage(
        upper_transfers(feed_piece) + [(mix_send, "dp", 1)],
        lambda mid_grad: finish(
            (back_a, back_c, back_d), base, mid_grad, norm1_gain[None], parcels, table_rows
        ),
        mid_grad,
    )
    bias_near = jnp.concatenate([bias_d, bias_c], 0)

    def by_owner(blocks):
        swapped = jnp.where(rank & 1 == 1, blocks[jnp.array([1, 0, 3, 2])], blocks)
        return jnp.where(rank & 2 == 2, swapped[jnp.array([2, 3, 0, 1])], swapped)

    up_rows = by_owner(jnp.concatenate([sums_first[:2], sums_second[:2]], 0))
    qkv_rows = jnp.stack([bias_near, bias_far])[:, :, 0].reshape(2, heads, 3, 2, HEAD_DIM)
    qkv_rows = qkv_rows.transpose(0, 3, 2, 1, 4).reshape(group, 3, local)
    qkv_rows = by_owner(qkv_rows).transpose(1, 0, 2).reshape(3, width)
    vectors = jnp.concatenate([sums_last[:2], sums_second[2:6], up_rows, qkv_rows], 0)
    vectors = jnp.pad(vectors, ((0, 32 - vectors.shape[0]), (0, 0)))
    small = jnp.concatenate([table_part.astype(bf16), vectors.astype(bf16)], 0)
    core = rank & 1
    count = small.shape[0] // 2
    small_keep = lax.dynamic_slice_in_dim(small, core * count, count, 0)
    small_send = lax.dynamic_slice_in_dim(small, (1 - core) * count, count, 0)
    segment = mix_keep.shape[1] // (heads + 1)
    mix_sum = add_low(mix_keep, mix_got)
    mate_share = mix_sum[:, -segment:]
    (got, mate_got), (down_part, up_part) = stage(
        [(small_send, "tensor", 1), (mate_share, "tensor", 1)],
        lambda pieces: place(pieces, bf16, "dp", 1, 2),
        [feed_piece] + feed_got,
    )
    small = add_low(small_keep, got)
    mix_own = add_low(mix_sum[:, :segment], mate_got)
    mix_steps = Scatter(jnp.concatenate([mix_own, mix_sum[:, segment:-segment]], 1))
    to_other = jnp.concatenate(grad_pieces[2:] + [small], 0)
    (*mix_got, crossed, down_other), _ = stage(
        mix_steps.transfers() + [(to_other, "tensor", 2), (flat(down_part), "dp", 1)], lambda: ()
    )
    small = add_low(small, crossed[2 * piece :])
    mix_piece = mix_steps.finish(mix_got)
    grad_across = [crossed[:piece], crossed[piece : 2 * piece]]
    (*mix_got, up_other, grad_got), down_grad = stage(
        upper_transfers(mix_piece)
        + [
            (jnp.concatenate([flat(up_part), small], 0), "dp", 1),
            mate_transfer(grad_pieces, grad_across),
        ],
        interleave,
        down_part,
        down_other,
    )
    size = flat(up_part).shape[0]
    small = add_low(small, up_other[size:])
    mix_part = place([mix_piece] + mix_got, bf16, "dp", 1)
    (*got, other), (up_grad, hidden_out, hidden_grad) = stage(
        upper_transfers(small) + [(flat(mix_part), "dp", 1)],
        lambda part, rows, out, grad: (
            interleave(part, rows),
            place(out, bf16, "tensor", 0),
            place(grad, f32, "tensor", 0),
        ),
        up_part,
        up_other,
        four(out_pieces, out_across, out_got),
        four(grad_pieces, grad_across, grad_got),
    )
    small = add_low(small, *got)
    (other_half,), mix_grad = stage(
        [(small, "tensor", 1)], interleave, mix_part, other
    )
    small = jnp.where(
        core == 0,
        jnp.concatenate([small, other_half], 0),
        jnp.concatenate([other_half, small], 0),
    ).astype(f32)
    owners = lax.axis_size("dp") // 4
    mix_grad = mix_grad.reshape(4, owners, heads, HEAD_DIM // owners, width)
    qkv_grad = mix_grad[:3].transpose(4, 0, 2, 1, 3).reshape(width, 3, local)
    out_grad = mix_grad[3].transpose(1, 0, 2, 3).reshape(local, width)
    at = table_rows
    rows = [small[at + k] for k in range(6)]
    up_bias_grad = lax.dynamic_index_in_dim(small[at + 6 : at + 6 + group], rank, 0, keepdims=False)
    qkv_bias_grad = lax.dynamic_slice_in_dim(
        small[at + 6 + group : at + 9 + group], rank * local, local, 1
    )
    return (
        hidden_out,
        hidden_grad,
        small[:table_rows],
        rows[0],
        rows[1],
        qkv_grad,
        qkv_bias_grad,
        out_grad,
        rows[4],
        rows[2],
        rows[3],
        up_grad,
        up_bias_grad,
        down_grad,
        rows[5],
    )


def solution(mesh):
    rows_placed = P("dp", "tensor", None)
    return jax.shard_map(
        on_device,
        mesh=mesh,
        in_specs=(
            rows_placed,
            P("dp", "tensor"),
            P("dp", "tensor"),
            rows_placed,
            P(),
            P(),
            P(),
            P(None, None, "tensor"),
            P(None, "tensor"),
            P("tensor", None),
            P(),
            P(),
            P(),
            P(None, "tensor"),
            P("tensor"),
            P("tensor", None),
            P(),
        ),
        out_specs=(
            rows_placed,
            rows_placed,
            P(),
            P(),
            P(),
            P(None, None, "tensor"),
            P(None, "tensor"),
            P("tensor", None),
            P(),
            P(),
            P(),
            P(None, "tensor"),
            P("tensor"),
            P("tensor", None),
            P(),
        ),
        check_vma=False,
    )
```
